32 devices in a mesh: grp: 4 (over y, core), seq: 2 (over x), mp: 4 (over z).
Axes of the slice: x: 2, y: 2, z: 4, core: 2. Of those that a mesh axis runs over, the one named last changes fastest.
Arguments:
- queries: bfloat16 [4, 256, 2048], P('grp', 'seq', 'mp'), may hold values from -16 to 16
- d_out: bfloat16 [4, 256, 2048], P('grp', 'seq', 'mp'), may hold values from -6 to 6
- neighbour_kv: bfloat16 [4, 8, 128, 2, 2048], P('grp', 'seq', None, None, 'mp'), may hold values from -16 to 16
- target: int32 [4, 8], P('grp', 'seq'), may hold values from -1 to 7, as said below
- bias: float32 [16, 191], P('mp'), may hold values from -6 to 6
Outputs:
- attended: bfloat16 [4, 256, 2048], P('grp', 'seq', 'mp')
- d_query: bfloat16 [4, 256, 2048], P('grp', 'seq', 'mp')
- d_kv: bfloat16 [4, 8, 128, 2, 2048], P('grp', 'seq', None, None, 'mp')
- d_bias: float32 [16, 191], P('mp')
The draws below stay inside these ranges and needn't reach their ends.
Inputs may be any that keep to these rules, and one draw needn't show every extreme that they name: `target`: in each group every entry 0..7 stands in exactly one slot and -1 marks an empty slot. The slots of one index of seq hold at most 2 entries e with the same e // 4, and some index reaches that; some index of seq holds 4 entries.
All inputs are finite; a program needn't handle non-finite values.
Results may differ from the reference program's by a relative error of at most 0.011.
Values may be sent and summed in bfloat16 or wider, within the bound.
A program may use at most 128 MiB of HBM per device.

```python
import jax
import jax.numpy as jnp
from jax import lax

HEADS = 16
HD = 128
STRETCH = 64
NB_LEN = 128
CH_DEV = 2
ATTN = 2048
TOKENS_G = 256
SEQ_LEN = 256
NB_SLOT = 4
SLOTS_G = 8
REL = 191
N_GRP = 4
N_SEQ = 2


def draw_queries(key, part):
    shape_all = (N_GRP, TOKENS_G, HEADS * HD)
    sample = jnp.clip(jax.random.normal(jax.random.fold_in(key, 11), shape_all, jnp.float32), -6.0, 6.0)
    return sample.astype(jnp.bfloat16)


def draw_neighbour_kv(key, part):
    shape_all = (N_GRP, SLOTS_G, NB_LEN, 2, HEADS * HD)
    sample = jnp.clip(jax.random.normal(jax.random.fold_in(key, 13), shape_all, jnp.float32), -6.0, 6.0)
    return sample.astype(jnp.bfloat16)


def group_targets(key):
    per_owner = 2 * CH_DEV
    group_size = min(N_SEQ, per_owner)
    full_count = NB_SLOT
    entry_total = per_owner * N_SEQ
    others = N_SEQ - group_size
    full_part = jnp.full((group_size,), full_count, jnp.int32)
    if others > 0:
        remain = entry_total - group_size * full_count
        base_count = remain // others
        extra = remain % others
        counts_rest = base_count + (jnp.arange(others) < extra).astype(jnp.int32)
        pair_count = others // 2
        if pair_count > 0:
            reach = min(base_count, full_count - base_count - 1)
            moves = jax.random.randint(jax.random.fold_in(key, 1), (pair_count,), 0, reach + 1).astype(jnp.int32)
            change = jnp.zeros((others,), jnp.int32)
            change = change.at[0:2 * pair_count:2].add(moves).at[1:2 * pair_count:2].add(-moves)
            counts_rest = counts_rest + change
        counts_pos = jnp.concatenate([full_part, counts_rest])
    else:
        counts_pos = full_part
    shard_perm = jax.random.permutation(jax.random.fold_in(key, 2), N_SEQ)
    counts = jnp.zeros((N_SEQ,), jnp.int32).at[shard_perm].set(counts_pos)
    slot_ids = jnp.arange(full_count)
    above = (counts[None, :] > slot_ids[:, None]).astype(jnp.int32)
    per_round = jnp.sum(above, axis=1)
    round_start = jnp.cumsum(per_round) - per_round
    within = jnp.cumsum(above, axis=1) - above
    entries = jnp.where(above > 0, round_start[:, None] + within, -1).T
    shard_keys = jax.random.split(jax.random.fold_in(key, 3), N_SEQ)
    slot_perm = jax.vmap(lambda sub: jax.random.permutation(sub, full_count))(shard_keys)
    placed = jnp.zeros((N_SEQ, full_count), jnp.int32).at[jnp.arange(N_SEQ)[:, None], slot_perm].set(entries)
    return placed.reshape(N_SEQ * full_count)


def draw_target(key, part):
    group_keys = jax.random.split(jax.random.fold_in(key, 77), N_GRP)
    return jax.vmap(group_targets)(group_keys).astype(jnp.int32)


def block_levels(rng, extent, cuts, low, top_value):
    def one(position, parts):
        steps = jax.random.uniform(jax.random.fold_in(jax.random.fold_in(rng, 6), position), (parts,), jnp.float32, low / len(cuts), top_value / len(cuts))
        return jnp.repeat(jnp.exp(steps), extent[position] // parts).reshape((-1,) + (1,) * (len(extent) - position - 1))

    level = one(*cuts[0])
    for cut in cuts[1:]:
        level = level * one(*cut)
    return level


def noise(rng, shape, deviation, most, cuts=(), kind=jnp.bfloat16):
    result = jax.random.normal(rng, shape, jnp.float32) * deviation
    if len(cuts) > 0:
        result = block_levels(rng, shape, cuts, -0.22, 0.18) * result
    return jnp.clip(result, min=-most, max=most).astype(kind)


def setup_inputs(seed: int = 0) -> dict:
    arg_keys = jax.random.split(jax.random.key(seed), 6)
    queries = draw_queries(jax.random.fold_in(arg_keys[5], 71), 0)
    d_out = noise(arg_keys[1], (N_GRP, TOKENS_G, ATTN), 1.0, 6.0, ((0, 4), (1, 2), (2, 4)))
    neighbour_kv = draw_neighbour_kv(jax.random.fold_in(arg_keys[5], 71), 0)
    target = draw_target(jax.random.fold_in(arg_keys[5], 71), 0)
    bias = noise(arg_keys[4], (HEADS, REL), 1.0, 6.0, ((0, 4),), jnp.float32)
    return {"queries": queries, "d_out": d_out, "neighbour_kv": neighbour_kv, "target": target, "bias": bias}


def bias_grid(lookup, row_count, col_count):
    head_num = lookup.shape[0]
    span = row_count + col_count
    padded = jnp.pad(lookup, ((0, 0), (0, 1)))
    flattened = jnp.tile(padded, (1, row_count))
    flattened = jnp.pad(flattened, ((0, 0), (0, row_count)))
    shaped = flattened.reshape(head_num, row_count, span + 1)[:, :, :col_count]
    return shaped[:, :, ::-1]

def bias_fold(grads):
    head_num, row_count, col_count = grads.shape
    turned = grads[:, :, ::-1]
    padded = jnp.pad(turned, ((0, 0), (0, 0), (0, row_count)))
    flattened = padded.reshape(head_num, row_count * (row_count + col_count))
    flattened = flattened[:, :row_count * (row_count + col_count - 1)]
    return lax.optimization_barrier(jnp.sum(flattened.reshape(head_num, row_count, row_count + col_count - 1), axis=1))

def to_wide(values_in):
    return lax.optimization_barrier(values_in.astype(jnp.bfloat16)).astype(jnp.float32)

def window_math(q_rows, g_rows, key_rows, value_rows, grid_rows, scale_factor, live_row):
    q_wide = q_rows.astype(jnp.float32)
    g_wide = g_rows.astype(jnp.float32)
    k_wide = key_rows.astype(jnp.float32)
    v_wide = value_rows.astype(jnp.float32)
    scores = jnp.einsum('ihd,njhd->nihj', q_wide, k_wide) * scale_factor + grid_rows[None]
    peak_val = lax.optimization_barrier(jnp.max(scores, axis=-1))
    weights = jnp.exp(scores - peak_val[..., None])
    row_total = lax.optimization_barrier(jnp.sum(weights, axis=-1))
    partial_value = jnp.einsum('nihj,njhd->nihd', to_wide(weights), v_wide)
    top_peak = lax.optimization_barrier(jnp.max(peak_val, axis=0))
    factor = jnp.exp(peak_val - top_peak[None])
    denominator = lax.optimization_barrier(jnp.sum(factor * row_total, axis=0))
    combined = lax.optimization_barrier(jnp.sum(factor[..., None] * partial_value, axis=0)) / denominator[..., None]
    combined = combined * live_row[:, None, None]
    log_total = top_peak + jnp.log(denominator)
    inner_dot = lax.optimization_barrier(jnp.sum(g_wide * combined, axis=-1))
    prob_full = jnp.exp(scores - log_total[None, ..., None])
    grad_values = jnp.einsum('nihj,ihd->njhd', to_wide(prob_full), g_wide)
    grad_prob = jnp.einsum('ihd,njhd->nihj', g_wide, v_wide)
    grad_scores = prob_full * (grad_prob - inner_dot[None, ..., None])
    scores_low = to_wide(grad_scores)
    grad_rows = jnp.einsum('nihj,njhd->ihd', scores_low, k_wide) * scale_factor
    grad_keys = jnp.einsum('nihj,ihd->njhd', scores_low, q_wide) * scale_factor
    bias_part = bias_fold(lax.optimization_barrier(jnp.sum(grad_scores, axis=0)).transpose(1, 0, 2))
    return (combined, grad_rows, grad_keys, grad_values, bias_part)

def reference(queries, d_out, neighbour_kv, target, bias):
    groups, tokens, full_width = queries.shape
    head_num = bias.shape[0]
    head_depth = full_width // head_num
    stretches = tokens // STRETCH
    seq_stretches = SEQ_LEN // STRETCH
    scale_factor = head_depth ** (-0.5)
    grid_rows = bias_grid(bias, STRETCH, NB_LEN).transpose(1, 0, 2)
    row_ids = jnp.arange(STRETCH)
    stretch_ids = jnp.arange(stretches)
    live_rows = ((row_ids[None, :] == 0) | ((stretch_ids[:, None] + 1) % seq_stretches != 0)).astype(jnp.float32)

    def one_group(group_idx):
        q_group = queries[group_idx]
        g_group = d_out[group_idx]
        kv_group = neighbour_kv[group_idx]
        t_group = target[group_idx]
        padding = jnp.zeros((STRETCH, full_width), queries.dtype)
        q_win = jnp.concatenate([q_group, padding])[STRETCH - 1:STRETCH - 1 + tokens]
        q_win = q_win.reshape(stretches, STRETCH, head_num, head_depth)
        g_win = jnp.concatenate([g_group, padding])[STRETCH - 1:STRETCH - 1 + tokens]
        g_win = g_win.reshape(stretches, STRETCH, head_num, head_depth) * live_rows[:, :, None, None].astype(d_out.dtype)
        entry_ids = jnp.arange(2 * stretches, dtype=jnp.int32)
        slot_of = jnp.argmax(t_group[None, :] == entry_ids[:, None], axis=1).astype(jnp.int32)
        blocks = kv_group[slot_of].reshape(stretches, 2, NB_LEN, 2, head_num, head_depth)

        def one_stretch(item):
            q_rows, g_rows, block, live_row = item
            combined, grad_rows, grad_keys, grad_values, bias_part = window_math(q_rows, g_rows, block[:, :, 0], block[:, :, 1], grid_rows, scale_factor, live_row)
            stacked = jnp.stack([grad_keys, grad_values], axis=2).astype(jnp.bfloat16)
            return (combined.astype(jnp.bfloat16), grad_rows.astype(jnp.bfloat16), stacked, bias_part)
        outs_win, grads_win, kv_grads, bias_parts = lax.map(one_stretch, (q_win, g_win, blocks, live_rows))
        lead = jnp.zeros((STRETCH - 1, full_width), jnp.bfloat16)
        attended = jnp.concatenate([lead, outs_win.reshape(tokens, full_width)[:tokens - STRETCH + 1]])
        d_query = jnp.concatenate([lead, grads_win.reshape(tokens, full_width)[:tokens - STRETCH + 1]])
        kv_entries = kv_grads.reshape(2 * stretches, NB_LEN, 2, full_width)
        slot_mask = (t_group >= 0).astype(jnp.bfloat16)
        d_kv = kv_entries[jnp.clip(t_group, 0, 2 * stretches - 1)] * slot_mask[:, None, None, None]
        return (attended, d_query, d_kv, lax.optimization_barrier(jnp.sum(bias_parts, axis=0)))
    attended, d_query, d_kv, bias_groups = lax.map(one_group, jnp.arange(groups))
    raw_sum = lax.optimization_barrier(jnp.sum(bias_groups, axis=0))
    norm_val = jnp.sqrt(jnp.sum(raw_sum * raw_sum) + 1e-12)
    d_bias = raw_sum * jnp.minimum(1.0, 1.0 / norm_val)
    return (attended, d_query, d_kv, d_bias)
```

```python
import jax
import jax.numpy as jnp
from jax import lax
from jax.experimental import pallas as pl
from jax.experimental.pallas import tpu as pltpu
from jax.sharding import PartitionSpec as P

STRETCH = 64
NB_LEN = 128


def passed_along(block, axis, distance):
    devices = range(lax.axis_size(axis))
    route = [(i - distance, i) for i in devices if i - distance in devices]
    return lax.ppermute(block, axis, route)


def bias_grid(lookup, row_count, col_count):
    head_num = lookup.shape[0]
    span = row_count + col_count
    padded = jnp.pad(lookup, ((0, 0), (0, 1)))
    flattened = jnp.tile(padded, (1, row_count))
    flattened = jnp.pad(flattened, ((0, 0), (0, row_count)))
    shaped = flattened.reshape(head_num, row_count, span + 1)[:, :, :col_count]
    return shaped[:, :, ::-1]


def bias_fold(grads):
    head_num, row_count, col_count = grads.shape
    turned = grads[:, :, ::-1]
    padded = jnp.pad(turned, ((0, 0), (0, 0), (0, row_count)))
    flattened = padded.reshape(head_num, row_count * (row_count + col_count))
    flattened = flattened[:, : row_count * (row_count + col_count - 1)]
    return jnp.sum(flattened.reshape(head_num, row_count, row_count + col_count - 1), axis=1)


def select_rows(picker, lookup):
    chosen = jnp.dot(
        picker.astype(lookup.dtype),
        lookup,
        preferred_element_type=jnp.float32,
        precision=lax.Precision.HIGHEST,
    )
    return chosen.astype(lookup.dtype)


def slot_places(target_row, owners, capacity, per_owner):
    is_used = target_row >= 0
    owner_of = jnp.where(is_used, target_row // per_owner, -1)
    positions = jnp.arange(target_row.shape[0])
    earlier = (
        (positions[None, :] < positions[:, None])
        & (owner_of[None, :] == owner_of[:, None])
        & is_used[None, :]
    )
    rank_of = jnp.sum(earlier.astype(jnp.int32), axis=1)
    match_owner = owner_of[None, :] == jnp.arange(owners)[:, None]
    match_rank = rank_of[None, :] == jnp.arange(capacity)[:, None]
    return match_owner[:, None, :] & match_rank[None, :, :] & is_used[None, None, :]


def shard_exchange(queries, d_out, neighbour_kv, target, bias):
    tok_rows = queries.shape[1]
    width_dev = queries.shape[2]
    head_count = bias.shape[0]
    head_depth = width_dev // head_count
    stretch_count = tok_rows // STRETCH
    per_owner = 2 * stretch_count
    shard_count = lax.axis_size("seq")
    my_index = lax.axis_index("seq")
    group_size = min(shard_count, per_owner)
    capacity = (per_owner + group_size - 1) // group_size
    seq_stretches = min(2048, tok_rows * shard_count) // STRETCH
    scale_factor = head_depth ** (-0.5)
    bias_rows = bias_grid(bias, STRETCH, NB_LEN).transpose(1, 0, 2)
    q_rows = queries[0]
    g_rows = d_out[0]
    next_pair = passed_along(jnp.stack([q_rows[:STRETCH], g_rows[:STRETCH]]), "seq", -1)
    row_ids = jnp.arange(STRETCH)
    stretch_ids = my_index * stretch_count + jnp.arange(stretch_count)
    is_live = (row_ids[None, :] == 0) | ((stretch_ids[:, None] + 1) % seq_stretches != 0)
    live_rows = is_live.astype(jnp.float32)
    q_win = jnp.concatenate([q_rows, next_pair[0]])[STRETCH - 1 : STRETCH - 1 + tok_rows]
    q_win = q_win.reshape(stretch_count, STRETCH * width_dev)
    g_win = jnp.concatenate([g_rows, next_pair[1]])[STRETCH - 1 : STRETCH - 1 + tok_rows]
    g_win = g_win.reshape(stretch_count, STRETCH, width_dev) * is_live[:, :, None].astype(
        jnp.bfloat16
    )
    g_win = g_win.reshape(stretch_count, STRETCH * width_dev)
    my_targets = target[0]
    slot_count = my_targets.shape[0]
    send_map = slot_places(my_targets, shard_count, capacity, per_owner)
    id_buffer = jnp.sum(jnp.where(send_map, my_targets[None, None, :] + 1, 0), axis=2) - 1
    recv_ids = lax.all_to_all(id_buffer, "seq", split_axis=0, concat_axis=0, tiled=True)
    flat_ids = recv_ids.reshape(shard_count * capacity)
    has_entry = flat_ids >= 0
    local_entry = flat_ids - my_index * per_owner
    entry_pick = (local_entry[:, None] == jnp.arange(per_owner)[None, :]) & has_entry[:, None]
    stretch_pick = (local_entry[:, None] // 2 == jnp.arange(stretch_count)[None, :]) & has_entry[
        :, None
    ]
    back_pick = send_map.reshape(shard_count * capacity, slot_count)
    slot_pick = back_pick.T
    q_send = select_rows(stretch_pick, q_win).reshape(shard_count, capacity, STRETCH * width_dev)
    g_send = select_rows(stretch_pick, g_win).reshape(shard_count, capacity, STRETCH * width_dev)
    q_recv, g_recv = (
        lax.all_to_all(q_send, "seq", split_axis=0, concat_axis=0, tiled=True),
        lax.all_to_all(g_send, "seq", split_axis=0, concat_axis=0, tiled=True),
    )
    q_slots = select_rows(slot_pick, q_recv.reshape(shard_count * capacity, -1))
    q_slots = q_slots.reshape(slot_count, STRETCH, head_count, head_depth)
    stored = neighbour_kv[0]
    key_rows = stored[:, :, 0].reshape(slot_count, NB_LEN, head_count, head_depth)
    value_rows = stored[:, :, 1].reshape(slot_count, NB_LEN, head_count, head_depth)
    scores = jnp.einsum("sihd,sjhd->sihj", q_slots, key_rows, preferred_element_type=jnp.float32)
    scores = scores * scale_factor + bias_rows[None]
    peak_val = jnp.max(scores, axis=-1)
    weights = jnp.exp(scores - peak_val[..., None])
    row_total = jnp.sum(weights, axis=-1)
    partial_value = jnp.einsum(
        "sihj,sjhd->sihd",
        weights.astype(jnp.bfloat16),
        value_rows,
        preferred_element_type=jnp.float32,
    )
    part_send = select_rows(back_pick, partial_value.reshape(slot_count, -1)).reshape(
        shard_count, capacity, -1
    )
    peak_send = select_rows(back_pick, peak_val.reshape(slot_count, -1)).reshape(
        shard_count, capacity, -1
    )
    total_send = select_rows(back_pick, row_total.reshape(slot_count, -1)).reshape(
        shard_count, capacity, -1
    )
    part_recv, peak_recv, total_recv = (
        lax.all_to_all(part_send, "seq", split_axis=0, concat_axis=0, tiled=True),
        lax.all_to_all(peak_send, "seq", split_axis=0, concat_axis=0, tiled=True),
        lax.all_to_all(total_send, "seq", split_axis=0, concat_axis=0, tiled=True),
    )
    entry_back = entry_pick.T
    parts_own = select_rows(entry_back, part_recv.reshape(shard_count * capacity, -1))
    parts_own = parts_own.reshape(stretch_count, 2, STRETCH, head_count, head_depth)
    peaks_own = select_rows(entry_back, peak_recv.reshape(shard_count * capacity, -1))
    peaks_own = peaks_own.reshape(stretch_count, 2, STRETCH, head_count)
    totals_own = select_rows(entry_back, total_recv.reshape(shard_count * capacity, -1))
    totals_own = totals_own.reshape(stretch_count, 2, STRETCH, head_count)
    top_peak = jnp.max(peaks_own, axis=1)
    factor = jnp.exp(peaks_own - top_peak[:, None])
    denominator = jnp.sum(factor * totals_own, axis=1)
    combined = jnp.sum(factor[..., None] * parts_own, axis=1) / denominator[..., None]
    combined = combined * live_rows[:, :, None, None]
    att_win = combined.astype(jnp.bfloat16).reshape(tok_rows, width_dev)
    log_total = top_peak + jnp.log(denominator)
    g_wide = g_win.reshape(stretch_count, STRETCH, head_count, head_depth).astype(jnp.float32)
    inner_dot = jnp.sum(g_wide * combined, axis=-1)
    row_stats = jnp.repeat(jnp.stack([log_total, inner_dot], axis=1), 2, axis=0)
    stats_send = select_rows(entry_pick, row_stats.reshape(per_owner, -1)).reshape(
        shard_count, capacity, -1
    )
    stats_recv = lax.all_to_all(stats_send, "seq", split_axis=0, concat_axis=0, tiled=True)
    g_slots = select_rows(slot_pick, g_recv.reshape(shard_count * capacity, -1))
    g_slots = g_slots.reshape(slot_count, STRETCH, head_count, head_depth)
    stats_slots = select_rows(slot_pick, stats_recv.reshape(shard_count * capacity, -1))
    stats_slots = stats_slots.reshape(slot_count, 2, STRETCH, head_count)
    prob_full = jnp.exp(scores - stats_slots[:, 0][..., None])
    prob_low = prob_full.astype(jnp.bfloat16)
    grad_values = jnp.einsum(
        "sihj,sihd->sjhd", prob_low, g_slots, preferred_element_type=jnp.float32
    )
    grad_prob = jnp.einsum(
        "sihd,sjhd->sihj", g_slots, value_rows, preferred_element_type=jnp.float32
    )
    grad_scores = prob_full * (grad_prob - stats_slots[:, 1][..., None])
    scores_low = grad_scores.astype(jnp.bfloat16)
    grad_rows = (
        jnp.einsum("sihj,sjhd->sihd", scores_low, key_rows, preferred_element_type=jnp.float32)
        * scale_factor
    )
    grad_keys = (
        jnp.einsum("sihj,sihd->sjhd", scores_low, q_slots, preferred_element_type=jnp.float32)
        * scale_factor
    )
    d_kv = jnp.stack(
        [
            grad_keys.reshape(slot_count, NB_LEN, width_dev),
            grad_values.reshape(slot_count, NB_LEN, width_dev),
        ],
        axis=2,
    ).astype(jnp.bfloat16)
    bias_part = bias_fold(jnp.sum(grad_scores, axis=0).transpose(1, 0, 2))
    rows_send = select_rows(back_pick, grad_rows.reshape(slot_count, -1)).reshape(
        shard_count, capacity, -1
    )
    rows_recv = lax.all_to_all(rows_send, "seq", split_axis=0, concat_axis=0, tiled=True)
    grad_entries = select_rows(entry_back, rows_recv.reshape(shard_count * capacity, -1))
    grad_entries = grad_entries.reshape(stretch_count, 2, STRETCH * width_dev)
    grad_win = (
        (grad_entries[:, 0] + grad_entries[:, 1]).astype(jnp.bfloat16).reshape(tok_rows, width_dev)
    )
    both_before = passed_along(
        jnp.stack([att_win[tok_rows - STRETCH :], grad_win[tok_rows - STRETCH :]]), "seq", 1
    )
    att_before = both_before[0]
    grad_before = both_before[1]
    attended = jnp.concatenate([att_before[1:], att_win[: tok_rows - STRETCH + 1]])
    d_query = jnp.concatenate([grad_before[1:], grad_win[: tok_rows - STRETCH + 1]])
    raw_sum = lax.psum(bias_part, ("grp", "seq"))
    squares = lax.psum(jnp.sum(raw_sum * raw_sum), "mp")
    d_bias = raw_sum * jnp.minimum(1.0, 1.0 / jnp.sqrt(squares + 1e-12))
    return (attended[None], d_query[None], d_kv[None], d_bias)


WIDE = 2 * NB_LEN
HALF = 256
MESH = pl.DeviceIdType.MESH


def dot(a, b, contract=((1,), (0,))):
    return lax.dot_general(a, b, (contract, ((), ())), preferred_element_type=jnp.float32)


def iota(shape, axis):
    return lax.broadcasted_iota(jnp.int32, shape, axis)


def pair_kernel(
    q_ref, g_ref, kv_ref, target_ref, bias_ref,
    att_ref, dq_ref, dkv_ref, dbias_ref,
    q_peer, g_peer, windows, weights, cotangents, mixed, rows_own, rows_send, rows_recv,
    stat_send, stat_recv, raw_all, norm_all,
    in_send, in_recv, stat_sems, row_send_sems, row_recv_sems,
    raw_send_sems, raw_recv_sems, norm_send_sems, norm_recv_sems,
):
    heads = bias_ref.shape[0]
    slots = kv_ref.shape[0]
    tok = q_ref.shape[0]
    depth = kv_ref.shape[-1]
    groups, mps = lax.axis_size("grp"), lax.axis_size("mp")
    plane = 2 * groups
    scale = depth ** (-0.5)
    grp, seq, mp = lax.axis_index("grp"), lax.axis_index("seq"), lax.axis_index("mp")
    here = grp * 2 + seq
    peer = {"seq": 1 - seq}

    def plane_at(step):
        there = lax.rem(here + step, plane)
        return {"grp": there // 2, "seq": there % 2}

    def mp_at(step):
        return {"mp": lax.rem(mp + step, mps)}

    barrier = pltpu.get_barrier_semaphore()
    for step in range(1, plane):
        pl.semaphore_signal(barrier, inc=1, device_id=plane_at(step), device_id_type=MESH)
    for step in range(1, mps):
        pl.semaphore_signal(barrier, inc=1, device_id=mp_at(step), device_id_type=MESH)
    pl.semaphore_wait(barrier, plane - 1 + mps - 1)

    def send(src, dst, send_sem, recv_sem, device):
        copy = pltpu.make_async_remote_copy(
            src_ref=src, dst_ref=dst, send_sem=send_sem, recv_sem=recv_sem,
            device_id=device, device_id_type=MESH,
        )
        copy.start()
        return copy

    in_copies = []
    for h in range(heads):
        cols = pl.ds(h * depth, depth)
        in_copies.append((
            send(q_ref.at[:, cols], q_peer.at[h], in_send.at[2 * h], in_recv.at[2 * h], peer),
            send(g_ref.at[:, cols], g_peer.at[h], in_send.at[2 * h + 1], in_recv.at[2 * h + 1], peer),
        ))

    entries = [target_ref[0, r] for r in range(slots)]
    firsts = [(STRETCH - 1) + STRETCH * (e // 2) for e in entries]

    def token_of(axis, shape):
        place = iota(shape, axis)
        return jnp.where(place < tok, tok * seq + place, tok * (1 - seq) + place - tok)

    def one_hot(flags):
        return jnp.where(flags, 1.0, 0.0).astype(jnp.bfloat16)

    gather = jnp.concatenate(
        [
            one_hot(token_of(1, (STRETCH, 2 * tok)) == iota((STRETCH, 2 * tok), 0) + firsts[r])
            for r in range(slots)
        ],
        axis=0,
    )
    odd = iota((STRETCH, WIDE), 1) % 2 == 1
    lane = iota((STRETCH, 128), 1)
    table = jnp.zeros((STRETCH, 128), jnp.float32)
    for h in range(heads):
        wide = jnp.broadcast_to(bias_ref[h : h + 1, :], (STRETCH, 2 * WIDE))
        grid = pltpu.roll(wide, 2 * WIDE - 126, 1, stride=2, stride_axis=0)[:, :WIDE]
        grid = jnp.where(odd, -1e30, grid)
        cols = pl.ds(h * depth, depth)
        mine = jnp.concatenate([q_ref[:, cols], g_ref[:, cols]], axis=1)
        for copy in in_copies[h]:
            copy.wait_recv()
        other = jnp.concatenate([q_peer[h], g_peer[h]], axis=1)
        picked = dot(gather, jnp.concatenate([mine, other], axis=0)).astype(jnp.bfloat16)
        for r in range(slots):
            rows = picked[r * STRETCH : (r + 1) * STRETCH]
            both = jnp.concatenate([rows[:, :depth], rows[:, depth:]], axis=0)
            windows[h, r] = both
            prod = dot(both, kv_ref[r, h], ((1,), (1,)))
            scores = prod[:STRETCH] * scale + grid
            grad_prob = prod[STRETCH:]
            peak = jnp.max(scores, axis=1, keepdims=True)
            expd = jnp.exp(scores - peak)
            total = jnp.sum(expd, axis=1, keepdims=True)
            expd = pltpu.roll(expd, 1, 1)
            inner = jnp.sum(expd * grad_prob, axis=1, keepdims=True)
            weights[h, r] = expd
            cotangents[h, r] = grad_prob
            base = entries[r] * heads + h
            table = jnp.where(lane == base, peak, table)
            table = jnp.where(lane == base + 32, total, table)
            table = jnp.where(lane == base + 64, inner, table)
    stat_send[...] = table
    stat_copy = send(stat_send, stat_recv, stat_sems.at[0], stat_sems.at[1], peer)
    stat_copy.wait_recv()
    table = table + stat_recv[...]

    def partner(x):
        return jnp.where((lane // heads) % 2 == 0, pltpu.roll(x, 128 - heads, 1), pltpu.roll(x, heads, 1))

    total = pltpu.roll(table, 96, 1)
    inner = pltpu.roll(table, 64, 1)
    other_peak = partner(table)
    top = jnp.maximum(table, other_peak)
    mine_f, other_f = jnp.exp(table - top), jnp.exp(other_peak - top)
    denominator = mine_f * total + other_f * partner(total)
    inner = (mine_f * inner + other_f * partner(inner)) / denominator
    norm = mine_f / denominator

    for h in range(heads):
        bias_sum = jnp.zeros((STRETCH, WIDE), jnp.float32)
        for r in range(slots):
            at = lane == entries[r] * heads + h
            factor = jnp.sum(jnp.where(at, norm, 0.0), axis=1, keepdims=True)
            shift = jnp.sum(jnp.where(at, inner, 0.0), axis=1, keepdims=True)
            prob = weights[h, r] * factor
            grad = prob * (cotangents[h, r] - shift)
            bias_sum = bias_sum + grad
            mixed[h, r, :STRETCH] = pltpu.roll(grad, WIDE - 1, 1).astype(jnp.bfloat16)
            mixed[h, r, STRETCH:] = prob.astype(jnp.bfloat16)
        folded = jnp.concatenate([bias_sum, jnp.zeros_like(bias_sum)], axis=1)
        half = STRETCH // 2
        while half >= 8:
            folded = pltpu.roll(folded[:half], 2 * half, 1) + folded[half:]
            half //= 2
        row8 = iota((8, 2 * WIDE), 0)
        for bit in (4, 2, 1):
            folded = jnp.where((row8 // bit) % 2 == 0, pltpu.roll(folded, 2 * bit, 1), folded)
        folded = jnp.sum(folded, axis=0, keepdims=True)
        if h == 0:
            stacked = jnp.zeros((8, 2 * WIDE), jnp.float32)
        stacked = jnp.where(row8 == h, folded, stacked)
    unmix = jnp.where(
        iota((2 * WIDE, WIDE), 0) == 381 - 2 * iota((2 * WIDE, WIDE), 1), 1.0, 0.0
    ).astype(jnp.float32)
    raw_all[here] = jnp.dot(
        stacked, unmix, preferred_element_type=jnp.float32, precision=lax.Precision.HIGHEST
    )
    raw_copies = [
        send(raw_all.at[here], raw_all.at[here], raw_send_sems.at[k], raw_recv_sems.at[k], plane_at(k))
        for k in range(1, plane)
    ]

    scatter = jnp.concatenate(
        [
            one_hot(token_of(0, (2 * tok, STRETCH)) == iota((2 * tok, STRETCH), 1) + firsts[r])
            for r in range(slots)
        ],
        axis=1,
    )
    row_scale = jnp.where(iota((WIDE, depth), 0) % 2 == 0, scale, 1.0)
    row_copies = []
    for h in range(heads):
        parts = []
        for r in range(slots):
            mix = mixed[h, r]
            out = dot(mix, kv_ref[r, h])
            parts.append(jnp.concatenate([out[STRETCH:], out[:STRETCH] * scale], axis=1).astype(jnp.bfloat16))
        rows = dot(scatter, jnp.concatenate(parts, axis=0))
        rows_own[h] = rows[:tok]
        rows_send[h] = rows[tok:].astype(jnp.bfloat16)
        row_copies.append(send(rows_send.at[h], rows_recv.at[h], row_send_sems.at[h], row_recv_sems.at[h], peer))
    for h in range(heads):
        for r in range(slots):
            dkv = dot(mixed[h, r], windows[h, r], ((0,), (0,))) * row_scale
            dkv_ref[r, h] = dkv.astype(jnp.bfloat16)

    for copy in raw_copies:
        copy.wait_recv()
    raw = raw_all[0]
    for k in range(1, plane):
        raw = raw + raw_all[k]
    norm_all[mp] = jnp.broadcast_to(jnp.sum(raw * raw, keepdims=True), (8, 128))
    norm_copies = [
        send(norm_all.at[mp], norm_all.at[mp], norm_send_sems.at[k], norm_recv_sems.at[k], mp_at(k))
        for k in range(1, mps)
    ]
    for h in range(heads):
        row_copies[h].wait_recv()
        rows = rows_own[h] + rows_recv[h].astype(jnp.float32)
        cols = pl.ds(h * depth, depth)
        att_ref[:, cols] = rows[:, :depth].astype(jnp.bfloat16)
        dq_ref[:, cols] = rows[:, depth:].astype(jnp.bfloat16)
    for copy in norm_copies:
        copy.wait_recv()
    squares = norm_all[0]
    for k in range(1, mps):
        squares = squares + norm_all[k]
    clip = jnp.minimum(1.0, 1.0 / jnp.sqrt(squares[:, :1] + 1e-12))
    dbias_ref[...] = (raw * clip)[: dbias_ref.shape[0], : dbias_ref.shape[1]]
    for pair in in_copies:
        for copy in pair:
            copy.wait_send()
    stat_copy.wait_send()
    for copy in raw_copies + row_copies + norm_copies:
        copy.wait_send()


def pair_exchange(queries, d_out, neighbour_kv, target, bias):
    _, tok, width = queries.shape
    heads, rel = bias.shape
    depth = width // heads
    slots = neighbour_kv.shape[1]
    plane, mps = 2 * lax.axis_size("grp"), lax.axis_size("mp")
    kv = neighbour_kv[0].reshape(slots, NB_LEN, 2, heads, depth).transpose(0, 3, 1, 2, 4)
    kv = kv.reshape(slots, heads, WIDE, depth)
    turned = lax.pad(bias[:, ::-1], jnp.float32(0), [(0, 0, 0), (0, 2 * WIDE - 2 * rel + 1, 1)])
    vmem = pl.BlockSpec(memory_space=pltpu.VMEM)
    f32, bf16, dma = jnp.float32, jnp.bfloat16, pltpu.SemaphoreType.DMA
    att, dq, dkv, dbias = pl.pallas_call(
        pair_kernel,
        out_shape=(
            jax.ShapeDtypeStruct((tok, width), bf16),
            jax.ShapeDtypeStruct((tok, width), bf16),
            jax.ShapeDtypeStruct(kv.shape, bf16),
            jax.ShapeDtypeStruct((heads, rel), f32),
        ),
        in_specs=[vmem, vmem, vmem, pl.BlockSpec(memory_space=pltpu.SMEM), vmem],
        out_specs=(vmem,) * 4,
        scratch_shapes=[
            pltpu.VMEM((heads, tok, depth), bf16),
            pltpu.VMEM((heads, tok, depth), bf16),
            pltpu.VMEM((heads, slots, 2 * STRETCH, depth), bf16),
            pltpu.VMEM((heads, slots, STRETCH, WIDE), f32),
            pltpu.VMEM((heads, slots, STRETCH, WIDE), f32),
            pltpu.VMEM((heads, slots, 2 * STRETCH, WIDE), bf16),
            pltpu.VMEM((heads, tok, 2 * depth), f32),
            pltpu.VMEM((heads, tok, 2 * depth), bf16),
            pltpu.VMEM((heads, tok, 2 * depth), bf16),
            pltpu.VMEM((STRETCH, 128), f32),
            pltpu.VMEM((STRETCH, 128), f32),
            pltpu.VMEM((plane, 8, WIDE), f32),
            pltpu.VMEM((mps, 8, 128), f32),
            dma((2 * heads,)),
            dma((2 * heads,)),
            dma((2,)),
            dma((heads,)),
            dma((heads,)),
            dma((plane,)),
            dma((plane,)),
            dma((mps,)),
            dma((mps,)),
        ],
        compiler_params=pltpu.CompilerParams(
            collective_id=0, has_side_effects=True, vmem_limit_bytes=24 * 1024 * 1024
        ),
    )(queries[0], d_out[0], kv, target, turned)
    dkv = dkv.reshape(slots, heads, NB_LEN, 2, depth).transpose(0, 2, 3, 1, 4)
    dkv = dkv.reshape(slots, NB_LEN, 2, width)
    return att[None], dq[None], dkv[None], dbias


def local(queries, d_out, neighbour_kv, target, bias):
    tok = queries.shape[1]
    fits = (
        lax.axis_size("seq") == 2
        and neighbour_kv.shape[1] == 2 * (tok // STRETCH)
        and tok == 128
        and bias.shape == (4, 191)
        and queries.shape[2] == 512
    )
    run = pair_exchange if fits else shard_exchange
    return run(queries, d_out, neighbour_kv, target, bias)


def solution(mesh):
    in_specs = (
        P("grp", "seq", "mp"),
        P("grp", "seq", "mp"),
        P("grp", "seq", None, None, "mp"),
        P("grp", "seq"),
        P("mp", None),
    )
    out_specs = (
        P("grp", "seq", "mp"),
        P("grp", "seq", "mp"),
        P("grp", "seq", None, None, "mp"),
        P("mp", None),
    )
    return jax.shard_map(local, mesh=mesh, in_specs=in_specs, out_specs=out_specs, check_vma=False)
```

```python
import jax
import jax.numpy as jnp
from jax import lax
from jax.experimental import pallas as pl
from jax.experimental.pallas import tpu as pltpu
from jax.sharding import PartitionSpec as P

STRETCH = 64
NB_LEN = 128


def passed_along(block, axis, distance):
    devices = range(lax.axis_size(axis))
    route = [(i - distance, i) for i in devices if i - distance in devices]
    return lax.ppermute(block, axis, route)


def bias_grid(lookup, row_count, col_count):
    head_num = lookup.shape[0]
    span = row_count + col_count
    padded = jnp.pad(lookup, ((0, 0), (0, 1)))
    flattened = jnp.tile(padded, (1, row_count))
    flattened = jnp.pad(flattened, ((0, 0), (0, row_count)))
    shaped = flattened.reshape(head_num, row_count, span + 1)[:, :, :col_count]
    return shaped[:, :, ::-1]


def bias_fold(grads):
    head_num, row_count, col_count = grads.shape
    turned = grads[:, :, ::-1]
    padded = jnp.pad(turned, ((0, 0), (0, 0), (0, row_count)))
    flattened = padded.reshape(head_num, row_count * (row_count + col_count))
    flattened = flattened[:, : row_count * (row_count + col_count - 1)]
    return jnp.sum(flattened.reshape(head_num, row_count, row_count + col_count - 1), axis=1)


def select_rows(picker, lookup):
    chosen = jnp.dot(
        picker.astype(lookup.dtype),
        lookup,
        preferred_element_type=jnp.float32,
        precision=lax.Precision.HIGHEST,
    )
    return chosen.astype(lookup.dtype)


def slot_places(target_row, owners, capacity, per_owner):
    is_used = target_row >= 0
    owner_of = jnp.where(is_used, target_row // per_owner, -1)
    positions = jnp.arange(target_row.shape[0])
    earlier = (
        (positions[None, :] < positions[:, None])
        & (owner_of[None, :] == owner_of[:, None])
        & is_used[None, :]
    )
    rank_of = jnp.sum(earlier.astype(jnp.int32), axis=1)
    match_owner = owner_of[None, :] == jnp.arange(owners)[:, None]
    match_rank = rank_of[None, :] == jnp.arange(capacity)[:, None]
    return match_owner[:, None, :] & match_rank[None, :, :] & is_used[None, None, :]


def shard_exchange(queries, d_out, neighbour_kv, target, bias):
    tok_rows = queries.shape[1]
    width_dev = queries.shape[2]
    head_count = bias.shape[0]
    head_depth = width_dev // head_count
    stretch_count = tok_rows // STRETCH
    per_owner = 2 * stretch_count
    shard_count = lax.axis_size("seq")
    my_index = lax.axis_index("seq")
    group_size = min(shard_count, per_owner)
    capacity = (per_owner + group_size - 1) // group_size
    seq_stretches = min(2048, tok_rows * shard_count) // STRETCH
    scale_factor = head_depth ** (-0.5)
    bias_rows = bias_grid(bias, STRETCH, NB_LEN).transpose(1, 0, 2)
    q_rows = queries[0]
    g_rows = d_out[0]
    next_pair = passed_along(jnp.stack([q_rows[:STRETCH], g_rows[:STRETCH]]), "seq", -1)
    row_ids = jnp.arange(STRETCH)
    stretch_ids = my_index * stretch_count + jnp.arange(stretch_count)
    is_live = (row_ids[None, :] == 0) | ((stretch_ids[:, None] + 1) % seq_stretches != 0)
    live_rows = is_live.astype(jnp.float32)
    q_win = jnp.concatenate([q_rows, next_pair[0]])[STRETCH - 1 : STRETCH - 1 + tok_rows]
    q_win = q_win.reshape(stretch_count, STRETCH * width_dev)
    g_win = jnp.concatenate([g_rows, next_pair[1]])[STRETCH - 1 : STRETCH - 1 + tok_rows]
    g_win = g_win.reshape(stretch_count, STRETCH, width_dev) * is_live[:, :, None].astype(
        jnp.bfloat16
    )
    g_win = g_win.reshape(stretch_count, STRETCH * width_dev)
    my_targets = target[0]
    slot_count = my_targets.shape[0]
    send_map = slot_places(my_targets, shard_count, capacity, per_owner)
    id_buffer = jnp.sum(jnp.where(send_map, my_targets[None, None, :] + 1, 0), axis=2) - 1
    recv_ids = lax.all_to_all(id_buffer, "seq", split_axis=0, concat_axis=0, tiled=True)
    flat_ids = recv_ids.reshape(shard_count * capacity)
    has_entry = flat_ids >= 0
    local_entry = flat_ids - my_index * per_owner
    entry_pick = (local_entry[:, None] == jnp.arange(per_owner)[None, :]) & has_entry[:, None]
    stretch_pick = (local_entry[:, None] // 2 == jnp.arange(stretch_count)[None, :]) & has_entry[
        :, None
    ]
    back_pick = send_map.reshape(shard_count * capacity, slot_count)
    slot_pick = back_pick.T
    q_send = select_rows(stretch_pick, q_win).reshape(shard_count, capacity, STRETCH * width_dev)
    g_send = select_rows(stretch_pick, g_win).reshape(shard_count, capacity, STRETCH * width_dev)
    q_recv, g_recv = (
        lax.all_to_all(q_send, "seq", split_axis=0, concat_axis=0, tiled=True),
        lax.all_to_all(g_send, "seq", split_axis=0, concat_axis=0, tiled=True),
    )
    q_slots = select_rows(slot_pick, q_recv.reshape(shard_count * capacity, -1))
    q_slots = q_slots.reshape(slot_count, STRETCH, head_count, head_depth)
    stored = neighbour_kv[0]
    key_rows = stored[:, :, 0].reshape(slot_count, NB_LEN, head_count, head_depth)
    value_rows = stored[:, :, 1].reshape(slot_count, NB_LEN, head_count, head_depth)
    scores = jnp.einsum("sihd,sjhd->sihj", q_slots, key_rows, preferred_element_type=jnp.float32)
    scores = scores * scale_factor + bias_rows[None]
    peak_val = jnp.max(scores, axis=-1)
    weights = jnp.exp(scores - peak_val[..., None])
    row_total = jnp.sum(weights, axis=-1)
    partial_value = jnp.einsum(
        "sihj,sjhd->sihd",
        weights.astype(jnp.bfloat16),
        value_rows,
        preferred_element_type=jnp.float32,
    )
    part_send = select_rows(back_pick, partial_value.reshape(slot_count, -1)).reshape(
        shard_count, capacity, -1
    )
    peak_send = select_rows(back_pick, peak_val.reshape(slot_count, -1)).reshape(
        shard_count, capacity, -1
    )
    total_send = select_rows(back_pick, row_total.reshape(slot_count, -1)).reshape(
        shard_count, capacity, -1
    )
    part_recv, peak_recv, total_recv = (
        lax.all_to_all(part_send, "seq", split_axis=0, concat_axis=0, tiled=True),
        lax.all_to_all(peak_send, "seq", split_axis=0, concat_axis=0, tiled=True),
        lax.all_to_all(total_send, "seq", split_axis=0, concat_axis=0, tiled=True),
    )
    entry_back = entry_pick.T
    parts_own = select_rows(entry_back, part_recv.reshape(shard_count * capacity, -1))
    parts_own = parts_own.reshape(stretch_count, 2, STRETCH, head_count, head_depth)
    peaks_own = select_rows(entry_back, peak_recv.reshape(shard_count * capacity, -1))
    peaks_own = peaks_own.reshape(stretch_count, 2, STRETCH, head_count)
    totals_own = select_rows(entry_back, total_recv.reshape(shard_count * capacity, -1))
    totals_own = totals_own.reshape(stretch_count, 2, STRETCH, head_count)
    top_peak = jnp.max(peaks_own, axis=1)
    factor = jnp.exp(peaks_own - top_peak[:, None])
    denominator = jnp.sum(factor * totals_own, axis=1)
    combined = jnp.sum(factor[..., None] * parts_own, axis=1) / denominator[..., None]
    combined = combined * live_rows[:, :, None, None]
    att_win = combined.astype(jnp.bfloat16).reshape(tok_rows, width_dev)
    log_total = top_peak + jnp.log(denominator)
    g_wide = g_win.reshape(stretch_count, STRETCH, head_count, head_depth).astype(jnp.float32)
    inner_dot = jnp.sum(g_wide * combined, axis=-1)
    row_stats = jnp.repeat(jnp.stack([log_total, inner_dot], axis=1), 2, axis=0)
    stats_send = select_rows(entry_pick, row_stats.reshape(per_owner, -1)).reshape(
        shard_count, capacity, -1
    )
    stats_recv = lax.all_to_all(stats_send, "seq", split_axis=0, concat_axis=0, tiled=True)
    g_slots = select_rows(slot_pick, g_recv.reshape(shard_count * capacity, -1))
    g_slots = g_slots.reshape(slot_count, STRETCH, head_count, head_depth)
    stats_slots = select_rows(slot_pick, stats_recv.reshape(shard_count * capacity, -1))
    stats_slots = stats_slots.reshape(slot_count, 2, STRETCH, head_count)
    prob_full = jnp.exp(scores - stats_slots[:, 0][..., None])
    prob_low = prob_full.astype(jnp.bfloat16)
    grad_values = jnp.einsum(
        "sihj,sihd->sjhd", prob_low, g_slots, preferred_element_type=jnp.float32
    )
    grad_prob = jnp.einsum(
        "sihd,sjhd->sihj", g_slots, value_rows, preferred_element_type=jnp.float32
    )
    grad_scores = prob_full * (grad_prob - stats_slots[:, 1][..., None])
    scores_low = grad_scores.astype(jnp.bfloat16)
    grad_rows = (
        jnp.einsum("sihj,sjhd->sihd", scores_low, key_rows, preferred_element_type=jnp.float32)
        * scale_factor
    )
    grad_keys = (
        jnp.einsum("sihj,sihd->sjhd", scores_low, q_slots, preferred_element_type=jnp.float32)
        * scale_factor
    )
    d_kv = jnp.stack(
        [
            grad_keys.reshape(slot_count, NB_LEN, width_dev),
            grad_values.reshape(slot_count, NB_LEN, width_dev),
        ],
        axis=2,
    ).astype(jnp.bfloat16)
    bias_part = bias_fold(jnp.sum(grad_scores, axis=0).transpose(1, 0, 2))
    rows_send = select_rows(back_pick, grad_rows.reshape(slot_count, -1)).reshape(
        shard_count, capacity, -1
    )
    rows_recv = lax.all_to_all(rows_send, "seq", split_axis=0, concat_axis=0, tiled=True)
    grad_entries = select_rows(entry_back, rows_recv.reshape(shard_count * capacity, -1))
    grad_entries = grad_entries.reshape(stretch_count, 2, STRETCH * width_dev)
    grad_win = (
        (grad_entries[:, 0] + grad_entries[:, 1]).astype(jnp.bfloat16).reshape(tok_rows, width_dev)
    )
    both_before = passed_along(
        jnp.stack([att_win[tok_rows - STRETCH :], grad_win[tok_rows - STRETCH :]]), "seq", 1
    )
    att_before = both_before[0]
    grad_before = both_before[1]
    attended = jnp.concatenate([att_before[1:], att_win[: tok_rows - STRETCH + 1]])
    d_query = jnp.concatenate([grad_before[1:], grad_win[: tok_rows - STRETCH + 1]])
    raw_sum = lax.psum(bias_part, ("grp", "seq"))
    squares = lax.psum(jnp.sum(raw_sum * raw_sum), "mp")
    d_bias = raw_sum * jnp.minimum(1.0, 1.0 / jnp.sqrt(squares + 1e-12))
    return (attended[None], d_query[None], d_kv[None], d_bias)


WIDE = 2 * NB_LEN
HALF = 256
MESH = pl.DeviceIdType.MESH


def dot(a, b, contract=((1,), (0,))):
    return lax.dot_general(a, b, (contract, ((), ())), preferred_element_type=jnp.float32)


def iota(shape, axis):
    return lax.broadcasted_iota(jnp.int32, shape, axis)


def pair_kernel(
    q_hbm, g_hbm, kv_hbm, target_hbm, bias_ref,
    att_ref, dq_ref, dkv_ref, dbias_ref,
    target_ref, q_ref, g_ref, kv_pairs, kv_ref, q_peer, g_peer, windows, weights, cotangents, mixed, rows_own, rows_send, rows_recv,
    stat_send, stat_recv, raw_all, norm_all,
    own_sems, kv_sems, in_send, in_recv, stat_send_sems, stat_recv_sems, row_send_sems, row_recv_sems,
    raw_send_sems, raw_recv_sems, norm_send_sems, norm_recv_sems,
):
    heads = bias_ref.shape[0]
    slots = kv_ref.shape[0]
    tok = q_ref.shape[0]
    group = heads // 2
    depth = kv_ref.shape[-1]
    groups, mps = lax.axis_size("grp"), lax.axis_size("mp")
    plane = 2 * groups
    scale = depth ** (-0.5)
    grp, seq, mp = lax.axis_index("grp"), lax.axis_index("seq"), lax.axis_index("mp")
    here = grp * 2 + seq
    peer = {"seq": 1 - seq}

    def plane_at(step):
        there = lax.rem(here + step, plane)
        return {"grp": there // 2, "seq": there % 2}

    def mp_at(step):
        return {"mp": lax.rem(mp + step, mps)}

    own_copies = [
        pltpu.make_async_copy(target_hbm, target_ref, own_sems.at[0]),
        pltpu.make_async_copy(q_hbm.at[0], q_ref, own_sems.at[1]),
        pltpu.make_async_copy(g_hbm.at[0], g_ref, own_sems.at[2]),
    ]
    for copy in own_copies:
        copy.start()
    kv_copies = {}
    for h in range(heads):
        for r in range(slots):
            kv_copies[h, r] = pltpu.make_async_copy(
                kv_hbm.at[0, r, :, :, pl.ds(h * depth, depth)], kv_pairs.at[h, r], kv_sems.at[h, r]
            )
            kv_copies[h, r].start()

    barrier = pltpu.get_barrier_semaphore()
    for step in range(1, plane):
        pl.semaphore_signal(barrier, inc=1, device_id=plane_at(step), device_id_type=MESH)
    for step in range(1, mps):
        pl.semaphore_signal(barrier, inc=1, device_id=mp_at(step), device_id_type=MESH)
    pl.semaphore_wait(barrier, plane - 1 + mps - 1)

    def send(src, dst, send_sem, recv_sem, device):
        copy = pltpu.make_async_remote_copy(
            src_ref=src, dst_ref=dst, send_sem=send_sem, recv_sem=recv_sem,
            device_id=device, device_id_type=MESH,
        )
        copy.start()
        return copy

    in_copies = []
    for h in range(heads):
        cols = pl.ds(h * depth, depth)
        in_copies.append((
            send(q_hbm.at[0, :, cols], q_peer.at[h], in_send.at[2 * h], in_recv.at[2 * h], peer),
            send(g_hbm.at[0, :, cols], g_peer.at[h], in_send.at[2 * h + 1], in_recv.at[2 * h + 1], peer),
        ))

    for copy in own_copies:
        copy.wait()
    entries = [target_ref[0, r] for r in range(slots)]
    firsts = [(STRETCH - 1) + STRETCH * (e // 2) for e in entries]

    def token_of(axis, shape):
        place = iota(shape, axis)
        return jnp.where(place < tok, tok * seq + place, tok * (1 - seq) + place - tok)

    def one_hot(flags):
        return jnp.where(flags, 1.0, 0.0).astype(jnp.bfloat16)

    gather = jnp.concatenate(
        [
            one_hot(token_of(1, (STRETCH, 2 * tok)) == iota((STRETCH, 2 * tok), 0) + firsts[r])
            for r in range(slots)
        ],
        axis=0,
    )
    odd = iota((STRETCH, WIDE), 1) % 2 == 1
    rel = bias_ref.shape[1]
    turn = jnp.where(
        iota((rel, 2 * WIDE), 1) == 2 * (rel - 1) - 2 * iota((rel, 2 * WIDE), 0), 1.0, 0.0
    ).astype(jnp.float32)
    turned = jnp.dot(
        bias_ref[...], turn, preferred_element_type=jnp.float32, precision=lax.Precision.HIGHEST
    )
    for h in range(heads):
        for r in range(slots):
            kv_copies[h, r].wait()
            kv_ref[r, h] = kv_pairs[h, r].reshape(WIDE, depth)
    lane = iota((STRETCH, 128), 1)
    stat_copies = []
    for h in range(heads):
        if h % group == 0:
            table = jnp.zeros((STRETCH, 128), jnp.float32)
        wide = jnp.broadcast_to(turned[h : h + 1, :], (STRETCH, 2 * WIDE))
        grid = pltpu.roll(wide, 2 * WIDE - 126, 1, stride=2, stride_axis=0)[:, :WIDE]
        grid = jnp.where(odd, -1e30, grid)
        cols = pl.ds(h * depth, depth)
        mine = jnp.concatenate([q_ref[:, cols], g_ref[:, cols]], axis=1)
        for copy in in_copies[h]:
            copy.wait_recv()
        other = jnp.concatenate([q_peer[h], g_peer[h]], axis=1)
        picked = dot(gather, jnp.concatenate([mine, other], axis=0)).astype(jnp.bfloat16)
        for r in range(slots):
            rows = picked[r * STRETCH : (r + 1) * STRETCH]
            both = jnp.concatenate([rows[:, :depth], rows[:, depth:]], axis=0)
            windows[h, r] = both
            prod = dot(both, kv_ref[r, h], ((1,), (1,)))
            scores = prod[:STRETCH] * scale + grid
            grad_prob = prod[STRETCH:]
            peak = jnp.max(scores, axis=1, keepdims=True)
            expd = jnp.exp(scores - peak)
            total = jnp.sum(expd, axis=1, keepdims=True)
            expd = pltpu.roll(expd, 1, 1)
            inner = jnp.sum(expd * grad_prob, axis=1, keepdims=True)
            weights[h, r] = expd
            cotangents[h, r] = grad_prob
            base = entries[r] * heads + h
            table = jnp.where(lane == base, peak, table)
            table = jnp.where(lane == base + 32, total, table)
            table = jnp.where(lane == base + 64, inner, table)
        if h % group == group - 1:
            part = h // group
            stat_send[part] = table
            stat_copies.append(send(
                stat_send.at[part], stat_recv.at[part],
                stat_send_sems.at[part], stat_recv_sems.at[part], peer,
            ))

    def partner(x):
        return jnp.where((lane // heads) % 2 == 0, pltpu.roll(x, 128 - heads, 1), pltpu.roll(x, heads, 1))

    scatter = jnp.concatenate(
        [
            one_hot(token_of(0, (2 * tok, STRETCH)) == iota((2 * tok, STRETCH), 1) + firsts[r])
            for r in range(slots)
        ],
        axis=1,
    )
    row8 = iota((8, 2 * WIDE), 0)
    stacked = jnp.zeros((8, 2 * WIDE), jnp.float32)
    row_copies = []
    for h in range(heads):
        if h % group == 0:
            part = h // group
            stat_copies[part].wait_recv()
            table = stat_send[part] + stat_recv[part]
            total = pltpu.roll(table, 96, 1)
            inner = pltpu.roll(table, 64, 1)
            other_peak = partner(table)
            top = jnp.maximum(table, other_peak)
            mine_f, other_f = jnp.exp(table - top), jnp.exp(other_peak - top)
            denominator = mine_f * total + other_f * partner(total)
            inner = (mine_f * inner + other_f * partner(inner)) / denominator
            norm = mine_f / denominator
        bias_sum = jnp.zeros((STRETCH, WIDE), jnp.float32)
        parts = []
        for r in range(slots):
            at = lane == entries[r] * heads + h
            factor = jnp.sum(jnp.where(at, norm, 0.0), axis=1, keepdims=True)
            shift = jnp.sum(jnp.where(at, inner, 0.0), axis=1, keepdims=True)
            prob = weights[h, r] * factor
            grad = prob * (cotangents[h, r] - shift)
            bias_sum = bias_sum + grad
            mix = jnp.concatenate([pltpu.roll(grad, WIDE - 1, 1), prob], axis=0).astype(jnp.bfloat16)
            mixed[h, r] = mix
            out = dot(mix, kv_ref[r, h])
            parts.append(jnp.concatenate([out[STRETCH:], out[:STRETCH] * scale], axis=1).astype(jnp.bfloat16))
        rows = dot(scatter, jnp.concatenate(parts, axis=0))
        rows_own[h] = rows[:tok]
        rows_send[h] = rows[tok:].astype(jnp.bfloat16)
        row_copies.append(send(rows_send.at[h], rows_recv.at[h], row_send_sems.at[h], row_recv_sems.at[h], peer))
        folded = jnp.concatenate([bias_sum, jnp.zeros_like(bias_sum)], axis=1)
        half = STRETCH // 2
        while half >= 8:
            folded = pltpu.roll(folded[:half], 2 * half, 1) + folded[half:]
            half //= 2
        for bit in (4, 2, 1):
            folded = jnp.where((row8 // bit) % 2 == 0, pltpu.roll(folded, 2 * bit, 1), folded)
        stacked = jnp.where(row8 == h, jnp.sum(folded, axis=0, keepdims=True), stacked)
    unmix = jnp.where(
        iota((2 * WIDE, WIDE), 0) == 2 * rel - 1 - 2 * iota((2 * WIDE, WIDE), 1), 1.0, 0.0
    ).astype(jnp.float32)
    raw_all[here] = jnp.dot(
        stacked, unmix, preferred_element_type=jnp.float32, precision=lax.Precision.HIGHEST
    )
    raw_copies = [
        send(raw_all.at[here], raw_all.at[here], raw_send_sems.at[k], raw_recv_sems.at[k], plane_at(k))
        for k in range(1, plane)
    ]

    row_scale = jnp.where(iota((WIDE, depth), 0) % 2 == 0, scale, 1.0)

    def finish_kv(some_heads):
        for h in some_heads:
            for r in range(slots):
                dkv = dot(mixed[h, r], windows[h, r], ((0,), (0,))) * row_scale
                dkv_ref[r, h] = dkv.astype(jnp.bfloat16).reshape(NB_LEN, 2, depth)

    finish_kv(range(group))
    for copy in raw_copies:
        copy.wait_recv()
    raw = raw_all[0]
    for k in range(1, plane):
        raw = raw + raw_all[k]
    norm_all[mp] = jnp.broadcast_to(jnp.sum(raw * raw, keepdims=True), (8, 128))
    norm_copies = [
        send(norm_all.at[mp], norm_all.at[mp], norm_send_sems.at[k], norm_recv_sems.at[k], mp_at(k))
        for k in range(1, mps)
    ]
    finish_kv(range(group, heads))
    for h in range(heads):
        row_copies[h].wait_recv()
        rows = rows_own[h] + rows_recv[h].astype(jnp.float32)
        cols = pl.ds(h * depth, depth)
        att_ref[:, cols] = rows[:, :depth].astype(jnp.bfloat16)
        dq_ref[:, cols] = rows[:, depth:].astype(jnp.bfloat16)
    for copy in norm_copies:
        copy.wait_recv()
    squares = norm_all[0]
    for k in range(1, mps):
        squares = squares + norm_all[k]
    clip = jnp.minimum(1.0, 1.0 / jnp.sqrt(squares[:, :1] + 1e-12))
    dbias_ref[...] = (raw * clip)[: dbias_ref.shape[0], : dbias_ref.shape[1]]
    for pair in in_copies:
        for copy in pair:
            copy.wait_send()
    for copy in stat_copies + raw_copies + row_copies + norm_copies:
        copy.wait_send()


def write_kernel(att, dq, dkv, dbias, att_out, dq_out, dkv_out, dbias_out, sems, kv_sems):
    copies = [
        pltpu.make_async_copy(att, att_out.at[0], sems.at[0]),
        pltpu.make_async_copy(dq, dq_out.at[0], sems.at[1]),
    ]
    slots, heads, _, _, depth = dkv.shape
    for r in range(slots):
        for h in range(heads):
            copies.append(pltpu.make_async_copy(
                dkv.at[r, h], dkv_out.at[0, r, :, :, pl.ds(h * depth, depth)], kv_sems.at[r, h]
            ))
    for copy in copies:
        copy.start()
    dbias_out[...] = dbias[...]
    for copy in copies:
        copy.wait()


def pair_exchange(queries, d_out, neighbour_kv, target, bias):
    _, tok, width = queries.shape
    heads, rel = bias.shape
    depth = width // heads
    slots = neighbour_kv.shape[1]
    plane, mps = 2 * lax.axis_size("grp"), lax.axis_size("mp")
    vmem = pl.BlockSpec(memory_space=pltpu.VMEM)
    hbm = pl.BlockSpec(memory_space=pltpu.HBM)
    f32, bf16, dma = jnp.float32, jnp.bfloat16, pltpu.SemaphoreType.DMA
    parts = pl.pallas_call(
        pair_kernel,
        out_shape=(
            jax.ShapeDtypeStruct((tok, width), bf16),
            jax.ShapeDtypeStruct((tok, width), bf16),
            jax.ShapeDtypeStruct((slots, heads, NB_LEN, 2, depth), bf16),
            jax.ShapeDtypeStruct((heads, rel), f32),
        ),
        in_specs=[hbm, hbm, hbm, hbm, vmem],
        out_specs=(vmem,) * 4,
        scratch_shapes=[
            pltpu.SMEM(target.shape, jnp.int32),
            pltpu.VMEM((tok, width), bf16),
            pltpu.VMEM((tok, width), bf16),
            pltpu.VMEM((heads, slots, NB_LEN, 2, depth), bf16),
            pltpu.VMEM((slots, heads, WIDE, depth), bf16),
            pltpu.VMEM((heads, tok, depth), bf16),
            pltpu.VMEM((heads, tok, depth), bf16),
            pltpu.VMEM((heads, slots, 2 * STRETCH, depth), bf16),
            pltpu.VMEM((heads, slots, STRETCH, WIDE), f32),
            pltpu.VMEM((heads, slots, STRETCH, WIDE), f32),
            pltpu.VMEM((heads, slots, 2 * STRETCH, WIDE), bf16),
            pltpu.VMEM((heads, tok, 2 * depth), f32),
            pltpu.VMEM((heads, tok, 2 * depth), bf16),
            pltpu.VMEM((heads, tok, 2 * depth), bf16),
            pltpu.VMEM((2, STRETCH, 128), f32),
            pltpu.VMEM((2, STRETCH, 128), f32),
            pltpu.VMEM((plane, 8, WIDE), f32),
            pltpu.VMEM((mps, 8, 128), f32),
            dma((3,)),
            dma((heads, slots)),
            dma((2 * heads,)),
            dma((2 * heads,)),
            dma((2,)),
            dma((2,)),
            dma((heads,)),
            dma((heads,)),
            dma((plane,)),
            dma((plane,)),
            dma((mps,)),
            dma((mps,)),
        ],
        compiler_params=pltpu.CompilerParams(
            collective_id=0, has_side_effects=True, vmem_limit_bytes=24 * 1024 * 1024
        ),
    )(queries, d_out, neighbour_kv, target, bias)
    return pl.pallas_call(
        write_kernel,
        out_shape=(
            jax.ShapeDtypeStruct(queries.shape, bf16),
            jax.ShapeDtypeStruct(queries.shape, bf16),
            jax.ShapeDtypeStruct(neighbour_kv.shape, bf16),
            jax.ShapeDtypeStruct(bias.shape, f32),
        ),
        in_specs=[vmem] * 4,
        out_specs=(hbm, hbm, hbm, vmem),
        scratch_shapes=[dma((2,)), dma((slots, heads))],
        compiler_params=pltpu.CompilerParams(vmem_limit_bytes=8 * 1024 * 1024),
    )(*parts)


def local(queries, d_out, neighbour_kv, target, bias):
    tok = queries.shape[1]
    fits = (
        lax.axis_size("seq") == 2
        and neighbour_kv.shape[1] == 2 * (tok // STRETCH)
        and tok == 128
        and bias.shape == (4, 191)
        and queries.shape[2] == 512
    )
    run = pair_exchange if fits else shard_exchange
    return run(queries, d_out, neighbour_kv, target, bias)


def solution(mesh):
    in_specs = (
        P("grp", "seq", "mp"),
        P("grp", "seq", "mp"),
        P("grp", "seq", None, None, "mp"),
        P("grp", "seq"),
        P("mp", None),
    )
    out_specs = (
        P("grp", "seq", "mp"),
        P("grp", "seq", "mp"),
        P("grp", "seq", None, None, "mp"),
        P("mp", None),
    )
    return jax.shard_map(local, mesh=mesh, in_specs=in_specs, out_specs=out_specs, check_vma=False)
```

```python
import jax
import jax.numpy as jnp
from jax import lax
from jax.experimental import pallas as pl
from jax.experimental.pallas import tpu as pltpu
from jax.sharding import PartitionSpec as P

STRETCH = 64
NB_LEN = 128


def passed_along(block, axis, distance):
    devices = range(lax.axis_size(axis))
    route = [(i - distance, i) for i in devices if i - distance in devices]
    return lax.ppermute(block, axis, route)


def bias_grid(lookup, row_count, col_count):
    head_num = lookup.shape[0]
    span = row_count + col_count
    padded = jnp.pad(lookup, ((0, 0), (0, 1)))
    flattened = jnp.tile(padded, (1, row_count))
    flattened = jnp.pad(flattened, ((0, 0), (0, row_count)))
    shaped = flattened.reshape(head_num, row_count, span + 1)[:, :, :col_count]
    return shaped[:, :, ::-1]


def bias_fold(grads):
    head_num, row_count, col_count = grads.shape
    turned = grads[:, :, ::-1]
    padded = jnp.pad(turned, ((0, 0), (0, 0), (0, row_count)))
    flattened = padded.reshape(head_num, row_count * (row_count + col_count))
    flattened = flattened[:, : row_count * (row_count + col_count - 1)]
    return jnp.sum(flattened.reshape(head_num, row_count, row_count + col_count - 1), axis=1)


def select_rows(picker, lookup):
    chosen = jnp.dot(
        picker.astype(lookup.dtype),
        lookup,
        preferred_element_type=jnp.float32,
        precision=lax.Precision.HIGHEST,
    )
    return chosen.astype(lookup.dtype)


def slot_places(target_row, owners, capacity, per_owner):
    is_used = target_row >= 0
    owner_of = jnp.where(is_used, target_row // per_owner, -1)
    positions = jnp.arange(target_row.shape[0])
    earlier = (
        (positions[None, :] < positions[:, None])
        & (owner_of[None, :] == owner_of[:, None])
        & is_used[None, :]
    )
    rank_of = jnp.sum(earlier.astype(jnp.int32), axis=1)
    match_owner = owner_of[None, :] == jnp.arange(owners)[:, None]
    match_rank = rank_of[None, :] == jnp.arange(capacity)[:, None]
    return match_owner[:, None, :] & match_rank[None, :, :] & is_used[None, None, :]


def shard_exchange(queries, d_out, neighbour_kv, target, bias):
    tok_rows = queries.shape[1]
    width_dev = queries.shape[2]
    head_count = bias.shape[0]
    head_depth = width_dev // head_count
    stretch_count = tok_rows // STRETCH
    per_owner = 2 * stretch_count
    shard_count = lax.axis_size("seq")
    my_index = lax.axis_index("seq")
    group_size = min(shard_count, per_owner)
    capacity = (per_owner + group_size - 1) // group_size
    seq_stretches = min(2048, tok_rows * shard_count) // STRETCH
    scale_factor = head_depth ** (-0.5)
    bias_rows = bias_grid(bias, STRETCH, NB_LEN).transpose(1, 0, 2)
    q_rows = queries[0]
    g_rows = d_out[0]
    next_pair = passed_along(jnp.stack([q_rows[:STRETCH], g_rows[:STRETCH]]), "seq", -1)
    row_ids = jnp.arange(STRETCH)
    stretch_ids = my_index * stretch_count + jnp.arange(stretch_count)
    is_live = (row_ids[None, :] == 0) | ((stretch_ids[:, None] + 1) % seq_stretches != 0)
    live_rows = is_live.astype(jnp.float32)
    q_win = jnp.concatenate([q_rows, next_pair[0]])[STRETCH - 1 : STRETCH - 1 + tok_rows]
    q_win = q_win.reshape(stretch_count, STRETCH * width_dev)
    g_win = jnp.concatenate([g_rows, next_pair[1]])[STRETCH - 1 : STRETCH - 1 + tok_rows]
    g_win = g_win.reshape(stretch_count, STRETCH, width_dev) * is_live[:, :, None].astype(
        jnp.bfloat16
    )
    g_win = g_win.reshape(stretch_count, STRETCH * width_dev)
    my_targets = target[0]
    slot_count = my_targets.shape[0]
    send_map = slot_places(my_targets, shard_count, capacity, per_owner)
    id_buffer = jnp.sum(jnp.where(send_map, my_targets[None, None, :] + 1, 0), axis=2) - 1
    recv_ids = lax.all_to_all(id_buffer, "seq", split_axis=0, concat_axis=0, tiled=True)
    flat_ids = recv_ids.reshape(shard_count * capacity)
    has_entry = flat_ids >= 0
    local_entry = flat_ids - my_index * per_owner
    entry_pick = (local_entry[:, None] == jnp.arange(per_owner)[None, :]) & has_entry[:, None]
    stretch_pick = (local_entry[:, None] // 2 == jnp.arange(stretch_count)[None, :]) & has_entry[
        :, None
    ]
    back_pick = send_map.reshape(shard_count * capacity, slot_count)
    slot_pick = back_pick.T
    q_send = select_rows(stretch_pick, q_win).reshape(shard_count, capacity, STRETCH * width_dev)
    g_send = select_rows(stretch_pick, g_win).reshape(shard_count, capacity, STRETCH * width_dev)
    q_recv, g_recv = (
        lax.all_to_all(q_send, "seq", split_axis=0, concat_axis=0, tiled=True),
        lax.all_to_all(g_send, "seq", split_axis=0, concat_axis=0, tiled=True),
    )
    q_slots = select_rows(slot_pick, q_recv.reshape(shard_count * capacity, -1))
    q_slots = q_slots.reshape(slot_count, STRETCH, head_count, head_depth)
    stored = neighbour_kv[0]
    key_rows = stored[:, :, 0].reshape(slot_count, NB_LEN, head_count, head_depth)
    value_rows = stored[:, :, 1].reshape(slot_count, NB_LEN, head_count, head_depth)
    scores = jnp.einsum("sihd,sjhd->sihj", q_slots, key_rows, preferred_element_type=jnp.float32)
    scores = scores * scale_factor + bias_rows[None]
    peak_val = jnp.max(scores, axis=-1)
    weights = jnp.exp(scores - peak_val[..., None])
    row_total = jnp.sum(weights, axis=-1)
    partial_value = jnp.einsum(
        "sihj,sjhd->sihd",
        weights.astype(jnp.bfloat16),
        value_rows,
        preferred_element_type=jnp.float32,
    )
    part_send = select_rows(back_pick, partial_value.reshape(slot_count, -1)).reshape(
        shard_count, capacity, -1
    )
    peak_send = select_rows(back_pick, peak_val.reshape(slot_count, -1)).reshape(
        shard_count, capacity, -1
    )
    total_send = select_rows(back_pick, row_total.reshape(slot_count, -1)).reshape(
        shard_count, capacity, -1
    )
    part_recv, peak_recv, total_recv = (
        lax.all_to_all(part_send, "seq", split_axis=0, concat_axis=0, tiled=True),
        lax.all_to_all(peak_send, "seq", split_axis=0, concat_axis=0, tiled=True),
        lax.all_to_all(total_send, "seq", split_axis=0, concat_axis=0, tiled=True),
    )
    entry_back = entry_pick.T
    parts_own = select_rows(entry_back, part_recv.reshape(shard_count * capacity, -1))
    parts_own = parts_own.reshape(stretch_count, 2, STRETCH, head_count, head_depth)
    peaks_own = select_rows(entry_back, peak_recv.reshape(shard_count * capacity, -1))
    peaks_own = peaks_own.reshape(stretch_count, 2, STRETCH, head_count)
    totals_own = select_rows(entry_back, total_recv.reshape(shard_count * capacity, -1))
    totals_own = totals_own.reshape(stretch_count, 2, STRETCH, head_count)
    top_peak = jnp.max(peaks_own, axis=1)
    factor = jnp.exp(peaks_own - top_peak[:, None])
    denominator = jnp.sum(factor * totals_own, axis=1)
    combined = jnp.sum(factor[..., None] * parts_own, axis=1) / denominator[..., None]
    combined = combined * live_rows[:, :, None, None]
    att_win = combined.astype(jnp.bfloat16).reshape(tok_rows, width_dev)
    log_total = top_peak + jnp.log(denominator)
    g_wide = g_win.reshape(stretch_count, STRETCH, head_count, head_depth).astype(jnp.float32)
    inner_dot = jnp.sum(g_wide * combined, axis=-1)
    row_stats = jnp.repeat(jnp.stack([log_total, inner_dot], axis=1), 2, axis=0)
    stats_send = select_rows(entry_pick, row_stats.reshape(per_owner, -1)).reshape(
        shard_count, capacity, -1
    )
    stats_recv = lax.all_to_all(stats_send, "seq", split_axis=0, concat_axis=0, tiled=True)
    g_slots = select_rows(slot_pick, g_recv.reshape(shard_count * capacity, -1))
    g_slots = g_slots.reshape(slot_count, STRETCH, head_count, head_depth)
    stats_slots = select_rows(slot_pick, stats_recv.reshape(shard_count * capacity, -1))
    stats_slots = stats_slots.reshape(slot_count, 2, STRETCH, head_count)
    prob_full = jnp.exp(scores - stats_slots[:, 0][..., None])
    prob_low = prob_full.astype(jnp.bfloat16)
    grad_values = jnp.einsum(
        "sihj,sihd->sjhd", prob_low, g_slots, preferred_element_type=jnp.float32
    )
    grad_prob = jnp.einsum(
        "sihd,sjhd->sihj", g_slots, value_rows, preferred_element_type=jnp.float32
    )
    grad_scores = prob_full * (grad_prob - stats_slots[:, 1][..., None])
    scores_low = grad_scores.astype(jnp.bfloat16)
    grad_rows = (
        jnp.einsum("sihj,sjhd->sihd", scores_low, key_rows, preferred_element_type=jnp.float32)
        * scale_factor
    )
    grad_keys = (
        jnp.einsum("sihj,sihd->sjhd", scores_low, q_slots, preferred_element_type=jnp.float32)
        * scale_factor
    )
    d_kv = jnp.stack(
        [
            grad_keys.reshape(slot_count, NB_LEN, width_dev),
            grad_values.reshape(slot_count, NB_LEN, width_dev),
        ],
        axis=2,
    ).astype(jnp.bfloat16)
    bias_part = bias_fold(jnp.sum(grad_scores, axis=0).transpose(1, 0, 2))
    rows_send = select_rows(back_pick, grad_rows.reshape(slot_count, -1)).reshape(
        shard_count, capacity, -1
    )
    rows_recv = lax.all_to_all(rows_send, "seq", split_axis=0, concat_axis=0, tiled=True)
    grad_entries = select_rows(entry_back, rows_recv.reshape(shard_count * capacity, -1))
    grad_entries = grad_entries.reshape(stretch_count, 2, STRETCH * width_dev)
    grad_win = (
        (grad_entries[:, 0] + grad_entries[:, 1]).astype(jnp.bfloat16).reshape(tok_rows, width_dev)
    )
    both_before = passed_along(
        jnp.stack([att_win[tok_rows - STRETCH :], grad_win[tok_rows - STRETCH :]]), "seq", 1
    )
    att_before = both_before[0]
    grad_before = both_before[1]
    attended = jnp.concatenate([att_before[1:], att_win[: tok_rows - STRETCH + 1]])
    d_query = jnp.concatenate([grad_before[1:], grad_win[: tok_rows - STRETCH + 1]])
    raw_sum = lax.psum(bias_part, ("grp", "seq"))
    squares = lax.psum(jnp.sum(raw_sum * raw_sum), "mp")
    d_bias = raw_sum * jnp.minimum(1.0, 1.0 / jnp.sqrt(squares + 1e-12))
    return (attended[None], d_query[None], d_kv[None], d_bias)


WIDE = 2 * NB_LEN
VMEM_USE = 60 * 1024 * 1024
MESH = pl.DeviceIdType.MESH


def dot(a, b, contract=((1,), (0,))):
    return lax.dot_general(a, b, (contract, ((), ())), preferred_element_type=jnp.float32)


def iota(shape, axis):
    return lax.broadcasted_iota(jnp.int32, shape, axis)


def pair_kernel(
    q_hbm, g_hbm, kv_hbm, target_hbm, bias_ref,
    att_hbm, dq_hbm, dkv_hbm, dbias_ref,
    target_ref, q_ref, g_ref, kv_pairs, kv_ref, q_peer, g_peer,
    windows, weights, cotangents, mixed, rows_own, rows_send, rows_recv,
    gather_ref, scatter_ref, turned_ref, dkv_pairs, att_ref, dq_ref,
    stat_send, stat_recv, raw_all, norm_all,
    own_sems, kv_sems, in_send, in_recv, stat_send_sems, stat_recv_sems, row_send_sems, row_recv_sems,
    raw_send_sems, raw_recv_sems, norm_send_sems, norm_recv_sems, out_sems, dkv_sems,
):
    heads, rel = bias_ref.shape
    slots = kv_ref.shape[0]
    tok = q_ref.shape[0]
    depth = kv_ref.shape[-1]
    group = heads // 2
    groups, mps = lax.axis_size("grp"), lax.axis_size("mp")
    plane = 2 * groups
    scale = depth ** (-0.5)
    grp, seq, mp = lax.axis_index("grp"), lax.axis_index("seq"), lax.axis_index("mp")
    here = grp * 2 + seq
    peer = {"seq": 1 - seq}

    def plane_at(step):
        there = lax.rem(here + step, plane)
        return {"grp": there // 2, "seq": there % 2}

    def mp_at(step):
        return {"mp": lax.rem(mp + step, mps)}

    def remote(src, dst, send_sem, recv_sem, device):
        return pltpu.make_async_remote_copy(
            src_ref=src, dst_ref=dst, send_sem=send_sem, recv_sem=recv_sem,
            device_id=device, device_id_type=MESH,
        )

    def cols(h):
        return pl.ds(pl.multiple_of(h * depth, depth), depth)

    def q_copy(h):
        return remote(q_hbm.at[0, :, cols(h)], q_peer.at[h], in_send.at[0, h], in_recv.at[0, h], peer)

    def g_copy(h):
        return remote(g_hbm.at[0, :, cols(h)], g_peer.at[h], in_send.at[1, h], in_recv.at[1, h], peer)

    def kv_copy(h, r):
        return pltpu.make_async_copy(kv_hbm.at[0, r, :, :, cols(h)], kv_pairs.at[h, r], kv_sems.at[h, r])

    def stat_copy(part):
        return remote(
            stat_send.at[part], stat_recv.at[part], stat_send_sems.at[part], stat_recv_sems.at[part], peer
        )

    def row_copy(h):
        return remote(rows_send.at[h], rows_recv.at[h], row_send_sems.at[h], row_recv_sems.at[h], peer)

    def raw_copy(k):
        return remote(raw_all.at[here], raw_all.at[here], raw_send_sems.at[k], raw_recv_sems.at[k], plane_at(k))

    def norm_copy(k):
        return remote(norm_all.at[mp], norm_all.at[mp], norm_send_sems.at[k], norm_recv_sems.at[k], mp_at(k))

    def dkv_copy(h, r):
        return pltpu.make_async_copy(dkv_pairs.at[h, r], dkv_hbm.at[0, r, :, :, cols(h)], dkv_sems.at[h, r])

    def out_copies():
        return (
            pltpu.make_async_copy(att_ref, att_hbm.at[0], out_sems.at[0]),
            pltpu.make_async_copy(dq_ref, dq_hbm.at[0], out_sems.at[1]),
        )

    def each(count, body):
        def step(i, carry):
            body(i)
            return carry

        lax.fori_loop(0, count, step, 0)

    barrier = pltpu.get_barrier_semaphore()
    for step in range(1, plane):
        pl.semaphore_signal(barrier, inc=1, device_id=plane_at(step), device_id_type=MESH)
    for step in range(1, mps):
        pl.semaphore_signal(barrier, inc=1, device_id=mp_at(step), device_id_type=MESH)
    own_copies = [
        pltpu.make_async_copy(target_hbm, target_ref, own_sems.at[0]),
        pltpu.make_async_copy(q_hbm.at[0], q_ref, own_sems.at[1]),
        pltpu.make_async_copy(g_hbm.at[0], g_ref, own_sems.at[2]),
    ]
    for copy in own_copies:
        copy.start()

    def start_kv(h):
        for r in range(slots):
            kv_copy(h, r).start()

    each(heads, start_kv)
    pl.semaphore_wait(barrier, plane - 1 + mps - 1)

    def start_rows(h):
        q_copy(h).start()
        g_copy(h).start()

    each(heads, start_rows)

    for copy in own_copies:
        copy.wait()
    entries = [target_ref[0, r] for r in range(slots)]

    def token_of(axis, shape):
        place = iota(shape, axis)
        return jnp.where(place < tok, tok * seq + place, tok * (1 - seq) + place - tok)

    def one_hot(flags):
        return jnp.where(flags, 1.0, 0.0).astype(jnp.bfloat16)

    for r in range(slots):
        rows = pl.ds(r * STRETCH, STRETCH)
        first = (STRETCH - 1) + STRETCH * (entries[r] // 2)
        flat = (STRETCH, 2 * tok)
        gather_ref[rows, :] = one_hot(token_of(1, flat) == iota(flat, 0) + first)
    scatter_ref[...] = gather_ref[...].T
    turn = jnp.where(
        iota((rel, 2 * WIDE), 1) == 2 * (rel - 1) - 2 * iota((rel, 2 * WIDE), 0), 1.0, 0.0
    ).astype(jnp.float32)
    turned = jnp.dot(
        bias_ref[...], turn, preferred_element_type=jnp.float32, precision=lax.Precision.HIGHEST
    )
    for h in range(heads):
        turned_ref[h] = jnp.broadcast_to(turned[h : h + 1], (8, 2 * WIDE))
    odd = iota((STRETCH, WIDE), 1) % 2 == 1
    lane = iota((STRETCH, 128), 1)

    def unpair(h):
        for r in range(slots):
            kv_copy(h, r).wait()
            kv_ref[r, h] = kv_pairs[h, r].reshape(WIDE, depth)

    each(heads, unpair)

    def forward(h, table):
        wide = jnp.broadcast_to(turned_ref[h][:1], (STRETCH, 2 * WIDE))
        grid = pltpu.roll(wide, 2 * WIDE - 126, 1, stride=2, stride_axis=0)[:, :WIDE]
        grid = jnp.where(odd, -1e30, grid)
        mine = jnp.concatenate([q_ref[:, cols(h)], g_ref[:, cols(h)]], axis=1)
        q_copy(h).wait_recv()
        g_copy(h).wait_recv()
        other = jnp.concatenate([q_peer[h], g_peer[h]], axis=1)
        picked = dot(gather_ref[...], jnp.concatenate([mine, other], axis=0)).astype(jnp.bfloat16)
        for r in range(slots):
            rows = picked[r * STRETCH : (r + 1) * STRETCH]
            both = jnp.concatenate([rows[:, :depth], rows[:, depth:]], axis=0)
            windows[h, r] = both
            prod = dot(both, kv_ref[r, h], ((1,), (1,)))
            scores = prod[:STRETCH] * scale + grid
            grad_prob = prod[STRETCH:]
            peak = jnp.max(scores, axis=1, keepdims=True)
            expd = jnp.exp(scores - peak)
            total = jnp.sum(expd, axis=1, keepdims=True)
            expd = pltpu.roll(expd, 1, 1)
            inner = jnp.sum(expd * grad_prob, axis=1, keepdims=True)
            weights[h, r] = expd
            cotangents[h, r] = grad_prob
            base = entries[r] * heads + h
            table = jnp.where(lane == base, peak, table)
            table = jnp.where(lane == base + 32, total, table)
            table = jnp.where(lane == base + 64, inner, table)
        return table

    def forward_part(part):
        table = jnp.zeros((STRETCH, 128), jnp.float32)
        table = lax.fori_loop(part * group, part * group + group, forward, table)
        stat_send[part] = table
        stat_copy(part).start()

    each(2, forward_part)

    def partner(x):
        return jnp.where((lane // heads) % 2 == 0, pltpu.roll(x, 128 - heads, 1), pltpu.roll(x, heads, 1))

    row8 = iota((8, 2 * WIDE), 0)

    def backward_part(part, stacked):
        stat_copy(part).wait_recv()
        table = stat_send[part] + stat_recv[part]
        total = pltpu.roll(table, 96, 1)
        inner = pltpu.roll(table, 64, 1)
        other_peak = partner(table)
        top = jnp.maximum(table, other_peak)
        mine_f, other_f = jnp.exp(table - top), jnp.exp(other_peak - top)
        denominator = mine_f * total + other_f * partner(total)
        inner = (mine_f * inner + other_f * partner(inner)) / denominator
        norm = mine_f / denominator

        def backward(h, stacked):
            bias_sum = jnp.zeros((STRETCH, WIDE), jnp.float32)
            parts = []
            for r in range(slots):
                at = lane == entries[r] * heads + h
                factor = jnp.sum(jnp.where(at, norm, 0.0), axis=1, keepdims=True)
                shift = jnp.sum(jnp.where(at, inner, 0.0), axis=1, keepdims=True)
                prob = weights[h, r] * factor
                grad = prob * (cotangents[h, r] - shift)
                bias_sum = bias_sum + grad
                mix = jnp.concatenate([pltpu.roll(grad, WIDE - 1, 1), prob], axis=0).astype(jnp.bfloat16)
                mixed[h, r] = mix
                out = dot(mix, kv_ref[r, h])
                parts.append(
                    jnp.concatenate([out[STRETCH:], out[:STRETCH] * scale], axis=1).astype(jnp.bfloat16)
                )
            rows = dot(scatter_ref[...], jnp.concatenate(parts, axis=0))
            rows_own[h] = rows[:tok]
            rows_send[h] = rows[tok:].astype(jnp.bfloat16)
            row_copy(h).start()
            folded = jnp.concatenate([bias_sum, jnp.zeros_like(bias_sum)], axis=1)
            half = STRETCH // 2
            while half >= 8:
                folded = pltpu.roll(folded[:half], 2 * half, 1) + folded[half:]
                half //= 2
            for bit in (4, 2, 1):
                folded = jnp.where((row8 // bit) % 2 == 0, pltpu.roll(folded, 2 * bit, 1), folded)
            return jnp.where(row8 == h, jnp.sum(folded, axis=0, keepdims=True), stacked)

        return lax.fori_loop(part * group, part * group + group, backward, stacked)

    stacked = lax.fori_loop(0, 2, backward_part, jnp.zeros((8, 2 * WIDE), jnp.float32))
    unmix = jnp.where(
        iota((2 * WIDE, WIDE), 0) == 2 * rel - 1 - 2 * iota((2 * WIDE, WIDE), 1), 1.0, 0.0
    ).astype(jnp.float32)
    raw_all[here] = jnp.dot(
        stacked, unmix, preferred_element_type=jnp.float32, precision=lax.Precision.HIGHEST
    )
    for k in range(1, plane):
        raw_copy(k).start()

    row_scale = jnp.where(iota((WIDE, depth), 0) % 2 == 0, scale, 1.0)

    def finish_kv(h):
        for r in range(slots):
            dkv = dot(mixed[h, r], windows[h, r], ((0,), (0,))) * row_scale
            dkv_pairs[h, r] = dkv.astype(jnp.bfloat16).reshape(NB_LEN, 2, depth)
            dkv_copy(h, r).start()

    each(heads, finish_kv)
    for k in range(1, plane):
        raw_copy(k).wait_recv()
    raw = raw_all[0]
    for k in range(1, plane):
        raw = raw + raw_all[k]
    norm_all[mp] = jnp.broadcast_to(jnp.sum(raw * raw, keepdims=True), (8, 128))
    for k in range(1, mps):
        norm_copy(k).start()

    def finish_rows(h):
        row_copy(h).wait_recv()
        rows = rows_own[h] + rows_recv[h].astype(jnp.float32)
        att_ref[:, cols(h)] = rows[:, :depth].astype(jnp.bfloat16)
        dq_ref[:, cols(h)] = rows[:, depth:].astype(jnp.bfloat16)

    each(heads, finish_rows)
    for copy in out_copies():
        copy.start()
    for k in range(1, mps):
        norm_copy(k).wait_recv()
    squares = norm_all[0]
    for k in range(1, mps):
        squares = squares + norm_all[k]
    clip = jnp.minimum(1.0, 1.0 / jnp.sqrt(squares[:, :1] + 1e-12))
    dbias_ref[...] = (raw * clip)[:heads, :rel]

    def drain(h):
        q_copy(h).wait_send()
        g_copy(h).wait_send()
        row_copy(h).wait_send()
        for r in range(slots):
            dkv_copy(h, r).wait()

    each(heads, drain)
    for part in range(2):
        stat_copy(part).wait_send()
    for k in range(1, plane):
        raw_copy(k).wait_send()
    for k in range(1, mps):
        norm_copy(k).wait_send()
    for copy in out_copies():
        copy.wait()


def write_kernel(att, dq, dkv, dbias, att_out, dq_out, dkv_out, dbias_out, sems):
    slots = dkv.shape[1]
    copies = [
        pltpu.make_async_copy(att, att_out, sems.at[slots]),
        pltpu.make_async_copy(dq, dq_out, sems.at[slots + 1]),
        pltpu.make_async_copy(dbias, dbias_out, sems.at[slots + 2]),
    ]
    for r in range(slots):
        copies.append(pltpu.make_async_copy(dkv.at[0, r], dkv_out.at[0, r], sems.at[r]))
    for copy in copies:
        copy.start()
    for copy in copies:
        copy.wait()


def pair_exchange(queries, d_out, neighbour_kv, target, bias):
    _, tok, width = queries.shape
    heads = bias.shape[0]
    depth = width // heads
    slots = neighbour_kv.shape[1]
    plane, mps = 2 * lax.axis_size("grp"), lax.axis_size("mp")
    vmem = pl.BlockSpec(memory_space=pltpu.VMEM)
    hbm = pl.BlockSpec(memory_space=pltpu.HBM)
    f32, bf16, dma = jnp.float32, jnp.bfloat16, pltpu.SemaphoreType.DMA
    results = tuple(jax.ShapeDtypeStruct(x.shape, x.dtype) for x in (queries, d_out, neighbour_kv, bias))
    parts = pl.pallas_call(
        pair_kernel,
        out_shape=results,
        in_specs=[hbm, hbm, hbm, hbm, vmem],
        out_specs=(hbm, hbm, hbm, vmem),
        scratch_shapes=[
            pltpu.SMEM(target.shape, jnp.int32),
            pltpu.VMEM((tok, width), bf16),
            pltpu.VMEM((tok, width), bf16),
            pltpu.VMEM((heads, slots, NB_LEN, 2, depth), bf16),
            pltpu.VMEM((slots, heads, WIDE, depth), bf16),
            pltpu.VMEM((heads, tok, depth), bf16),
            pltpu.VMEM((heads, tok, depth), bf16),
            pltpu.VMEM((heads, slots, 2 * STRETCH, depth), bf16),
            pltpu.VMEM((heads, slots, STRETCH, WIDE), f32),
            pltpu.VMEM((heads, slots, STRETCH, WIDE), f32),
            pltpu.VMEM((heads, slots, 2 * STRETCH, WIDE), bf16),
            pltpu.VMEM((heads, tok, 2 * depth), f32),
            pltpu.VMEM((heads, tok, 2 * depth), bf16),
            pltpu.VMEM((heads, tok, 2 * depth), bf16),
            pltpu.VMEM((slots * STRETCH, 2 * tok), bf16),
            pltpu.VMEM((2 * tok, slots * STRETCH), bf16),
            pltpu.VMEM((heads, 8, 2 * WIDE), f32),
            pltpu.VMEM((heads, slots, NB_LEN, 2, depth), bf16),
            pltpu.VMEM((tok, width), bf16),
            pltpu.VMEM((tok, width), bf16),
            pltpu.VMEM((2, STRETCH, 128), f32),
            pltpu.VMEM((2, STRETCH, 128), f32),
            pltpu.VMEM((plane, 8, WIDE), f32),
            pltpu.VMEM((mps, 8, 128), f32),
            dma((3,)),
            dma((heads, slots)),
            dma((2, heads)),
            dma((2, heads)),
            dma((2,)),
            dma((2,)),
            dma((heads,)),
            dma((heads,)),
            dma((plane,)),
            dma((plane,)),
            dma((mps,)),
            dma((mps,)),
            dma((2,)),
            dma((heads, slots)),
        ],
        compiler_params=pltpu.CompilerParams(
            collective_id=0, has_side_effects=True, vmem_limit_bytes=VMEM_USE
        ),
    )(queries, d_out, neighbour_kv, target, bias)
    return pl.pallas_call(
        write_kernel,
        out_shape=results,
        in_specs=[hbm] * 4,
        out_specs=(hbm,) * 4,
        scratch_shapes=[dma((slots + 3,))],
        compiler_params=pltpu.CompilerParams(vmem_limit_bytes=VMEM_USE),
    )(*parts)


def local(queries, d_out, neighbour_kv, target, bias):
    tok = queries.shape[1]
    fits = (
        lax.axis_size("seq") == 2
        and neighbour_kv.shape[1] == 2 * (tok // STRETCH)
        and tok == 128
        and bias.shape == (4, 191)
        and queries.shape[2] == 512
    )
    run = pair_exchange if fits else shard_exchange
    return run(queries, d_out, neighbour_kv, target, bias)


def solution(mesh):
    in_specs = (
        P("grp", "seq", "mp"),
        P("grp", "seq", "mp"),
        P("grp", "seq", None, None, "mp"),
        P("grp", "seq"),
        P("mp", None),
    )
    out_specs = (
        P("grp", "seq", "mp"),
        P("grp", "seq", "mp"),
        P("grp", "seq", None, None, "mp"),
        P("mp", None),
    )
    return jax.shard_map(local, mesh=mesh, in_specs=in_specs, out_specs=out_specs, check_vma=False)
```

```python
import jax
import jax.numpy as jnp
from jax import lax
from jax.experimental import pallas as pl
from jax.experimental.pallas import tpu as pltpu
from jax.sharding import PartitionSpec as P

STRETCH = 64
NB_LEN = 128


def passed_along(block, axis, distance):
    devices = range(lax.axis_size(axis))
    route = [(i - distance, i) for i in devices if i - distance in devices]
    return lax.ppermute(block, axis, route)


def bias_grid(lookup, row_count, col_count):
    head_num = lookup.shape[0]
    span = row_count + col_count
    padded = jnp.pad(lookup, ((0, 0), (0, 1)))
    flattened = jnp.tile(padded, (1, row_count))
    flattened = jnp.pad(flattened, ((0, 0), (0, row_count)))
    shaped = flattened.reshape(head_num, row_count, span + 1)[:, :, :col_count]
    return shaped[:, :, ::-1]


def bias_fold(grads):
    head_num, row_count, col_count = grads.shape
    turned = grads[:, :, ::-1]
    padded = jnp.pad(turned, ((0, 0), (0, 0), (0, row_count)))
    flattened = padded.reshape(head_num, row_count * (row_count + col_count))
    flattened = flattened[:, : row_count * (row_count + col_count - 1)]
    return jnp.sum(flattened.reshape(head_num, row_count, row_count + col_count - 1), axis=1)


def select_rows(picker, lookup):
    chosen = jnp.dot(
        picker.astype(lookup.dtype),
        lookup,
        preferred_element_type=jnp.float32,
        precision=lax.Precision.HIGHEST,
    )
    return chosen.astype(lookup.dtype)


def slot_places(target_row, owners, capacity, per_owner):
    is_used = target_row >= 0
    owner_of = jnp.where(is_used, target_row // per_owner, -1)
    positions = jnp.arange(target_row.shape[0])
    earlier = (
        (positions[None, :] < positions[:, None])
        & (owner_of[None, :] == owner_of[:, None])
        & is_used[None, :]
    )
    rank_of = jnp.sum(earlier.astype(jnp.int32), axis=1)
    match_owner = owner_of[None, :] == jnp.arange(owners)[:, None]
    match_rank = rank_of[None, :] == jnp.arange(capacity)[:, None]
    return match_owner[:, None, :] & match_rank[None, :, :] & is_used[None, None, :]


def shard_exchange(queries, d_out, neighbour_kv, target, bias):
    tok_rows = queries.shape[1]
    width_dev = queries.shape[2]
    head_count = bias.shape[0]
    head_depth = width_dev // head_count
    stretch_count = tok_rows // STRETCH
    per_owner = 2 * stretch_count
    shard_count = lax.axis_size("seq")
    my_index = lax.axis_index("seq")
    group_size = min(shard_count, per_owner)
    capacity = (per_owner + group_size - 1) // group_size
    seq_stretches = min(2048, tok_rows * shard_count) // STRETCH
    scale_factor = head_depth ** (-0.5)
    bias_rows = bias_grid(bias, STRETCH, NB_LEN).transpose(1, 0, 2)
    q_rows = queries[0]
    g_rows = d_out[0]
    next_pair = passed_along(jnp.stack([q_rows[:STRETCH], g_rows[:STRETCH]]), "seq", -1)
    row_ids = jnp.arange(STRETCH)
    stretch_ids = my_index * stretch_count + jnp.arange(stretch_count)
    is_live = (row_ids[None, :] == 0) | ((stretch_ids[:, None] + 1) % seq_stretches != 0)
    live_rows = is_live.astype(jnp.float32)
    q_win = jnp.concatenate([q_rows, next_pair[0]])[STRETCH - 1 : STRETCH - 1 + tok_rows]
    q_win = q_win.reshape(stretch_count, STRETCH * width_dev)
    g_win = jnp.concatenate([g_rows, next_pair[1]])[STRETCH - 1 : STRETCH - 1 + tok_rows]
    g_win = g_win.reshape(stretch_count, STRETCH, width_dev) * is_live[:, :, None].astype(
        jnp.bfloat16
    )
    g_win = g_win.reshape(stretch_count, STRETCH * width_dev)
    my_targets = target[0]
    slot_count = my_targets.shape[0]
    send_map = slot_places(my_targets, shard_count, capacity, per_owner)
    id_buffer = jnp.sum(jnp.where(send_map, my_targets[None, None, :] + 1, 0), axis=2) - 1
    recv_ids = lax.all_to_all(id_buffer, "seq", split_axis=0, concat_axis=0, tiled=True)
    flat_ids = recv_ids.reshape(shard_count * capacity)
    has_entry = flat_ids >= 0
    local_entry = flat_ids - my_index * per_owner
    entry_pick = (local_entry[:, None] == jnp.arange(per_owner)[None, :]) & has_entry[:, None]
    stretch_pick = (local_entry[:, None] // 2 == jnp.arange(stretch_count)[None, :]) & has_entry[
        :, None
    ]
    back_pick = send_map.reshape(shard_count * capacity, slot_count)
    slot_pick = back_pick.T
    q_send = select_rows(stretch_pick, q_win).reshape(shard_count, capacity, STRETCH * width_dev)
    g_send = select_rows(stretch_pick, g_win).reshape(shard_count, capacity, STRETCH * width_dev)
    q_recv, g_recv = (
        lax.all_to_all(q_send, "seq", split_axis=0, concat_axis=0, tiled=True),
        lax.all_to_all(g_send, "seq", split_axis=0, concat_axis=0, tiled=True),
    )
    q_slots = select_rows(slot_pick, q_recv.reshape(shard_count * capacity, -1))
    q_slots = q_slots.reshape(slot_count, STRETCH, head_count, head_depth)
    stored = neighbour_kv[0]
    key_rows = stored[:, :, 0].reshape(slot_count, NB_LEN, head_count, head_depth)
    value_rows = stored[:, :, 1].reshape(slot_count, NB_LEN, head_count, head_depth)
    scores = jnp.einsum("sihd,sjhd->sihj", q_slots, key_rows, preferred_element_type=jnp.float32)
    scores = scores * scale_factor + bias_rows[None]
    peak_val = jnp.max(scores, axis=-1)
    weights = jnp.exp(scores - peak_val[..., None])
    row_total = jnp.sum(weights, axis=-1)
    partial_value = jnp.einsum(
        "sihj,sjhd->sihd",
        weights.astype(jnp.bfloat16),
        value_rows,
        preferred_element_type=jnp.float32,
    )
    part_send = select_rows(back_pick, partial_value.reshape(slot_count, -1)).reshape(
        shard_count, capacity, -1
    )
    peak_send = select_rows(back_pick, peak_val.reshape(slot_count, -1)).reshape(
        shard_count, capacity, -1
    )
    total_send = select_rows(back_pick, row_total.reshape(slot_count, -1)).reshape(
        shard_count, capacity, -1
    )
    part_recv, peak_recv, total_recv = (
        lax.all_to_all(part_send, "seq", split_axis=0, concat_axis=0, tiled=True),
        lax.all_to_all(peak_send, "seq", split_axis=0, concat_axis=0, tiled=True),
        lax.all_to_all(total_send, "seq", split_axis=0, concat_axis=0, tiled=True),
    )
    entry_back = entry_pick.T
    parts_own = select_rows(entry_back, part_recv.reshape(shard_count * capacity, -1))
    parts_own = parts_own.reshape(stretch_count, 2, STRETCH, head_count, head_depth)
    peaks_own = select_rows(entry_back, peak_recv.reshape(shard_count * capacity, -1))
    peaks_own = peaks_own.reshape(stretch_count, 2, STRETCH, head_count)
    totals_own = select_rows(entry_back, total_recv.reshape(shard_count * capacity, -1))
    totals_own = totals_own.reshape(stretch_count, 2, STRETCH, head_count)
    top_peak = jnp.max(peaks_own, axis=1)
    factor = jnp.exp(peaks_own - top_peak[:, None])
    denominator = jnp.sum(factor * totals_own, axis=1)
    combined = jnp.sum(factor[..., None] * parts_own, axis=1) / denominator[..., None]
    combined = combined * live_rows[:, :, None, None]
    att_win = combined.astype(jnp.bfloat16).reshape(tok_rows, width_dev)
    log_total = top_peak + jnp.log(denominator)
    g_wide = g_win.reshape(stretch_count, STRETCH, head_count, head_depth).astype(jnp.float32)
    inner_dot = jnp.sum(g_wide * combined, axis=-1)
    row_stats = jnp.repeat(jnp.stack([log_total, inner_dot], axis=1), 2, axis=0)
    stats_send = select_rows(entry_pick, row_stats.reshape(per_owner, -1)).reshape(
        shard_count, capacity, -1
    )
    stats_recv = lax.all_to_all(stats_send, "seq", split_axis=0, concat_axis=0, tiled=True)
    g_slots = select_rows(slot_pick, g_recv.reshape(shard_count * capacity, -1))
    g_slots = g_slots.reshape(slot_count, STRETCH, head_count, head_depth)
    stats_slots = select_rows(slot_pick, stats_recv.reshape(shard_count * capacity, -1))
    stats_slots = stats_slots.reshape(slot_count, 2, STRETCH, head_count)
    prob_full = jnp.exp(scores - stats_slots[:, 0][..., None])
    prob_low = prob_full.astype(jnp.bfloat16)
    grad_values = jnp.einsum(
        "sihj,sihd->sjhd", prob_low, g_slots, preferred_element_type=jnp.float32
    )
    grad_prob = jnp.einsum(
        "sihd,sjhd->sihj", g_slots, value_rows, preferred_element_type=jnp.float32
    )
    grad_scores = prob_full * (grad_prob - stats_slots[:, 1][..., None])
    scores_low = grad_scores.astype(jnp.bfloat16)
    grad_rows = (
        jnp.einsum("sihj,sjhd->sihd", scores_low, key_rows, preferred_element_type=jnp.float32)
        * scale_factor
    )
    grad_keys = (
        jnp.einsum("sihj,sihd->sjhd", scores_low, q_slots, preferred_element_type=jnp.float32)
        * scale_factor
    )
    d_kv = jnp.stack(
        [
            grad_keys.reshape(slot_count, NB_LEN, width_dev),
            grad_values.reshape(slot_count, NB_LEN, width_dev),
        ],
        axis=2,
    ).astype(jnp.bfloat16)
    bias_part = bias_fold(jnp.sum(grad_scores, axis=0).transpose(1, 0, 2))
    rows_send = select_rows(back_pick, grad_rows.reshape(slot_count, -1)).reshape(
        shard_count, capacity, -1
    )
    rows_recv = lax.all_to_all(rows_send, "seq", split_axis=0, concat_axis=0, tiled=True)
    grad_entries = select_rows(entry_back, rows_recv.reshape(shard_count * capacity, -1))
    grad_entries = grad_entries.reshape(stretch_count, 2, STRETCH * width_dev)
    grad_win = (
        (grad_entries[:, 0] + grad_entries[:, 1]).astype(jnp.bfloat16).reshape(tok_rows, width_dev)
    )
    both_before = passed_along(
        jnp.stack([att_win[tok_rows - STRETCH :], grad_win[tok_rows - STRETCH :]]), "seq", 1
    )
    att_before = both_before[0]
    grad_before = both_before[1]
    attended = jnp.concatenate([att_before[1:], att_win[: tok_rows - STRETCH + 1]])
    d_query = jnp.concatenate([grad_before[1:], grad_win[: tok_rows - STRETCH + 1]])
    raw_sum = lax.psum(bias_part, ("grp", "seq"))
    squares = lax.psum(jnp.sum(raw_sum * raw_sum), "mp")
    d_bias = raw_sum * jnp.minimum(1.0, 1.0 / jnp.sqrt(squares + 1e-12))
    return (attended[None], d_query[None], d_kv[None], d_bias)


WIDE = 2 * NB_LEN
VMEM_USE = 60 * 1024 * 1024
MESH = pl.DeviceIdType.MESH


def dot(a, b, contract=((1,), (0,))):
    return lax.dot_general(a, b, (contract, ((), ())), preferred_element_type=jnp.float32)


def iota(shape, axis):
    return lax.broadcasted_iota(jnp.int32, shape, axis)


def pair_kernel(
    q_hbm, g_hbm, kv_hbm, target_hbm, bias_ref,
    att_hbm, dq_hbm, dkv_hbm, dbias_ref,
    target_ref, q_ref, g_ref, kv_pairs, kv_ref, q_peer, g_peer,
    windows, weights, cotangents, mixed, rows_own, rows_send, rows_recv,
    gather_ref, scatter_ref, turned_ref, dkv_pairs, att_ref, dq_ref,
    stat_send, stat_recv, raw_all, norm_all,
    own_sems, kv_sems, in_send, in_recv, stat_send_sems, stat_recv_sems, row_send_sems, row_recv_sems,
    raw_send_sems, raw_recv_sems, norm_send_sems, norm_recv_sems, out_sems, dkv_sems,
):
    heads, rel = bias_ref.shape
    slots = kv_ref.shape[0]
    tok = q_ref.shape[0]
    depth = kv_ref.shape[-1]
    lead = (STRETCH - 1) // 16 * 16
    late = pl.ds(lead, tok - lead)
    early = pl.ds(0, lead)
    groups, mps = lax.axis_size("grp"), lax.axis_size("mp")
    plane = 2 * groups
    scale = depth ** (-0.5)
    grp, seq, mp = lax.axis_index("grp"), lax.axis_index("seq"), lax.axis_index("mp")
    here = grp * 2 + seq
    peer = {"seq": 1 - seq}

    def plane_at(step):
        there = lax.rem(here + step, plane)
        return {"grp": there // 2, "seq": there % 2}

    def mp_at(step):
        return {"mp": lax.rem(mp + step, mps)}

    def remote(src, dst, send_sem, recv_sem, device):
        return pltpu.make_async_remote_copy(
            src_ref=src, dst_ref=dst, send_sem=send_sem, recv_sem=recv_sem,
            device_id=device, device_id_type=MESH,
        )

    def cols(h):
        return pl.ds(pl.multiple_of(h * depth, depth), depth)

    def q_copy(h, rows, lane):
        return remote(
            q_hbm.at[0, rows, cols(h)], q_peer.at[h, rows], in_send.at[lane, h], in_recv.at[lane, h], peer
        )

    def g_copy(h, rows, lane):
        return remote(
            g_hbm.at[0, rows, cols(h)], g_peer.at[h, rows], in_send.at[lane, h], in_recv.at[lane, h], peer
        )

    def in_late(h):
        return q_copy(h, late, 0), g_copy(h, late, 1)

    def in_early(h):
        return q_copy(h, early, 2), g_copy(h, early, 3)

    def kv_copy(h, r):
        return pltpu.make_async_copy(kv_hbm.at[0, r, :, :, cols(h)], kv_pairs.at[h, r], kv_sems.at[h, r])

    def stat_copy(part):
        return remote(
            stat_send.at[part], stat_recv.at[part], stat_send_sems.at[part], stat_recv_sems.at[part], peer
        )

    def row_copy(h, rows, lane):
        return remote(
            rows_send.at[h, rows], rows_recv.at[h, rows],
            row_send_sems.at[lane, h], row_recv_sems.at[lane, h], peer,
        )

    def row_late(h):
        return row_copy(h, late, 0)

    def row_early(h):
        return row_copy(h, early, 1)

    def raw_copy(k):
        return remote(raw_all.at[here], raw_all.at[here], raw_send_sems.at[k], raw_recv_sems.at[k], plane_at(k))

    def norm_copy(k):
        return remote(norm_all.at[mp], norm_all.at[mp], norm_send_sems.at[k], norm_recv_sems.at[k], mp_at(k))

    def dkv_copy(h, r):
        return pltpu.make_async_copy(dkv_pairs.at[h, r], dkv_hbm.at[0, r, :, :, cols(h)], dkv_sems.at[h, r])

    def out_copies():
        return (
            pltpu.make_async_copy(att_ref, att_hbm.at[0], out_sems.at[0]),
            pltpu.make_async_copy(dq_ref, dq_hbm.at[0], out_sems.at[1]),
        )

    def each(count, body):
        def step(i, carry):
            body(i)
            return carry

        lax.fori_loop(0, count, step, 0)

    barrier = pltpu.get_barrier_semaphore()
    for step in range(1, plane):
        pl.semaphore_signal(barrier, inc=1, device_id=plane_at(step), device_id_type=MESH)
    for step in range(1, mps):
        pl.semaphore_signal(barrier, inc=1, device_id=mp_at(step), device_id_type=MESH)
    own_copies = [
        pltpu.make_async_copy(target_hbm, target_ref, own_sems.at[0]),
        pltpu.make_async_copy(q_hbm.at[0], q_ref, own_sems.at[1]),
        pltpu.make_async_copy(g_hbm.at[0], g_ref, own_sems.at[2]),
    ]
    for copy in own_copies:
        copy.start()

    def start_kv(h):
        for r in range(slots):
            kv_copy(h, r).start()

    each(heads, start_kv)
    pl.semaphore_wait(barrier, plane - 1 + mps - 1)

    def start_rows(h):
        for copy in in_late(h):
            copy.start()

        @pl.when(seq == 1)
        def _():
            for copy in in_early(h):
                copy.start()

    each(heads, start_rows)

    @pl.when(seq == 1)
    def _():
        q_peer[:, early] = jnp.zeros((heads, lead, depth), jnp.bfloat16)
        g_peer[:, early] = jnp.zeros((heads, lead, depth), jnp.bfloat16)

    @pl.when(seq == 0)
    def _():
        rows_recv[:, early] = jnp.zeros((heads, lead, 2 * depth), jnp.bfloat16)

    for copy in own_copies:
        copy.wait()
    entries = [target_ref[0, r] for r in range(slots)]

    def token_of(axis, shape):
        place = iota(shape, axis)
        return jnp.where(place < tok, tok * seq + place, tok * (1 - seq) + place - tok)

    def one_hot(flags):
        return jnp.where(flags, 1.0, 0.0).astype(jnp.bfloat16)

    for r in range(slots):
        rows = pl.ds(r * STRETCH, STRETCH)
        first = (STRETCH - 1) + STRETCH * (entries[r] // 2)
        flat = (STRETCH, 2 * tok)
        gather_ref[rows, :] = one_hot(token_of(1, flat) == iota(flat, 0) + first)
    scatter_ref[...] = gather_ref[...].T
    turn = jnp.where(
        iota((rel, 2 * WIDE), 1) == 2 * (rel - 1) - 2 * iota((rel, 2 * WIDE), 0), 1.0, 0.0
    ).astype(jnp.float32)
    turned = jnp.dot(
        bias_ref[...], turn, preferred_element_type=jnp.float32, precision=lax.Precision.HIGHEST
    )
    for h in range(heads):
        turned_ref[h] = jnp.broadcast_to(turned[h : h + 1], (8, 2 * WIDE))
    odd = iota((STRETCH, WIDE), 1) % 2 == 1
    lane = iota((STRETCH, 128), 1)

    def unpair(h):
        for r in range(slots):
            kv_copy(h, r).wait()
            kv_ref[r, h] = kv_pairs[h, r].reshape(WIDE, depth)

    each(heads, unpair)

    def forward(h):
        table = jnp.zeros((STRETCH, 128), jnp.float32)
        wide = jnp.broadcast_to(turned_ref[h][:1], (STRETCH, 2 * WIDE))
        grid = pltpu.roll(wide, 2 * WIDE - 126, 1, stride=2, stride_axis=0)[:, :WIDE]
        grid = jnp.where(odd, -1e30, grid)
        mine = jnp.concatenate([q_ref[:, cols(h)], g_ref[:, cols(h)]], axis=1)
        for copy in in_late(h):
            copy.wait_recv()

        @pl.when(seq == 0)
        def _():
            for copy in in_early(h):
                copy.wait_recv()

        other = jnp.concatenate([q_peer[h], g_peer[h]], axis=1)
        picked = dot(gather_ref[...], jnp.concatenate([mine, other], axis=0)).astype(jnp.bfloat16)
        for r in range(slots):
            rows = picked[r * STRETCH : (r + 1) * STRETCH]
            both = jnp.concatenate([rows[:, :depth], rows[:, depth:]], axis=0)
            windows[h, r] = both
            prod = dot(both, kv_ref[r, h], ((1,), (1,)))
            scores = prod[:STRETCH] * scale + grid
            grad_prob = prod[STRETCH:]
            peak = jnp.max(scores, axis=1, keepdims=True)
            expd = jnp.exp(scores - peak)
            total = jnp.sum(expd, axis=1, keepdims=True)
            expd = pltpu.roll(expd, 1, 1)
            inner = jnp.sum(expd * grad_prob, axis=1, keepdims=True)
            weights[h, r] = expd
            cotangents[h, r] = grad_prob
            base = entries[r]
            table = jnp.where(lane == base, peak, table)
            table = jnp.where(lane == base + 8, total, table)
            table = jnp.where(lane == base + 16, inner, table)
        quarter = STRETCH // 4
        packed = table[:quarter]
        for k in range(1, 4):
            packed = packed + pltpu.roll(table[k * quarter : (k + 1) * quarter], 32 * k, 1)
        stat_send[h] = packed
        stat_copy(h).start()

    def partner(x):
        return jnp.where(lane % 2 == 0, pltpu.roll(x, 127, 1), pltpu.roll(x, 1, 1))

    row8 = iota((8, 2 * WIDE), 0)

    def backward(h, stacked):
        stat_copy(h).wait_recv()
        packed = stat_send[h] + stat_recv[h]
        table = jnp.concatenate(
            [packed] + [pltpu.roll(packed, 128 - 32 * k, 1) for k in range(1, 4)], axis=0
        )
        table = jnp.where(lane < 32, table, 0.0)
        total = pltpu.roll(table, 120, 1)
        inner = pltpu.roll(table, 112, 1)
        other_peak = partner(table)
        top = jnp.maximum(table, other_peak)
        mine_f, other_f = jnp.exp(table - top), jnp.exp(other_peak - top)
        denominator = mine_f * total + other_f * partner(total)
        inner = (mine_f * inner + other_f * partner(inner)) / denominator
        norm = mine_f / denominator
        bias_sum = jnp.zeros((STRETCH, WIDE), jnp.float32)
        parts = []
        for r in range(slots):
            at = lane == entries[r]
            factor = jnp.sum(jnp.where(at, norm, 0.0), axis=1, keepdims=True)
            shift = jnp.sum(jnp.where(at, inner, 0.0), axis=1, keepdims=True)
            prob = weights[h, r] * factor
            grad = prob * (cotangents[h, r] - shift)
            bias_sum = bias_sum + grad
            mix = jnp.concatenate([pltpu.roll(grad, WIDE - 1, 1), prob], axis=0).astype(jnp.bfloat16)
            mixed[h, r] = mix
            out = dot(mix, kv_ref[r, h])
            parts.append(
                jnp.concatenate([out[STRETCH:], out[:STRETCH] * scale], axis=1).astype(jnp.bfloat16)
            )
        rows = dot(scatter_ref[...], jnp.concatenate(parts, axis=0))
        rows_own[h] = rows[:tok]
        rows_send[h] = rows[tok:].astype(jnp.bfloat16)
        row_late(h).start()

        @pl.when(seq == 0)
        def _():
            row_early(h).start()

        folded = jnp.concatenate([bias_sum, jnp.zeros_like(bias_sum)], axis=1)
        half = STRETCH // 2
        while half >= 8:
            folded = pltpu.roll(folded[:half], 2 * half, 1) + folded[half:]
            half //= 2
        for bit in (4, 2, 1):
            folded = jnp.where((row8 // bit) % 2 == 0, pltpu.roll(folded, 2 * bit, 1), folded)
        return jnp.where(row8 == h, jnp.sum(folded, axis=0, keepdims=True), stacked)

    def both(h, stacked):
        forward(h + 1)
        return backward(h, stacked)

    forward(0)
    stacked = lax.fori_loop(0, heads - 1, both, jnp.zeros((8, 2 * WIDE), jnp.float32))
    stacked = backward(heads - 1, stacked)
    unmix = jnp.where(
        iota((2 * WIDE, WIDE), 0) == 2 * rel - 1 - 2 * iota((2 * WIDE, WIDE), 1), 1.0, 0.0
    ).astype(jnp.float32)
    raw_all[here] = jnp.dot(
        stacked, unmix, preferred_element_type=jnp.float32, precision=lax.Precision.HIGHEST
    )
    for k in range(1, plane):
        raw_copy(k).start()

    row_scale = jnp.where(iota((WIDE, depth), 0) % 2 == 0, scale, 1.0)

    def finish_kv(h):
        for r in range(slots):
            dkv = dot(mixed[h, r], windows[h, r], ((0,), (0,))) * row_scale
            dkv_pairs[h, r] = dkv.astype(jnp.bfloat16).reshape(NB_LEN, 2, depth)
            dkv_copy(h, r).start()

    each(heads // 2, finish_kv)
    for k in range(1, plane):
        raw_copy(k).wait_recv()
    raw = raw_all[0]
    for k in range(1, plane):
        raw = raw + raw_all[k]
    norm_all[mp] = jnp.broadcast_to(jnp.sum(raw * raw, keepdims=True), (8, 128))
    for k in range(1, mps):
        norm_copy(k).start()

    each(heads - heads // 2, lambda h: finish_kv(h + heads // 2))

    def finish_rows(h):
        row_late(h).wait_recv()

        @pl.when(seq == 1)
        def _():
            row_early(h).wait_recv()

        rows = rows_own[h] + rows_recv[h].astype(jnp.float32)
        att_ref[:, cols(h)] = rows[:, :depth].astype(jnp.bfloat16)
        dq_ref[:, cols(h)] = rows[:, depth:].astype(jnp.bfloat16)

    each(heads, finish_rows)
    for copy in out_copies():
        copy.start()
    for k in range(1, mps):
        norm_copy(k).wait_recv()
    squares = norm_all[0]
    for k in range(1, mps):
        squares = squares + norm_all[k]
    clip = jnp.minimum(1.0, 1.0 / jnp.sqrt(squares[:, :1] + 1e-12))
    dbias_ref[...] = (raw * clip)[:heads, :rel]

    def drain(h):
        for copy in in_late(h):
            copy.wait_send()
        row_late(h).wait_send()
        stat_copy(h).wait_send()

        @pl.when(seq == 1)
        def _():
            for copy in in_early(h):
                copy.wait_send()

        @pl.when(seq == 0)
        def _():
            row_early(h).wait_send()

        for r in range(slots):
            dkv_copy(h, r).wait()

    each(heads, drain)
    for k in range(1, plane):
        raw_copy(k).wait_send()
    for k in range(1, mps):
        norm_copy(k).wait_send()
    for copy in out_copies():
        copy.wait()


def write_kernel(
    att, dq, dkv, dbias, att_out, dq_out, dkv_out, dbias_out,
    att_held, dq_held, dkv_held, dbias_held, load_sems, store_sems,
):
    slots = dkv.shape[1]
    routes = [(dkv.at[0, r], dkv_held.at[r], dkv_out.at[0, r]) for r in range(slots)]
    routes += [(att, att_held, att_out), (dq, dq_held, dq_out), (dbias, dbias_held, dbias_out)]
    loads = [pltpu.make_async_copy(a, b, load_sems.at[k]) for k, (a, b, _) in enumerate(routes)]
    stores = [pltpu.make_async_copy(b, c, store_sems.at[k]) for k, (_, b, c) in enumerate(routes)]
    for copy in loads:
        copy.start()
    for load, store in zip(loads, stores):
        load.wait()
        store.start()
    for copy in stores:
        copy.wait()


def pair_exchange(queries, d_out, neighbour_kv, target, bias):
    _, tok, width = queries.shape
    heads = bias.shape[0]
    depth = width // heads
    slots = neighbour_kv.shape[1]
    plane, mps = 2 * lax.axis_size("grp"), lax.axis_size("mp")
    vmem = pl.BlockSpec(memory_space=pltpu.VMEM)
    hbm = pl.BlockSpec(memory_space=pltpu.HBM)
    f32, bf16, dma = jnp.float32, jnp.bfloat16, pltpu.SemaphoreType.DMA
    results = tuple(jax.ShapeDtypeStruct(x.shape, x.dtype) for x in (queries, d_out, neighbour_kv, bias))
    parts = pl.pallas_call(
        pair_kernel,
        out_shape=results,
        in_specs=[hbm, hbm, hbm, hbm, vmem],
        out_specs=(hbm, hbm, hbm, vmem),
        scratch_shapes=[
            pltpu.SMEM(target.shape, jnp.int32),
            pltpu.VMEM((tok, width), bf16),
            pltpu.VMEM((tok, width), bf16),
            pltpu.VMEM((heads, slots, NB_LEN, 2, depth), bf16),
            pltpu.VMEM((slots, heads, WIDE, depth), bf16),
            pltpu.VMEM((heads, tok, depth), bf16),
            pltpu.VMEM((heads, tok, depth), bf16),
            pltpu.VMEM((heads, slots, 2 * STRETCH, depth), bf16),
            pltpu.VMEM((heads, slots, STRETCH, WIDE), f32),
            pltpu.VMEM((heads, slots, STRETCH, WIDE), f32),
            pltpu.VMEM((heads, slots, 2 * STRETCH, WIDE), bf16),
            pltpu.VMEM((heads, tok, 2 * depth), f32),
            pltpu.VMEM((heads, tok, 2 * depth), bf16),
            pltpu.VMEM((heads, tok, 2 * depth), bf16),
            pltpu.VMEM((slots * STRETCH, 2 * tok), bf16),
            pltpu.VMEM((2 * tok, slots * STRETCH), bf16),
            pltpu.VMEM((heads, 8, 2 * WIDE), f32),
            pltpu.VMEM((heads, slots, NB_LEN, 2, depth), bf16),
            pltpu.VMEM((tok, width), bf16),
            pltpu.VMEM((tok, width), bf16),
            pltpu.VMEM((heads, STRETCH // 4, 128), f32),
            pltpu.VMEM((heads, STRETCH // 4, 128), f32),
            pltpu.VMEM((plane, 8, WIDE), f32),
            pltpu.VMEM((mps, 8, 128), f32),
            dma((3,)),
            dma((heads, slots)),
            dma((4, heads)),
            dma((4, heads)),
            dma((heads,)),
            dma((heads,)),
            dma((2, heads)),
            dma((2, heads)),
            dma((plane,)),
            dma((plane,)),
            dma((mps,)),
            dma((mps,)),
            dma((2,)),
            dma((heads, slots)),
        ],
        compiler_params=pltpu.CompilerParams(
            collective_id=0, has_side_effects=True, vmem_limit_bytes=VMEM_USE
        ),
    )(queries, d_out, neighbour_kv, target, bias)
    return pl.pallas_call(
        write_kernel,
        out_shape=results,
        in_specs=[hbm] * 4,
        out_specs=(hbm,) * 4,
        scratch_shapes=[
            pltpu.VMEM(queries.shape, bf16),
            pltpu.VMEM(d_out.shape, bf16),
            pltpu.VMEM(neighbour_kv.shape[1:], bf16),
            pltpu.VMEM(bias.shape, f32),
            dma((slots + 3,)),
            dma((slots + 3,)),
        ],
        compiler_params=pltpu.CompilerParams(vmem_limit_bytes=VMEM_USE),
    )(*parts)


def local(queries, d_out, neighbour_kv, target, bias):
    tok = queries.shape[1]
    fits = (
        lax.axis_size("seq") == 2
        and neighbour_kv.shape[1] == 2 * (tok // STRETCH)
        and tok == 128
        and bias.shape == (4, 191)
        and queries.shape[2] == 512
    )
    run = pair_exchange if fits else shard_exchange
    return run(queries, d_out, neighbour_kv, target, bias)


def solution(mesh):
    in_specs = (
        P("grp", "seq", "mp"),
        P("grp", "seq", "mp"),
        P("grp", "seq", None, None, "mp"),
        P("grp", "seq"),
        P("mp", None),
    )
    out_specs = (
        P("grp", "seq", "mp"),
        P("grp", "seq", "mp"),
        P("grp", "seq", None, None, "mp"),
        P("mp", None),
    )
    return jax.shard_map(local, mesh=mesh, in_specs=in_specs, out_specs=out_specs, check_vma=False)
```

```python
import jax
import jax.numpy as jnp
from jax import lax
from jax.experimental import pallas as pl
from jax.experimental.pallas import tpu as pltpu
from jax.sharding import PartitionSpec as P

STRETCH = 64
NB_LEN = 128


def passed_along(block, axis, distance):
    devices = range(lax.axis_size(axis))
    route = [(i - distance, i) for i in devices if i - distance in devices]
    return lax.ppermute(block, axis, route)


def bias_grid(lookup, row_count, col_count):
    head_num = lookup.shape[0]
    span = row_count + col_count
    padded = jnp.pad(lookup, ((0, 0), (0, 1)))
    flattened = jnp.tile(padded, (1, row_count))
    flattened = jnp.pad(flattened, ((0, 0), (0, row_count)))
    shaped = flattened.reshape(head_num, row_count, span + 1)[:, :, :col_count]
    return shaped[:, :, ::-1]


def bias_fold(grads):
    head_num, row_count, col_count = grads.shape
    turned = grads[:, :, ::-1]
    padded = jnp.pad(turned, ((0, 0), (0, 0), (0, row_count)))
    flattened = padded.reshape(head_num, row_count * (row_count + col_count))
    flattened = flattened[:, : row_count * (row_count + col_count - 1)]
    return jnp.sum(flattened.reshape(head_num, row_count, row_count + col_count - 1), axis=1)


def select_rows(picker, lookup):
    chosen = jnp.dot(
        picker.astype(lookup.dtype),
        lookup,
        preferred_element_type=jnp.float32,
        precision=lax.Precision.HIGHEST,
    )
    return chosen.astype(lookup.dtype)


def slot_places(target_row, owners, capacity, per_owner):
    is_used = target_row >= 0
    owner_of = jnp.where(is_used, target_row // per_owner, -1)
    positions = jnp.arange(target_row.shape[0])
    earlier = (
        (positions[None, :] < positions[:, None])
        & (owner_of[None, :] == owner_of[:, None])
        & is_used[None, :]
    )
    rank_of = jnp.sum(earlier.astype(jnp.int32), axis=1)
    match_owner = owner_of[None, :] == jnp.arange(owners)[:, None]
    match_rank = rank_of[None, :] == jnp.arange(capacity)[:, None]
    return match_owner[:, None, :] & match_rank[None, :, :] & is_used[None, None, :]


def shard_exchange(queries, d_out, neighbour_kv, target, bias):
    tok_rows = queries.shape[1]
    width_dev = queries.shape[2]
    head_count = bias.shape[0]
    head_depth = width_dev // head_count
    stretch_count = tok_rows // STRETCH
    per_owner = 2 * stretch_count
    shard_count = lax.axis_size("seq")
    my_index = lax.axis_index("seq")
    group_size = min(shard_count, per_owner)
    capacity = (per_owner + group_size - 1) // group_size
    seq_stretches = min(2048, tok_rows * shard_count) // STRETCH
    scale_factor = head_depth ** (-0.5)
    bias_rows = bias_grid(bias, STRETCH, NB_LEN).transpose(1, 0, 2)
    q_rows = queries[0]
    g_rows = d_out[0]
    next_pair = passed_along(jnp.stack([q_rows[:STRETCH], g_rows[:STRETCH]]), "seq", -1)
    row_ids = jnp.arange(STRETCH)
    stretch_ids = my_index * stretch_count + jnp.arange(stretch_count)
    is_live = (row_ids[None, :] == 0) | ((stretch_ids[:, None] + 1) % seq_stretches != 0)
    live_rows = is_live.astype(jnp.float32)
    q_win = jnp.concatenate([q_rows, next_pair[0]])[STRETCH - 1 : STRETCH - 1 + tok_rows]
    q_win = q_win.reshape(stretch_count, STRETCH * width_dev)
    g_win = jnp.concatenate([g_rows, next_pair[1]])[STRETCH - 1 : STRETCH - 1 + tok_rows]
    g_win = g_win.reshape(stretch_count, STRETCH, width_dev) * is_live[:, :, None].astype(
        jnp.bfloat16
    )
    g_win = g_win.reshape(stretch_count, STRETCH * width_dev)
    my_targets = target[0]
    slot_count = my_targets.shape[0]
    send_map = slot_places(my_targets, shard_count, capacity, per_owner)
    id_buffer = jnp.sum(jnp.where(send_map, my_targets[None, None, :] + 1, 0), axis=2) - 1
    recv_ids = lax.all_to_all(id_buffer, "seq", split_axis=0, concat_axis=0, tiled=True)
    flat_ids = recv_ids.reshape(shard_count * capacity)
    has_entry = flat_ids >= 0
    local_entry = flat_ids - my_index * per_owner
    entry_pick = (local_entry[:, None] == jnp.arange(per_owner)[None, :]) & has_entry[:, None]
    stretch_pick = (local_entry[:, None] // 2 == jnp.arange(stretch_count)[None, :]) & has_entry[
        :, None
    ]
    back_pick = send_map.reshape(shard_count * capacity, slot_count)
    slot_pick = back_pick.T
    q_send = select_rows(stretch_pick, q_win).reshape(shard_count, capacity, STRETCH * width_dev)
    g_send = select_rows(stretch_pick, g_win).reshape(shard_count, capacity, STRETCH * width_dev)
    q_recv, g_recv = (
        lax.all_to_all(q_send, "seq", split_axis=0, concat_axis=0, tiled=True),
        lax.all_to_all(g_send, "seq", split_axis=0, concat_axis=0, tiled=True),
    )
    q_slots = select_rows(slot_pick, q_recv.reshape(shard_count * capacity, -1))
    q_slots = q_slots.reshape(slot_count, STRETCH, head_count, head_depth)
    stored = neighbour_kv[0]
    key_rows = stored[:, :, 0].reshape(slot_count, NB_LEN, head_count, head_depth)
    value_rows = stored[:, :, 1].reshape(slot_count, NB_LEN, head_count, head_depth)
    scores = jnp.einsum("sihd,sjhd->sihj", q_slots, key_rows, preferred_element_type=jnp.float32)
    scores = scores * scale_factor + bias_rows[None]
    peak_val = jnp.max(scores, axis=-1)
    weights = jnp.exp(scores - peak_val[..., None])
    row_total = jnp.sum(weights, axis=-1)
    partial_value = jnp.einsum(
        "sihj,sjhd->sihd",
        weights.astype(jnp.bfloat16),
        value_rows,
        preferred_element_type=jnp.float32,
    )
    part_send = select_rows(back_pick, partial_value.reshape(slot_count, -1)).reshape(
        shard_count, capacity, -1
    )
    peak_send = select_rows(back_pick, peak_val.reshape(slot_count, -1)).reshape(
        shard_count, capacity, -1
    )
    total_send = select_rows(back_pick, row_total.reshape(slot_count, -1)).reshape(
        shard_count, capacity, -1
    )
    part_recv, peak_recv, total_recv = (
        lax.all_to_all(part_send, "seq", split_axis=0, concat_axis=0, tiled=True),
        lax.all_to_all(peak_send, "seq", split_axis=0, concat_axis=0, tiled=True),
        lax.all_to_all(total_send, "seq", split_axis=0, concat_axis=0, tiled=True),
    )
    entry_back = entry_pick.T
    parts_own = select_rows(entry_back, part_recv.reshape(shard_count * capacity, -1))
    parts_own = parts_own.reshape(stretch_count, 2, STRETCH, head_count, head_depth)
    peaks_own = select_rows(entry_back, peak_recv.reshape(shard_count * capacity, -1))
    peaks_own = peaks_own.reshape(stretch_count, 2, STRETCH, head_count)
    totals_own = select_rows(entry_back, total_recv.reshape(shard_count * capacity, -1))
    totals_own = totals_own.reshape(stretch_count, 2, STRETCH, head_count)
    top_peak = jnp.max(peaks_own, axis=1)
    factor = jnp.exp(peaks_own - top_peak[:, None])
    denominator = jnp.sum(factor * totals_own, axis=1)
    combined = jnp.sum(factor[..., None] * parts_own, axis=1) / denominator[..., None]
    combined = combined * live_rows[:, :, None, None]
    att_win = combined.astype(jnp.bfloat16).reshape(tok_rows, width_dev)
    log_total = top_peak + jnp.log(denominator)
    g_wide = g_win.reshape(stretch_count, STRETCH, head_count, head_depth).astype(jnp.float32)
    inner_dot = jnp.sum(g_wide * combined, axis=-1)
    row_stats = jnp.repeat(jnp.stack([log_total, inner_dot], axis=1), 2, axis=0)
    stats_send = select_rows(entry_pick, row_stats.reshape(per_owner, -1)).reshape(
        shard_count, capacity, -1
    )
    stats_recv = lax.all_to_all(stats_send, "seq", split_axis=0, concat_axis=0, tiled=True)
    g_slots = select_rows(slot_pick, g_recv.reshape(shard_count * capacity, -1))
    g_slots = g_slots.reshape(slot_count, STRETCH, head_count, head_depth)
    stats_slots = select_rows(slot_pick, stats_recv.reshape(shard_count * capacity, -1))
    stats_slots = stats_slots.reshape(slot_count, 2, STRETCH, head_count)
    prob_full = jnp.exp(scores - stats_slots[:, 0][..., None])
    prob_low = prob_full.astype(jnp.bfloat16)
    grad_values = jnp.einsum(
        "sihj,sihd->sjhd", prob_low, g_slots, preferred_element_type=jnp.float32
    )
    grad_prob = jnp.einsum(
        "sihd,sjhd->sihj", g_slots, value_rows, preferred_element_type=jnp.float32
    )
    grad_scores = prob_full * (grad_prob - stats_slots[:, 1][..., None])
    scores_low = grad_scores.astype(jnp.bfloat16)
    grad_rows = (
        jnp.einsum("sihj,sjhd->sihd", scores_low, key_rows, preferred_element_type=jnp.float32)
        * scale_factor
    )
    grad_keys = (
        jnp.einsum("sihj,sihd->sjhd", scores_low, q_slots, preferred_element_type=jnp.float32)
        * scale_factor
    )
    d_kv = jnp.stack(
        [
            grad_keys.reshape(slot_count, NB_LEN, width_dev),
            grad_values.reshape(slot_count, NB_LEN, width_dev),
        ],
        axis=2,
    ).astype(jnp.bfloat16)
    bias_part = bias_fold(jnp.sum(grad_scores, axis=0).transpose(1, 0, 2))
    rows_send = select_rows(back_pick, grad_rows.reshape(slot_count, -1)).reshape(
        shard_count, capacity, -1
    )
    rows_recv = lax.all_to_all(rows_send, "seq", split_axis=0, concat_axis=0, tiled=True)
    grad_entries = select_rows(entry_back, rows_recv.reshape(shard_count * capacity, -1))
    grad_entries = grad_entries.reshape(stretch_count, 2, STRETCH * width_dev)
    grad_win = (
        (grad_entries[:, 0] + grad_entries[:, 1]).astype(jnp.bfloat16).reshape(tok_rows, width_dev)
    )
    both_before = passed_along(
        jnp.stack([att_win[tok_rows - STRETCH :], grad_win[tok_rows - STRETCH :]]), "seq", 1
    )
    att_before = both_before[0]
    grad_before = both_before[1]
    attended = jnp.concatenate([att_before[1:], att_win[: tok_rows - STRETCH + 1]])
    d_query = jnp.concatenate([grad_before[1:], grad_win[: tok_rows - STRETCH + 1]])
    raw_sum = lax.psum(bias_part, ("grp", "seq"))
    squares = lax.psum(jnp.sum(raw_sum * raw_sum), "mp")
    d_bias = raw_sum * jnp.minimum(1.0, 1.0 / jnp.sqrt(squares + 1e-12))
    return (attended[None], d_query[None], d_kv[None], d_bias)


WIDE = 2 * NB_LEN
VMEM_USE = 60 * 1024 * 1024
MESH = pl.DeviceIdType.MESH


def dot(a, b, contract=((1,), (0,))):
    return lax.dot_general(a, b, (contract, ((), ())), preferred_element_type=jnp.float32)


def iota(shape, axis):
    return lax.broadcasted_iota(jnp.int32, shape, axis)


def one_hot(flags):
    return jnp.where(flags, 1.0, 0.0).astype(jnp.bfloat16)


def halves(x):
    high = x.astype(jnp.bfloat16)
    return high, (x - high.astype(jnp.float32)).astype(jnp.bfloat16)


def dot_chosen(x, picker):
    high, rest = halves(x)
    left = x - high.astype(jnp.float32)
    low = (left - rest.astype(jnp.float32)).astype(jnp.bfloat16)
    wide = jnp.concatenate([p.astype(jnp.float32) for p in (high, rest, low)], axis=0)
    out = dot(wide.astype(jnp.bfloat16), picker)
    return out[:8] + out[8:16] + out[16:]


def pair_kernel(
    q_hbm, g_hbm, kv_hbm, target_hbm, bias_ref,
    att_hbm, dq_hbm, dkv_hbm, dbias_ref,
    target_ref, q_ref, g_ref, kv_pairs, kv_ref, q_peer, g_peer,
    windows, weights, cotangents, mixed, rows_own, rows_send, rows_recv,
    gather_ref, scatter_ref, turned_ref, pick_ref, unmix_ref, bias_rows, dkv_pairs, att_ref, dq_ref,
    stat_send, stat_recv, raw_all, norm_all,
    own_sems, kv_sems, in_send, in_recv, stat_send_sems, stat_recv_sems, row_send_sems, row_recv_sems,
    raw_send_sems, raw_recv_sems, norm_send_sems, norm_recv_sems, out_sems, dkv_sems,
):
    heads, rel = bias_ref.shape
    slots = kv_ref.shape[0]
    tok = q_ref.shape[0]
    depth = kv_ref.shape[-1]
    lead = (STRETCH - 1) // 16 * 16
    late = pl.ds(lead, tok - lead)
    early = pl.ds(0, lead)
    groups, mps = lax.axis_size("grp"), lax.axis_size("mp")
    plane = 2 * groups
    scale = depth ** (-0.5)
    grp, seq, mp = lax.axis_index("grp"), lax.axis_index("seq"), lax.axis_index("mp")
    here = grp * 2 + seq
    peer = {"seq": 1 - seq}

    def plane_at(step):
        there = lax.rem(here + step, plane)
        return {"grp": there // 2, "seq": there % 2}

    def mp_at(step):
        return {"mp": lax.rem(mp + step, mps)}

    def remote(src, dst, send_sem, recv_sem, device):
        return pltpu.make_async_remote_copy(
            src_ref=src, dst_ref=dst, send_sem=send_sem, recv_sem=recv_sem,
            device_id=device, device_id_type=MESH,
        )

    def cols(h):
        return pl.ds(pl.multiple_of(h * depth, depth), depth)

    def q_copy(h, rows, lane):
        return remote(
            q_hbm.at[0, rows, cols(h)], q_peer.at[h, rows], in_send.at[lane, h], in_recv.at[lane, h], peer
        )

    def g_copy(h, rows, lane):
        return remote(
            g_hbm.at[0, rows, cols(h)], g_peer.at[h, rows], in_send.at[lane, h], in_recv.at[lane, h], peer
        )

    def in_late(h):
        return q_copy(h, late, 0), g_copy(h, late, 1)

    def in_early(h):
        return q_copy(h, early, 2), g_copy(h, early, 3)

    def kv_copy(h, r):
        return pltpu.make_async_copy(kv_hbm.at[0, r, :, :, cols(h)], kv_pairs.at[h, r], kv_sems.at[h, r])

    def stat_copy(part):
        return remote(
            stat_send.at[part], stat_recv.at[part], stat_send_sems.at[part], stat_recv_sems.at[part], peer
        )

    def row_copy(h, rows, lane):
        return remote(
            rows_send.at[h, rows], rows_recv.at[h, rows],
            row_send_sems.at[lane, h], row_recv_sems.at[lane, h], peer,
        )

    def row_late(h):
        return row_copy(h, late, 0)

    def row_early(h):
        return row_copy(h, early, 1)

    def raw_copy(k):
        return remote(raw_all.at[here], raw_all.at[here], raw_send_sems.at[k], raw_recv_sems.at[k], plane_at(k))

    def norm_copy(k):
        return remote(norm_all.at[mp], norm_all.at[mp], norm_send_sems.at[k], norm_recv_sems.at[k], mp_at(k))

    def dkv_copy(h, r):
        return pltpu.make_async_copy(dkv_pairs.at[h, r], dkv_hbm.at[0, r, :, :, cols(h)], dkv_sems.at[h, r])

    def out_copies():
        return (
            pltpu.make_async_copy(att_ref, att_hbm.at[0], out_sems.at[0]),
            pltpu.make_async_copy(dq_ref, dq_hbm.at[0], out_sems.at[1]),
        )

    def each(count, body):
        def step(i, carry):
            body(i)
            return carry

        lax.fori_loop(0, count, step, 0)

    barrier = pltpu.get_barrier_semaphore()
    for step in range(1, plane):
        pl.semaphore_signal(barrier, inc=1, device_id=plane_at(step), device_id_type=MESH)
    for step in range(1, mps):
        pl.semaphore_signal(barrier, inc=1, device_id=mp_at(step), device_id_type=MESH)
    own_copies = [
        pltpu.make_async_copy(target_hbm, target_ref, own_sems.at[0]),
        pltpu.make_async_copy(q_hbm.at[0], q_ref, own_sems.at[1]),
        pltpu.make_async_copy(g_hbm.at[0], g_ref, own_sems.at[2]),
    ]
    for copy in own_copies:
        copy.start()

    def start_kv(h):
        for r in range(slots):
            kv_copy(h, r).start()

    each(heads, start_kv)
    place = iota((2 * WIDE, WIDE), 0) + 2 * iota((2 * WIDE, WIDE), 1)
    unmix_ref[...] = one_hot(place == 2 * rel - 1)
    place = iota((WIDE, 2 * WIDE), 1) + 2 * iota((WIDE, 2 * WIDE), 0)
    bias_rows[...] = jnp.zeros((8, WIDE), jnp.float32)
    bias_rows[:heads, :rel] = bias_ref[...]
    turned = dot_chosen(bias_rows[...], one_hot(place == 2 * (rel - 1)))
    for h in range(heads):
        turned_ref[h] = jnp.broadcast_to(turned[h : h + 1], (8, 2 * WIDE))
    pl.semaphore_wait(barrier, plane - 1 + mps - 1)

    def start_rows(h):
        for copy in in_late(h):
            copy.start()

        @pl.when(seq == 1)
        def _():
            for copy in in_early(h):
                copy.start()

    each(heads, start_rows)

    @pl.when(seq == 1)
    def _():
        q_peer[:, early] = jnp.zeros((heads, lead, depth), jnp.bfloat16)
        g_peer[:, early] = jnp.zeros((heads, lead, depth), jnp.bfloat16)

    @pl.when(seq == 0)
    def _():
        rows_recv[:, early] = jnp.zeros((heads, lead, 2 * depth), jnp.bfloat16)

    for copy in own_copies:
        copy.wait()
    entries = [target_ref[0, r] for r in range(slots)]

    def token_of(axis, shape):
        place = iota(shape, axis)
        return jnp.where(place < tok, tok * seq + place, tok * (1 - seq) + place - tok)

    for r in range(slots):
        rows = pl.ds(r * STRETCH, STRETCH)
        first = (STRETCH - 1) + STRETCH * (entries[r] // 2)
        flat = (STRETCH, 2 * tok)
        gather_ref[rows, :] = one_hot(token_of(1, flat) == iota(flat, 0) + first)
        column = iota((2 * 128, 128), 0) % 128
        pick_ref[:, pl.ds(r * 128, 128)] = one_hot(column == entries[r])
    scatter_ref[...] = gather_ref[...].T
    ones = jnp.ones((WIDE, 128), jnp.bfloat16)
    odd = iota((STRETCH, WIDE), 1) % 2 == 1
    lane = iota((STRETCH, 128), 1)

    def unpair(h):
        for r in range(slots):
            kv_copy(h, r).wait()
            kv_ref[r, h] = kv_pairs[h, r].reshape(WIDE, depth)

    each(heads, unpair)

    def forward(h):
        table = jnp.zeros((STRETCH, 128), jnp.float32)
        wide = jnp.broadcast_to(turned_ref[h][:1], (STRETCH, 2 * WIDE))
        grid = pltpu.roll(wide, 2 * WIDE - 126, 1, stride=2, stride_axis=0)[:, :WIDE]
        grid = jnp.where(odd, -1e30, grid)
        mine = jnp.concatenate([q_ref[:, cols(h)], g_ref[:, cols(h)]], axis=1)
        for copy in in_late(h):
            copy.wait_recv()

        @pl.when(seq == 0)
        def _():
            for copy in in_early(h):
                copy.wait_recv()

        other = jnp.concatenate([q_peer[h], g_peer[h]], axis=1)
        picked = dot(gather_ref[...], jnp.concatenate([mine, other], axis=0)).astype(jnp.bfloat16)
        for r in range(slots):
            rows = picked[r * STRETCH : (r + 1) * STRETCH]
            both = jnp.concatenate([rows[:, :depth], rows[:, depth:]], axis=0)
            windows[h, r] = both
            prod = dot(both, kv_ref[r, h], ((1,), (1,)))
            scores = prod[:STRETCH] * scale + grid
            grad_prob = prod[STRETCH:]
            peak = jnp.max(scores, axis=1, keepdims=True)
            expd = jnp.exp(scores - peak)
            rolled = pltpu.roll(expd, 1, 1)
            high, low = halves(jnp.concatenate([expd, rolled * grad_prob], axis=0))
            sums = dot(high, ones) + dot(low, ones)
            total, inner = sums[:STRETCH], sums[STRETCH:]
            weights[h, r] = rolled
            cotangents[h, r] = grad_prob
            base = entries[r]
            table = jnp.where(lane == base, peak, table)
            table = jnp.where(lane == base + 8, total, table)
            table = jnp.where(lane == base + 16, inner, table)
        quarter = STRETCH // 4
        packed = table[:quarter]
        for k in range(1, 4):
            packed = packed + pltpu.roll(table[k * quarter : (k + 1) * quarter], 32 * k, 1)
        stat_send[h] = packed
        stat_copy(h).start()

    def partner(x):
        return jnp.where(lane % 2 == 0, pltpu.roll(x, 127, 1), pltpu.roll(x, 1, 1))

    row8 = iota((8, 2 * WIDE), 0)

    def backward(h, stacked):
        stat_copy(h).wait_recv()
        packed = stat_send[h] + stat_recv[h]
        table = jnp.concatenate(
            [packed] + [pltpu.roll(packed, 128 - 32 * k, 1) for k in range(1, 4)], axis=0
        )
        table = jnp.where(lane < 32, table, 0.0)
        total = pltpu.roll(table, 120, 1)
        inner = pltpu.roll(table, 112, 1)
        other_peak = partner(table)
        top = jnp.maximum(table, other_peak)
        mine_f, other_f = jnp.exp(table - top), jnp.exp(other_peak - top)
        denominator = mine_f * total + other_f * partner(total)
        inner = (mine_f * inner + other_f * partner(inner)) / denominator
        stats = jnp.concatenate([mine_f / denominator, inner], axis=0)
        stats = jnp.where(iota((2 * STRETCH, 128), 1) < 8, stats, 0.0)
        spread = dot(jnp.concatenate(halves(stats), axis=1), pick_ref[...])
        bias_sum = jnp.zeros((STRETCH, WIDE), jnp.float32)
        parts = []
        for r in range(slots):
            slot = spread[:, r * 128 : (r + 1) * 128]
            slot = jnp.concatenate([slot, slot], axis=1)
            factor, shift = slot[:STRETCH], slot[STRETCH:]
            prob = weights[h, r] * factor
            grad = prob * (cotangents[h, r] - shift)
            bias_sum = bias_sum + grad
            mix = jnp.concatenate([pltpu.roll(grad, WIDE - 1, 1), prob], axis=0).astype(jnp.bfloat16)
            mixed[h, r] = mix
            out = dot(mix, kv_ref[r, h])
            parts.append(
                jnp.concatenate([out[STRETCH:], out[:STRETCH] * scale], axis=1).astype(jnp.bfloat16)
            )
        rows = dot(scatter_ref[...], jnp.concatenate(parts, axis=0))
        rows_own[h] = rows[:tok]
        rows_send[h] = rows[tok:].astype(jnp.bfloat16)
        row_late(h).start()

        @pl.when(seq == 0)
        def _():
            row_early(h).start()

        folded = jnp.concatenate([bias_sum, jnp.zeros_like(bias_sum)], axis=1)
        half = STRETCH // 2
        while half >= 8:
            folded = pltpu.roll(folded[:half], 2 * half, 1) + folded[half:]
            half //= 2
        for bit in (4, 2, 1):
            folded = jnp.where((row8 // bit) % 2 == 0, pltpu.roll(folded, 2 * bit, 1), folded)
        return jnp.where(row8 == h, jnp.sum(folded, axis=0, keepdims=True), stacked)

    def both(h, stacked):
        forward(h + 1)
        return backward(h, stacked)

    forward(0)
    stacked = lax.fori_loop(0, heads - 1, both, jnp.zeros((8, 2 * WIDE), jnp.float32))
    stacked = backward(heads - 1, stacked)
    raw_all[here] = dot_chosen(stacked, unmix_ref[...])
    for k in range(1, plane):
        raw_copy(k).start()

    row_scale = jnp.where(iota((WIDE, depth), 0) % 2 == 0, scale, 1.0)

    def finish_kv(h):
        for r in range(slots):
            dkv = dot(mixed[h, r], windows[h, r], ((0,), (0,))) * row_scale
            dkv_pairs[h, r] = dkv.astype(jnp.bfloat16).reshape(NB_LEN, 2, depth)
            dkv_copy(h, r).start()

    each(heads // 2, finish_kv)
    for k in range(1, plane):
        raw_copy(k).wait_recv()
    raw = raw_all[0]
    for k in range(1, plane):
        raw = raw + raw_all[k]
    norm_all[mp] = jnp.broadcast_to(jnp.sum(raw * raw, keepdims=True), (8, 128))
    for k in range(1, mps):
        norm_copy(k).start()

    each(heads - heads // 2, lambda h: finish_kv(h + heads // 2))

    def finish_rows(h):
        row_late(h).wait_recv()

        @pl.when(seq == 1)
        def _():
            row_early(h).wait_recv()

        rows = rows_own[h] + rows_recv[h].astype(jnp.float32)
        att_ref[:, cols(h)] = rows[:, :depth].astype(jnp.bfloat16)
        dq_ref[:, cols(h)] = rows[:, depth:].astype(jnp.bfloat16)

    each(heads, finish_rows)
    for copy in out_copies():
        copy.start()
    for k in range(1, mps):
        norm_copy(k).wait_recv()
    squares = norm_all[0]
    for k in range(1, mps):
        squares = squares + norm_all[k]
    clip = jnp.minimum(1.0, 1.0 / jnp.sqrt(squares[:, :1] + 1e-12))
    dbias_ref[...] = (raw * clip)[:heads, :rel]

    def drain(h):
        for copy in in_late(h):
            copy.wait_send()
        row_late(h).wait_send()
        stat_copy(h).wait_send()

        @pl.when(seq == 1)
        def _():
            for copy in in_early(h):
                copy.wait_send()

        @pl.when(seq == 0)
        def _():
            row_early(h).wait_send()

        for r in range(slots):
            dkv_copy(h, r).wait()

    each(heads, drain)
    for k in range(1, plane):
        raw_copy(k).wait_send()
    for k in range(1, mps):
        norm_copy(k).wait_send()
    for copy in out_copies():
        copy.wait()


def write_kernel(
    att, dq, dkv, dbias, att_out, dq_out, dkv_out, dbias_out,
    att_held, dq_held, dkv_held, dbias_held, load_sems, store_sems,
):
    slots = dkv.shape[1]
    routes = [(dkv.at[0, r], dkv_held.at[r], dkv_out.at[0, r]) for r in range(slots)]
    routes += [(att, att_held, att_out), (dq, dq_held, dq_out), (dbias, dbias_held, dbias_out)]
    loads = [pltpu.make_async_copy(a, b, load_sems.at[k]) for k, (a, b, _) in enumerate(routes)]
    stores = [pltpu.make_async_copy(b, c, store_sems.at[k]) for k, (_, b, c) in enumerate(routes)]
    for copy in loads:
        copy.start()
    for load, store in zip(loads, stores):
        load.wait()
        store.start()
    for copy in stores:
        copy.wait()


def pair_exchange(queries, d_out, neighbour_kv, target, bias):
    _, tok, width = queries.shape
    heads = bias.shape[0]
    depth = width // heads
    slots = neighbour_kv.shape[1]
    plane, mps = 2 * lax.axis_size("grp"), lax.axis_size("mp")
    vmem = pl.BlockSpec(memory_space=pltpu.VMEM)
    hbm = pl.BlockSpec(memory_space=pltpu.HBM)
    f32, bf16, dma = jnp.float32, jnp.bfloat16, pltpu.SemaphoreType.DMA
    results = tuple(jax.ShapeDtypeStruct(x.shape, x.dtype) for x in (queries, d_out, neighbour_kv, bias))
    parts = pl.pallas_call(
        pair_kernel,
        out_shape=results,
        in_specs=[hbm, hbm, hbm, hbm, vmem],
        out_specs=(hbm, hbm, hbm, vmem),
        scratch_shapes=[
            pltpu.SMEM(target.shape, jnp.int32),
            pltpu.VMEM((tok, width), bf16),
            pltpu.VMEM((tok, width), bf16),
            pltpu.VMEM((heads, slots, NB_LEN, 2, depth), bf16),
            pltpu.VMEM((slots, heads, WIDE, depth), bf16),
            pltpu.VMEM((heads, tok, depth), bf16),
            pltpu.VMEM((heads, tok, depth), bf16),
            pltpu.VMEM((heads, slots, 2 * STRETCH, depth), bf16),
            pltpu.VMEM((heads, slots, STRETCH, WIDE), f32),
            pltpu.VMEM((heads, slots, STRETCH, WIDE), f32),
            pltpu.VMEM((heads, slots, 2 * STRETCH, WIDE), bf16),
            pltpu.VMEM((heads, tok, 2 * depth), f32),
            pltpu.VMEM((heads, tok, 2 * depth), bf16),
            pltpu.VMEM((heads, tok, 2 * depth), bf16),
            pltpu.VMEM((slots * STRETCH, 2 * tok), bf16),
            pltpu.VMEM((2 * tok, slots * STRETCH), bf16),
            pltpu.VMEM((heads, 8, 2 * WIDE), f32),
            pltpu.VMEM((2 * 128, slots * 128), bf16),
            pltpu.VMEM((2 * WIDE, WIDE), bf16),
            pltpu.VMEM((8, WIDE), f32),
            pltpu.VMEM((heads, slots, NB_LEN, 2, depth), bf16),
            pltpu.VMEM((tok, width), bf16),
            pltpu.VMEM((tok, width), bf16),
            pltpu.VMEM((heads, STRETCH // 4, 128), f32),
            pltpu.VMEM((heads, STRETCH // 4, 128), f32),
            pltpu.VMEM((plane, 8, WIDE), f32),
            pltpu.VMEM((mps, 8, 128), f32),
            dma((3,)),
            dma((heads, slots)),
            dma((4, heads)),
            dma((4, heads)),
            dma((heads,)),
            dma((heads,)),
            dma((2, heads)),
            dma((2, heads)),
            dma((plane,)),
            dma((plane,)),
            dma((mps,)),
            dma((mps,)),
            dma((2,)),
            dma((heads, slots)),
        ],
        compiler_params=pltpu.CompilerParams(
            collective_id=0, has_side_effects=True, vmem_limit_bytes=VMEM_USE
        ),
    )(queries, d_out, neighbour_kv, target, bias)
    return pl.pallas_call(
        write_kernel,
        out_shape=results,
        in_specs=[hbm] * 4,
        out_specs=(hbm,) * 4,
        scratch_shapes=[
            pltpu.VMEM(queries.shape, bf16),
            pltpu.VMEM(d_out.shape, bf16),
            pltpu.VMEM(neighbour_kv.shape[1:], bf16),
            pltpu.VMEM(bias.shape, f32),
            dma((slots + 3,)),
            dma((slots + 3,)),
        ],
        compiler_params=pltpu.CompilerParams(vmem_limit_bytes=VMEM_USE),
    )(*parts)


def local(queries, d_out, neighbour_kv, target, bias):
    tok = queries.shape[1]
    fits = (
        lax.axis_size("seq") == 2
        and neighbour_kv.shape[1] == 2 * (tok // STRETCH)
        and tok == 128
        and bias.shape == (4, 191)
        and queries.shape[2] == 512
    )
    run = pair_exchange if fits else shard_exchange
    return run(queries, d_out, neighbour_kv, target, bias)


def solution(mesh):
    in_specs = (
        P("grp", "seq", "mp"),
        P("grp", "seq", "mp"),
        P("grp", "seq", None, None, "mp"),
        P("grp", "seq"),
        P("mp", None),
    )
    out_specs = (
        P("grp", "seq", "mp"),
        P("grp", "seq", "mp"),
        P("grp", "seq", None, None, "mp"),
        P("mp", None),
    )
    return jax.shard_map(local, mesh=mesh, in_specs=in_specs, out_specs=out_specs, check_vma=False)
```

```python
import jax
import jax.numpy as jnp
from jax import lax
from jax.experimental import pallas as pl
from jax.experimental.pallas import tpu as pltpu
from jax.sharding import PartitionSpec as P

STRETCH = 64
NB_LEN = 128


def passed_along(block, axis, distance):
    devices = range(lax.axis_size(axis))
    route = [(i - distance, i) for i in devices if i - distance in devices]
    return lax.ppermute(block, axis, route)


def bias_grid(lookup, row_count, col_count):
    head_num = lookup.shape[0]
    span = row_count + col_count
    padded = jnp.pad(lookup, ((0, 0), (0, 1)))
    flattened = jnp.tile(padded, (1, row_count))
    flattened = jnp.pad(flattened, ((0, 0), (0, row_count)))
    shaped = flattened.reshape(head_num, row_count, span + 1)[:, :, :col_count]
    return shaped[:, :, ::-1]


def bias_fold(grads):
    head_num, row_count, col_count = grads.shape
    turned = grads[:, :, ::-1]
    padded = jnp.pad(turned, ((0, 0), (0, 0), (0, row_count)))
    flattened = padded.reshape(head_num, row_count * (row_count + col_count))
    flattened = flattened[:, : row_count * (row_count + col_count - 1)]
    return jnp.sum(flattened.reshape(head_num, row_count, row_count + col_count - 1), axis=1)


def select_rows(picker, lookup):
    chosen = jnp.dot(
        picker.astype(lookup.dtype),
        lookup,
        preferred_element_type=jnp.float32,
        precision=lax.Precision.HIGHEST,
    )
    return chosen.astype(lookup.dtype)


def slot_places(target_row, owners, capacity, per_owner):
    is_used = target_row >= 0
    owner_of = jnp.where(is_used, target_row // per_owner, -1)
    positions = jnp.arange(target_row.shape[0])
    earlier = (
        (positions[None, :] < positions[:, None])
        & (owner_of[None, :] == owner_of[:, None])
        & is_used[None, :]
    )
    rank_of = jnp.sum(earlier.astype(jnp.int32), axis=1)
    match_owner = owner_of[None, :] == jnp.arange(owners)[:, None]
    match_rank = rank_of[None, :] == jnp.arange(capacity)[:, None]
    return match_owner[:, None, :] & match_rank[None, :, :] & is_used[None, None, :]


def shard_exchange(queries, d_out, neighbour_kv, target, bias):
    tok_rows = queries.shape[1]
    width_dev = queries.shape[2]
    head_count = bias.shape[0]
    head_depth = width_dev // head_count
    stretch_count = tok_rows // STRETCH
    per_owner = 2 * stretch_count
    shard_count = lax.axis_size("seq")
    my_index = lax.axis_index("seq")
    group_size = min(shard_count, per_owner)
    capacity = (per_owner + group_size - 1) // group_size
    seq_stretches = min(2048, tok_rows * shard_count) // STRETCH
    scale_factor = head_depth ** (-0.5)
    bias_rows = bias_grid(bias, STRETCH, NB_LEN).transpose(1, 0, 2)
    q_rows = queries[0]
    g_rows = d_out[0]
    next_pair = passed_along(jnp.stack([q_rows[:STRETCH], g_rows[:STRETCH]]), "seq", -1)
    row_ids = jnp.arange(STRETCH)
    stretch_ids = my_index * stretch_count + jnp.arange(stretch_count)
    is_live = (row_ids[None, :] == 0) | ((stretch_ids[:, None] + 1) % seq_stretches != 0)
    live_rows = is_live.astype(jnp.float32)
    q_win = jnp.concatenate([q_rows, next_pair[0]])[STRETCH - 1 : STRETCH - 1 + tok_rows]
    q_win = q_win.reshape(stretch_count, STRETCH * width_dev)
    g_win = jnp.concatenate([g_rows, next_pair[1]])[STRETCH - 1 : STRETCH - 1 + tok_rows]
    g_win = g_win.reshape(stretch_count, STRETCH, width_dev) * is_live[:, :, None].astype(
        jnp.bfloat16
    )
    g_win = g_win.reshape(stretch_count, STRETCH * width_dev)
    my_targets = target[0]
    slot_count = my_targets.shape[0]
    send_map = slot_places(my_targets, shard_count, capacity, per_owner)
    id_buffer = jnp.sum(jnp.where(send_map, my_targets[None, None, :] + 1, 0), axis=2) - 1
    recv_ids = lax.all_to_all(id_buffer, "seq", split_axis=0, concat_axis=0, tiled=True)
    flat_ids = recv_ids.reshape(shard_count * capacity)
    has_entry = flat_ids >= 0
    local_entry = flat_ids - my_index * per_owner
    entry_pick = (local_entry[:, None] == jnp.arange(per_owner)[None, :]) & has_entry[:, None]
    stretch_pick = (local_entry[:, None] // 2 == jnp.arange(stretch_count)[None, :]) & has_entry[
        :, None
    ]
    back_pick = send_map.reshape(shard_count * capacity, slot_count)
    slot_pick = back_pick.T
    q_send = select_rows(stretch_pick, q_win).reshape(shard_count, capacity, STRETCH * width_dev)
    g_send = select_rows(stretch_pick, g_win).reshape(shard_count, capacity, STRETCH * width_dev)
    q_recv, g_recv = (
        lax.all_to_all(q_send, "seq", split_axis=0, concat_axis=0, tiled=True),
        lax.all_to_all(g_send, "seq", split_axis=0, concat_axis=0, tiled=True),
    )
    q_slots = select_rows(slot_pick, q_recv.reshape(shard_count * capacity, -1))
    q_slots = q_slots.reshape(slot_count, STRETCH, head_count, head_depth)
    stored = neighbour_kv[0]
    key_rows = stored[:, :, 0].reshape(slot_count, NB_LEN, head_count, head_depth)
    value_rows = stored[:, :, 1].reshape(slot_count, NB_LEN, head_count, head_depth)
    scores = jnp.einsum("sihd,sjhd->sihj", q_slots, key_rows, preferred_element_type=jnp.float32)
    scores = scores * scale_factor + bias_rows[None]
    peak_val = jnp.max(scores, axis=-1)
    weights = jnp.exp(scores - peak_val[..., None])
    row_total = jnp.sum(weights, axis=-1)
    partial_value = jnp.einsum(
        "sihj,sjhd->sihd",
        weights.astype(jnp.bfloat16),
        value_rows,
        preferred_element_type=jnp.float32,
    )
    part_send = select_rows(back_pick, partial_value.reshape(slot_count, -1)).reshape(
        shard_count, capacity, -1
    )
    peak_send = select_rows(back_pick, peak_val.reshape(slot_count, -1)).reshape(
        shard_count, capacity, -1
    )
    total_send = select_rows(back_pick, row_total.reshape(slot_count, -1)).reshape(
        shard_count, capacity, -1
    )
    part_recv, peak_recv, total_recv = (
        lax.all_to_all(part_send, "seq", split_axis=0, concat_axis=0, tiled=True),
        lax.all_to_all(peak_send, "seq", split_axis=0, concat_axis=0, tiled=True),
        lax.all_to_all(total_send, "seq", split_axis=0, concat_axis=0, tiled=True),
    )
    entry_back = entry_pick.T
    parts_own = select_rows(entry_back, part_recv.reshape(shard_count * capacity, -1))
    parts_own = parts_own.reshape(stretch_count, 2, STRETCH, head_count, head_depth)
    peaks_own = select_rows(entry_back, peak_recv.reshape(shard_count * capacity, -1))
    peaks_own = peaks_own.reshape(stretch_count, 2, STRETCH, head_count)
    totals_own = select_rows(entry_back, total_recv.reshape(shard_count * capacity, -1))
    totals_own = totals_own.reshape(stretch_count, 2, STRETCH, head_count)
    top_peak = jnp.max(peaks_own, axis=1)
    factor = jnp.exp(peaks_own - top_peak[:, None])
    denominator = jnp.sum(factor * totals_own, axis=1)
    combined = jnp.sum(factor[..., None] * parts_own, axis=1) / denominator[..., None]
    combined = combined * live_rows[:, :, None, None]
    att_win = combined.astype(jnp.bfloat16).reshape(tok_rows, width_dev)
    log_total = top_peak + jnp.log(denominator)
    g_wide = g_win.reshape(stretch_count, STRETCH, head_count, head_depth).astype(jnp.float32)
    inner_dot = jnp.sum(g_wide * combined, axis=-1)
    row_stats = jnp.repeat(jnp.stack([log_total, inner_dot], axis=1), 2, axis=0)
    stats_send = select_rows(entry_pick, row_stats.reshape(per_owner, -1)).reshape(
        shard_count, capacity, -1
    )
    stats_recv = lax.all_to_all(stats_send, "seq", split_axis=0, concat_axis=0, tiled=True)
    g_slots = select_rows(slot_pick, g_recv.reshape(shard_count * capacity, -1))
    g_slots = g_slots.reshape(slot_count, STRETCH, head_count, head_depth)
    stats_slots = select_rows(slot_pick, stats_recv.reshape(shard_count * capacity, -1))
    stats_slots = stats_slots.reshape(slot_count, 2, STRETCH, head_count)
    prob_full = jnp.exp(scores - stats_slots[:, 0][..., None])
    prob_low = prob_full.astype(jnp.bfloat16)
    grad_values = jnp.einsum(
        "sihj,sihd->sjhd", prob_low, g_slots, preferred_element_type=jnp.float32
    )
    grad_prob = jnp.einsum(
        "sihd,sjhd->sihj", g_slots, value_rows, preferred_element_type=jnp.float32
    )
    grad_scores = prob_full * (grad_prob - stats_slots[:, 1][..., None])
    scores_low = grad_scores.astype(jnp.bfloat16)
    grad_rows = (
        jnp.einsum("sihj,sjhd->sihd", scores_low, key_rows, preferred_element_type=jnp.float32)
        * scale_factor
    )
    grad_keys = (
        jnp.einsum("sihj,sihd->sjhd", scores_low, q_slots, preferred_element_type=jnp.float32)
        * scale_factor
    )
    d_kv = jnp.stack(
        [
            grad_keys.reshape(slot_count, NB_LEN, width_dev),
            grad_values.reshape(slot_count, NB_LEN, width_dev),
        ],
        axis=2,
    ).astype(jnp.bfloat16)
    bias_part = bias_fold(jnp.sum(grad_scores, axis=0).transpose(1, 0, 2))
    rows_send = select_rows(back_pick, grad_rows.reshape(slot_count, -1)).reshape(
        shard_count, capacity, -1
    )
    rows_recv = lax.all_to_all(rows_send, "seq", split_axis=0, concat_axis=0, tiled=True)
    grad_entries = select_rows(entry_back, rows_recv.reshape(shard_count * capacity, -1))
    grad_entries = grad_entries.reshape(stretch_count, 2, STRETCH * width_dev)
    grad_win = (
        (grad_entries[:, 0] + grad_entries[:, 1]).astype(jnp.bfloat16).reshape(tok_rows, width_dev)
    )
    both_before = passed_along(
        jnp.stack([att_win[tok_rows - STRETCH :], grad_win[tok_rows - STRETCH :]]), "seq", 1
    )
    att_before = both_before[0]
    grad_before = both_before[1]
    attended = jnp.concatenate([att_before[1:], att_win[: tok_rows - STRETCH + 1]])
    d_query = jnp.concatenate([grad_before[1:], grad_win[: tok_rows - STRETCH + 1]])
    raw_sum = lax.psum(bias_part, ("grp", "seq"))
    squares = lax.psum(jnp.sum(raw_sum * raw_sum), "mp")
    d_bias = raw_sum * jnp.minimum(1.0, 1.0 / jnp.sqrt(squares + 1e-12))
    return (attended[None], d_query[None], d_kv[None], d_bias)


WIDE = 2 * NB_LEN
VMEM_USE = 60 * 1024 * 1024
MESH = pl.DeviceIdType.MESH


def dot(a, b, contract=((1,), (0,))):
    return lax.dot_general(a, b, (contract, ((), ())), preferred_element_type=jnp.float32)


def iota(shape, axis):
    return lax.broadcasted_iota(jnp.int32, shape, axis)


def one_hot(flags):
    return jnp.where(flags, 1.0, 0.0).astype(jnp.bfloat16)


def halves(x):
    high = x.astype(jnp.bfloat16)
    return high, (x - high.astype(jnp.float32)).astype(jnp.bfloat16)


def dot_chosen(x, picker):
    high, rest = halves(x)
    left = x - high.astype(jnp.float32)
    low = (left - rest.astype(jnp.float32)).astype(jnp.bfloat16)
    wide = jnp.concatenate([p.astype(jnp.float32) for p in (high, rest, low)], axis=0)
    out = dot(wide.astype(jnp.bfloat16), picker)
    return out[:8] + out[8:16] + out[16:]


def pair_kernel(
    q_hbm, g_hbm, kv_hbm, target_hbm, bias_ref,
    att_hbm, dq_hbm, dkv_hbm, dbias_ref,
    target_ref, q_ref, g_ref, kv_pairs, kv_ref, q_peer, g_peer,
    windows, weights, cotangents, mixed, rows_own, rows_send, rows_recv,
    gather_ref, scatter_ref, turned_ref, unmix_ref, bias_rows, dkv_pairs, att_ref, dq_ref,
    stat_send, stat_recv, raw_all, norm_all,
    own_sems, kv_sems, in_send, in_recv, stat_send_sems, stat_recv_sems, row_send_sems, row_recv_sems,
    raw_send_sems, raw_recv_sems, norm_send_sems, norm_recv_sems, out_sems, dkv_sems,
):
    heads, rel = bias_ref.shape
    slots = kv_ref.shape[0]
    tok = q_ref.shape[0]
    depth = kv_ref.shape[-1]
    lead = (STRETCH - 1) // 16 * 16
    late = pl.ds(lead, tok - lead)
    early = pl.ds(0, lead)
    groups, mps = lax.axis_size("grp"), lax.axis_size("mp")
    plane = 2 * groups
    scale = depth ** (-0.5)
    grp, seq, mp = lax.axis_index("grp"), lax.axis_index("seq"), lax.axis_index("mp")
    here = grp * 2 + seq
    peer = {"seq": 1 - seq}

    def plane_at(step):
        there = lax.rem(here + step, plane)
        return {"grp": there // 2, "seq": there % 2}

    def mp_at(step):
        return {"mp": lax.rem(mp + step, mps)}

    def remote(src, dst, send_sem, recv_sem, device):
        return pltpu.make_async_remote_copy(
            src_ref=src, dst_ref=dst, send_sem=send_sem, recv_sem=recv_sem,
            device_id=device, device_id_type=MESH,
        )

    def cols(h):
        return pl.ds(h * depth, depth)

    def q_copy(h, rows, lane):
        return remote(
            q_hbm.at[0, rows, cols(h)], q_peer.at[h, rows], in_send.at[lane, h], in_recv.at[lane, h], peer
        )

    def g_copy(h, rows, lane):
        return remote(
            g_hbm.at[0, rows, cols(h)], g_peer.at[h, rows], in_send.at[lane, h], in_recv.at[lane, h], peer
        )

    def in_late(h):
        return q_copy(h, late, 0), g_copy(h, late, 1)

    def in_early(h):
        return q_copy(h, early, 2), g_copy(h, early, 3)

    def kv_copy(h, r):
        return pltpu.make_async_copy(kv_hbm.at[0, r, :, :, cols(h)], kv_pairs.at[h, r], kv_sems.at[h, r])

    def stat_copy(part):
        return remote(
            stat_send.at[part], stat_recv.at[part], stat_send_sems.at[part], stat_recv_sems.at[part], peer
        )

    def row_copy(h, rows, lane):
        return remote(
            rows_send.at[h, rows], rows_recv.at[h, rows],
            row_send_sems.at[lane, h], row_recv_sems.at[lane, h], peer,
        )

    def row_late(h):
        return row_copy(h, late, 0)

    def row_early(h):
        return row_copy(h, early, 1)

    def raw_copy(k):
        return remote(raw_all.at[here], raw_all.at[here], raw_send_sems.at[k], raw_recv_sems.at[k], plane_at(k))

    def norm_copy(k):
        return remote(norm_all.at[mp], norm_all.at[mp], norm_send_sems.at[k], norm_recv_sems.at[k], mp_at(k))

    def dkv_copy(h, r):
        return pltpu.make_async_copy(dkv_pairs.at[h, r], dkv_hbm.at[0, r, :, :, cols(h)], dkv_sems.at[h, r])

    def out_copies():
        return (
            pltpu.make_async_copy(att_ref, att_hbm.at[0], out_sems.at[0]),
            pltpu.make_async_copy(dq_ref, dq_hbm.at[0], out_sems.at[1]),
        )

    def each(count, body):
        for i in range(count):
            body(i)

    barrier = pltpu.get_barrier_semaphore()
    for step in range(1, plane):
        pl.semaphore_signal(barrier, inc=1, device_id=plane_at(step), device_id_type=MESH)
    for step in range(1, mps):
        pl.semaphore_signal(barrier, inc=1, device_id=mp_at(step), device_id_type=MESH)
    own_copies = [
        pltpu.make_async_copy(target_hbm, target_ref, own_sems.at[0]),
        pltpu.make_async_copy(q_hbm.at[0], q_ref, own_sems.at[1]),
        pltpu.make_async_copy(g_hbm.at[0], g_ref, own_sems.at[2]),
    ]
    for copy in own_copies:
        copy.start()

    def start_kv(h):
        for r in range(slots):
            kv_copy(h, r).start()

    each(heads, start_kv)
    place = iota((2 * WIDE, WIDE), 0) + 2 * iota((2 * WIDE, WIDE), 1)
    unmix_ref[...] = one_hot(place == 2 * rel - 1)
    place = iota((WIDE, 2 * WIDE), 1) + 2 * iota((WIDE, 2 * WIDE), 0)
    bias_rows[...] = jnp.zeros((8, WIDE), jnp.float32)
    bias_rows[:heads, :rel] = bias_ref[...]
    turned = dot_chosen(bias_rows[...], one_hot(place == 2 * (rel - 1)))
    for h in range(heads):
        turned_ref[h] = jnp.broadcast_to(turned[h : h + 1], (8, 2 * WIDE))
    pl.semaphore_wait(barrier, plane - 1 + mps - 1)

    def start_rows(h):
        for copy in in_late(h):
            copy.start()

        @pl.when(seq == 1)
        def _():
            for copy in in_early(h):
                copy.start()

    each(heads, start_rows)

    @pl.when(seq == 1)
    def _():
        q_peer[:, early] = jnp.zeros((heads, lead, depth), jnp.bfloat16)
        g_peer[:, early] = jnp.zeros((heads, lead, depth), jnp.bfloat16)

    @pl.when(seq == 0)
    def _():
        rows_recv[:, early] = jnp.zeros((heads, lead, 2 * depth), jnp.bfloat16)

    for copy in own_copies:
        copy.wait()
    entries = [target_ref[0, r] for r in range(slots)]

    def token_of(axis, shape):
        place = iota(shape, axis)
        return jnp.where(place < tok, tok * seq + place, tok * (1 - seq) + place - tok)

    for r in range(slots):
        rows = pl.ds(r * STRETCH, STRETCH)
        first = (STRETCH - 1) + STRETCH * (entries[r] // 2)
        flat = (STRETCH, 2 * tok)
        gather_ref[rows, :] = one_hot(token_of(1, flat) == iota(flat, 0) + first)
    scatter_ref[...] = gather_ref[...].T
    odd = iota((STRETCH, WIDE), 1) % 2 == 1
    lane = iota((STRETCH, 128), 1)

    def unpair(h):
        for r in range(slots):
            kv_copy(h, r).wait()
            kv_ref[r, h] = kv_pairs[h, r].reshape(WIDE, depth)

    each(heads, unpair)

    def forward(h):
        table = jnp.zeros((STRETCH, 128), jnp.float32)
        wide = jnp.broadcast_to(turned_ref[h][:1], (STRETCH, 2 * WIDE))
        grid = pltpu.roll(wide, 2 * WIDE - 126, 1, stride=2, stride_axis=0)[:, :WIDE]
        grid = jnp.where(odd, -1e30, grid)
        mine = jnp.concatenate([q_ref[:, cols(h)], g_ref[:, cols(h)]], axis=1)
        for copy in in_late(h):
            copy.wait_recv()

        @pl.when(seq == 0)
        def _():
            for copy in in_early(h):
                copy.wait_recv()

        other = jnp.concatenate([q_peer[h], g_peer[h]], axis=1)
        picked = dot(gather_ref[...], jnp.concatenate([mine, other], axis=0)).astype(jnp.bfloat16)
        for r in range(slots):
            rows = picked[r * STRETCH : (r + 1) * STRETCH]
            both = jnp.concatenate([rows[:, :depth], rows[:, depth:]], axis=0)
            windows[h, r] = both
            prod = dot(both, kv_ref[r, h], ((1,), (1,)))
            scores = prod[:STRETCH] * scale + grid
            grad_prob = prod[STRETCH:]
            peak = jnp.max(scores, axis=1, keepdims=True)
            expd = jnp.exp(scores - peak)
            total = jnp.sum(expd, axis=1, keepdims=True)
            expd = pltpu.roll(expd, 1, 1)
            inner = jnp.sum(expd * grad_prob, axis=1, keepdims=True)
            weights[h, r] = expd
            cotangents[h, r] = grad_prob
            base = entries[r]
            table = jnp.where(lane == base, peak, table)
            table = jnp.where(lane == base + 8, total, table)
            table = jnp.where(lane == base + 16, inner, table)
        quarter = STRETCH // 4
        packed = table[:quarter]
        for k in range(1, 4):
            packed = packed + pltpu.roll(table[k * quarter : (k + 1) * quarter], 32 * k, 1)
        stat_send[h] = packed
        stat_copy(h).start()

    def partner(x):
        return jnp.where(lane % 2 == 0, pltpu.roll(x, 127, 1), pltpu.roll(x, 1, 1))

    row8 = iota((8, 2 * WIDE), 0)

    def backward(h, stacked):
        stat_copy(h).wait_recv()
        packed = stat_send[h] + stat_recv[h]
        table = jnp.concatenate(
            [packed] + [pltpu.roll(packed, 128 - 32 * k, 1) for k in range(1, 4)], axis=0
        )
        table = jnp.where(lane < 32, table, 0.0)
        total = pltpu.roll(table, 120, 1)
        inner = pltpu.roll(table, 112, 1)
        other_peak = partner(table)
        top = jnp.maximum(table, other_peak)
        mine_f, other_f = jnp.exp(table - top), jnp.exp(other_peak - top)
        denominator = mine_f * total + other_f * partner(total)
        inner = (mine_f * inner + other_f * partner(inner)) / denominator
        norm = mine_f / denominator
        bias_sum = jnp.zeros((STRETCH, WIDE), jnp.float32)
        parts = []
        for r in range(slots):
            at = lane == entries[r]
            factor = jnp.sum(jnp.where(at, norm, 0.0), axis=1, keepdims=True)
            shift = jnp.sum(jnp.where(at, inner, 0.0), axis=1, keepdims=True)
            prob = weights[h, r] * factor
            grad = prob * (cotangents[h, r] - shift)
            bias_sum = bias_sum + grad
            mix = jnp.concatenate([pltpu.roll(grad, WIDE - 1, 1), prob], axis=0).astype(jnp.bfloat16)
            mixed[h, r] = mix
            out = dot(mix, kv_ref[r, h])
            parts.append(
                jnp.concatenate([out[STRETCH:], out[:STRETCH] * scale], axis=1).astype(jnp.bfloat16)
            )
        rows = dot(scatter_ref[...], jnp.concatenate(parts, axis=0))
        rows_own[h] = rows[:tok]
        rows_send[h] = rows[tok:].astype(jnp.bfloat16)
        row_late(h).start()

        @pl.when(seq == 0)
        def _():
            row_early(h).start()

        folded = jnp.concatenate([bias_sum, jnp.zeros_like(bias_sum)], axis=1)
        half = STRETCH // 2
        while half >= 8:
            folded = pltpu.roll(folded[:half], 2 * half, 1) + folded[half:]
            half //= 2
        for bit in (4, 2, 1):
            folded = jnp.where((row8 // bit) % 2 == 0, pltpu.roll(folded, 2 * bit, 1), folded)
        return jnp.where(row8 == h, jnp.sum(folded, axis=0, keepdims=True), stacked)

    stacked = jnp.zeros((8, 2 * WIDE), jnp.float32)
    forward(0)
    for h in range(heads):
        if h + 1 < heads:
            forward(h + 1)
        stacked = backward(h, stacked)
    raw_all[here] = dot_chosen(stacked, unmix_ref[...])
    for k in range(1, plane):
        raw_copy(k).start()

    row_scale = jnp.where(iota((WIDE, depth), 0) % 2 == 0, scale, 1.0)

    def finish_kv(h):
        for r in range(slots):
            dkv = dot(mixed[h, r], windows[h, r], ((0,), (0,))) * row_scale
            dkv_pairs[h, r] = dkv.astype(jnp.bfloat16).reshape(NB_LEN, 2, depth)
            dkv_copy(h, r).start()

    each(heads // 2, finish_kv)
    for k in range(1, plane):
        raw_copy(k).wait_recv()
    raw = raw_all[0]
    for k in range(1, plane):
        raw = raw + raw_all[k]
    norm_all[mp] = jnp.broadcast_to(jnp.sum(raw * raw, keepdims=True), (8, 128))
    for k in range(1, mps):
        norm_copy(k).start()

    each(heads - heads // 2, lambda h: finish_kv(h + heads // 2))

    def finish_rows(h):
        row_late(h).wait_recv()

        @pl.when(seq == 1)
        def _():
            row_early(h).wait_recv()

        rows = rows_own[h] + rows_recv[h].astype(jnp.float32)
        att_ref[:, cols(h)] = rows[:, :depth].astype(jnp.bfloat16)
        dq_ref[:, cols(h)] = rows[:, depth:].astype(jnp.bfloat16)

    each(heads, finish_rows)
    for copy in out_copies():
        copy.start()
    for k in range(1, mps):
        norm_copy(k).wait_recv()
    squares = norm_all[0]
    for k in range(1, mps):
        squares = squares + norm_all[k]
    clip = jnp.minimum(1.0, 1.0 / jnp.sqrt(squares[:, :1] + 1e-12))
    dbias_ref[...] = (raw * clip)[:heads, :rel]

    def drain(h):
        for copy in in_late(h):
            copy.wait_send()
        row_late(h).wait_send()
        stat_copy(h).wait_send()

        @pl.when(seq == 1)
        def _():
            for copy in in_early(h):
                copy.wait_send()

        @pl.when(seq == 0)
        def _():
            row_early(h).wait_send()

        for r in range(slots):
            dkv_copy(h, r).wait()

    each(heads, drain)
    for k in range(1, plane):
        raw_copy(k).wait_send()
    for k in range(1, mps):
        norm_copy(k).wait_send()
    for copy in out_copies():
        copy.wait()


def write_kernel(
    att, dq, dkv, dbias, att_out, dq_out, dkv_out, dbias_out,
    att_held, dq_held, dkv_held, dbias_held, load_sems, store_sems,
):
    slots = dkv.shape[1]
    routes = [(dkv.at[0, r], dkv_held.at[r], dkv_out.at[0, r]) for r in range(slots)]
    routes += [(att, att_held, att_out), (dq, dq_held, dq_out), (dbias, dbias_held, dbias_out)]
    loads = [pltpu.make_async_copy(a, b, load_sems.at[k]) for k, (a, b, _) in enumerate(routes)]
    stores = [pltpu.make_async_copy(b, c, store_sems.at[k]) for k, (_, b, c) in enumerate(routes)]
    for copy in loads:
        copy.start()
    for load, store in zip(loads, stores):
        load.wait()
        store.start()
    for copy in stores:
        copy.wait()


def pair_exchange(queries, d_out, neighbour_kv, target, bias):
    _, tok, width = queries.shape
    heads = bias.shape[0]
    depth = width // heads
    slots = neighbour_kv.shape[1]
    plane, mps = 2 * lax.axis_size("grp"), lax.axis_size("mp")
    vmem = pl.BlockSpec(memory_space=pltpu.VMEM)
    hbm = pl.BlockSpec(memory_space=pltpu.HBM)
    f32, bf16, dma = jnp.float32, jnp.bfloat16, pltpu.SemaphoreType.DMA
    results = tuple(jax.ShapeDtypeStruct(x.shape, x.dtype) for x in (queries, d_out, neighbour_kv, bias))
    parts = pl.pallas_call(
        pair_kernel,
        out_shape=results,
        in_specs=[hbm, hbm, hbm, hbm, vmem],
        out_specs=(hbm, hbm, hbm, vmem),
        scratch_shapes=[
            pltpu.SMEM(target.shape, jnp.int32),
            pltpu.VMEM((tok, width), bf16),
            pltpu.VMEM((tok, width), bf16),
            pltpu.VMEM((heads, slots, NB_LEN, 2, depth), bf16),
            pltpu.VMEM((slots, heads, WIDE, depth), bf16),
            pltpu.VMEM((heads, tok, depth), bf16),
            pltpu.VMEM((heads, tok, depth), bf16),
            pltpu.VMEM((heads, slots, 2 * STRETCH, depth), bf16),
            pltpu.VMEM((heads, slots, STRETCH, WIDE), f32),
            pltpu.VMEM((heads, slots, STRETCH, WIDE), f32),
            pltpu.VMEM((heads, slots, 2 * STRETCH, WIDE), bf16),
            pltpu.VMEM((heads, tok, 2 * depth), f32),
            pltpu.VMEM((heads, tok, 2 * depth), bf16),
            pltpu.VMEM((heads, tok, 2 * depth), bf16),
            pltpu.VMEM((slots * STRETCH, 2 * tok), bf16),
            pltpu.VMEM((2 * tok, slots * STRETCH), bf16),
            pltpu.VMEM((heads, 8, 2 * WIDE), f32),
            pltpu.VMEM((2 * WIDE, WIDE), bf16),
            pltpu.VMEM((8, WIDE), f32),
            pltpu.VMEM((heads, slots, NB_LEN, 2, depth), bf16),
            pltpu.VMEM((tok, width), bf16),
            pltpu.VMEM((tok, width), bf16),
            pltpu.VMEM((heads, STRETCH // 4, 128), f32),
            pltpu.VMEM((heads, STRETCH // 4, 128), f32),
            pltpu.VMEM((plane, 8, WIDE), f32),
            pltpu.VMEM((mps, 8, 128), f32),
            dma((3,)),
            dma((heads, slots)),
            dma((4, heads)),
            dma((4, heads)),
            dma((heads,)),
            dma((heads,)),
            dma((2, heads)),
            dma((2, heads)),
            dma((plane,)),
            dma((plane,)),
            dma((mps,)),
            dma((mps,)),
            dma((2,)),
            dma((heads, slots)),
        ],
        compiler_params=pltpu.CompilerParams(
            collective_id=0, has_side_effects=True, vmem_limit_bytes=VMEM_USE
        ),
    )(queries, d_out, neighbour_kv, target, bias)
    return pl.pallas_call(
        write_kernel,
        out_shape=results,
        in_specs=[hbm] * 4,
        out_specs=(hbm,) * 4,
        scratch_shapes=[
            pltpu.VMEM(queries.shape, bf16),
            pltpu.VMEM(d_out.shape, bf16),
            pltpu.VMEM(neighbour_kv.shape[1:], bf16),
            pltpu.VMEM(bias.shape, f32),
            dma((slots + 3,)),
            dma((slots + 3,)),
        ],
        compiler_params=pltpu.CompilerParams(vmem_limit_bytes=VMEM_USE),
    )(*parts)


def local(queries, d_out, neighbour_kv, target, bias):
    tok = queries.shape[1]
    fits = (
        lax.axis_size("seq") == 2
        and neighbour_kv.shape[1] == 2 * (tok // STRETCH)
        and tok == 128
        and bias.shape == (4, 191)
        and queries.shape[2] == 512
    )
    run = pair_exchange if fits else shard_exchange
    return run(queries, d_out, neighbour_kv, target, bias)


def solution(mesh):
    in_specs = (
        P("grp", "seq", "mp"),
        P("grp", "seq", "mp"),
        P("grp", "seq", None, None, "mp"),
        P("grp", "seq"),
        P("mp", None),
    )
    out_specs = (
        P("grp", "seq", "mp"),
        P("grp", "seq", "mp"),
        P("grp", "seq", None, None, "mp"),
        P("mp", None),
    )
    return jax.shard_map(local, mesh=mesh, in_specs=in_specs, out_specs=out_specs, check_vma=False)
```

```python
import jax
import jax.numpy as jnp
from jax import lax
from jax.experimental import pallas as pl
from jax.experimental.pallas import tpu as pltpu
from jax.sharding import PartitionSpec as P

STRETCH = 64
NB_LEN = 128


def passed_along(block, axis, distance):
    devices = range(lax.axis_size(axis))
    route = [(i - distance, i) for i in devices if i - distance in devices]
    return lax.ppermute(block, axis, route)


def bias_grid(lookup, row_count, col_count):
    head_num = lookup.shape[0]
    span = row_count + col_count
    padded = jnp.pad(lookup, ((0, 0), (0, 1)))
    flattened = jnp.tile(padded, (1, row_count))
    flattened = jnp.pad(flattened, ((0, 0), (0, row_count)))
    shaped = flattened.reshape(head_num, row_count, span + 1)[:, :, :col_count]
    return shaped[:, :, ::-1]


def bias_fold(grads):
    head_num, row_count, col_count = grads.shape
    turned = grads[:, :, ::-1]
    padded = jnp.pad(turned, ((0, 0), (0, 0), (0, row_count)))
    flattened = padded.reshape(head_num, row_count * (row_count + col_count))
    flattened = flattened[:, : row_count * (row_count + col_count - 1)]
    return jnp.sum(flattened.reshape(head_num, row_count, row_count + col_count - 1), axis=1)


def select_rows(picker, lookup):
    chosen = jnp.dot(
        picker.astype(lookup.dtype),
        lookup,
        preferred_element_type=jnp.float32,
        precision=lax.Precision.HIGHEST,
    )
    return chosen.astype(lookup.dtype)


def slot_places(target_row, owners, capacity, per_owner):
    is_used = target_row >= 0
    owner_of = jnp.where(is_used, target_row // per_owner, -1)
    positions = jnp.arange(target_row.shape[0])
    earlier = (
        (positions[None, :] < positions[:, None])
        & (owner_of[None, :] == owner_of[:, None])
        & is_used[None, :]
    )
    rank_of = jnp.sum(earlier.astype(jnp.int32), axis=1)
    match_owner = owner_of[None, :] == jnp.arange(owners)[:, None]
    match_rank = rank_of[None, :] == jnp.arange(capacity)[:, None]
    return match_owner[:, None, :] & match_rank[None, :, :] & is_used[None, None, :]


def shard_exchange(queries, d_out, neighbour_kv, target, bias):
    tok_rows = queries.shape[1]
    width_dev = queries.shape[2]
    head_count = bias.shape[0]
    head_depth = width_dev // head_count
    stretch_count = tok_rows // STRETCH
    per_owner = 2 * stretch_count
    shard_count = lax.axis_size("seq")
    my_index = lax.axis_index("seq")
    group_size = min(shard_count, per_owner)
    capacity = (per_owner + group_size - 1) // group_size
    seq_stretches = min(2048, tok_rows * shard_count) // STRETCH
    scale_factor = head_depth ** (-0.5)
    bias_rows = bias_grid(bias, STRETCH, NB_LEN).transpose(1, 0, 2)
    q_rows = queries[0]
    g_rows = d_out[0]
    next_pair = passed_along(jnp.stack([q_rows[:STRETCH], g_rows[:STRETCH]]), "seq", -1)
    row_ids = jnp.arange(STRETCH)
    stretch_ids = my_index * stretch_count + jnp.arange(stretch_count)
    is_live = (row_ids[None, :] == 0) | ((stretch_ids[:, None] + 1) % seq_stretches != 0)
    live_rows = is_live.astype(jnp.float32)
    q_win = jnp.concatenate([q_rows, next_pair[0]])[STRETCH - 1 : STRETCH - 1 + tok_rows]
    q_win = q_win.reshape(stretch_count, STRETCH * width_dev)
    g_win = jnp.concatenate([g_rows, next_pair[1]])[STRETCH - 1 : STRETCH - 1 + tok_rows]
    g_win = g_win.reshape(stretch_count, STRETCH, width_dev) * is_live[:, :, None].astype(
        jnp.bfloat16
    )
    g_win = g_win.reshape(stretch_count, STRETCH * width_dev)
    my_targets = target[0]
    slot_count = my_targets.shape[0]
    send_map = slot_places(my_targets, shard_count, capacity, per_owner)
    id_buffer = jnp.sum(jnp.where(send_map, my_targets[None, None, :] + 1, 0), axis=2) - 1
    recv_ids = lax.all_to_all(id_buffer, "seq", split_axis=0, concat_axis=0, tiled=True)
    flat_ids = recv_ids.reshape(shard_count * capacity)
    has_entry = flat_ids >= 0
    local_entry = flat_ids - my_index * per_owner
    entry_pick = (local_entry[:, None] == jnp.arange(per_owner)[None, :]) & has_entry[:, None]
    stretch_pick = (local_entry[:, None] // 2 == jnp.arange(stretch_count)[None, :]) & has_entry[
        :, None
    ]
    back_pick = send_map.reshape(shard_count * capacity, slot_count)
    slot_pick = back_pick.T
    q_send = select_rows(stretch_pick, q_win).reshape(shard_count, capacity, STRETCH * width_dev)
    g_send = select_rows(stretch_pick, g_win).reshape(shard_count, capacity, STRETCH * width_dev)
    q_recv, g_recv = (
        lax.all_to_all(q_send, "seq", split_axis=0, concat_axis=0, tiled=True),
        lax.all_to_all(g_send, "seq", split_axis=0, concat_axis=0, tiled=True),
    )
    q_slots = select_rows(slot_pick, q_recv.reshape(shard_count * capacity, -1))
    q_slots = q_slots.reshape(slot_count, STRETCH, head_count, head_depth)
    stored = neighbour_kv[0]
    key_rows = stored[:, :, 0].reshape(slot_count, NB_LEN, head_count, head_depth)
    value_rows = stored[:, :, 1].reshape(slot_count, NB_LEN, head_count, head_depth)
    scores = jnp.einsum("sihd,sjhd->sihj", q_slots, key_rows, preferred_element_type=jnp.float32)
    scores = scores * scale_factor + bias_rows[None]
    peak_val = jnp.max(scores, axis=-1)
    weights = jnp.exp(scores - peak_val[..., None])
    row_total = jnp.sum(weights, axis=-1)
    partial_value = jnp.einsum(
        "sihj,sjhd->sihd",
        weights.astype(jnp.bfloat16),
        value_rows,
        preferred_element_type=jnp.float32,
    )
    part_send = select_rows(back_pick, partial_value.reshape(slot_count, -1)).reshape(
        shard_count, capacity, -1
    )
    peak_send = select_rows(back_pick, peak_val.reshape(slot_count, -1)).reshape(
        shard_count, capacity, -1
    )
    total_send = select_rows(back_pick, row_total.reshape(slot_count, -1)).reshape(
        shard_count, capacity, -1
    )
    part_recv, peak_recv, total_recv = (
        lax.all_to_all(part_send, "seq", split_axis=0, concat_axis=0, tiled=True),
        lax.all_to_all(peak_send, "seq", split_axis=0, concat_axis=0, tiled=True),
        lax.all_to_all(total_send, "seq", split_axis=0, concat_axis=0, tiled=True),
    )
    entry_back = entry_pick.T
    parts_own = select_rows(entry_back, part_recv.reshape(shard_count * capacity, -1))
    parts_own = parts_own.reshape(stretch_count, 2, STRETCH, head_count, head_depth)
    peaks_own = select_rows(entry_back, peak_recv.reshape(shard_count * capacity, -1))
    peaks_own = peaks_own.reshape(stretch_count, 2, STRETCH, head_count)
    totals_own = select_rows(entry_back, total_recv.reshape(shard_count * capacity, -1))
    totals_own = totals_own.reshape(stretch_count, 2, STRETCH, head_count)
    top_peak = jnp.max(peaks_own, axis=1)
    factor = jnp.exp(peaks_own - top_peak[:, None])
    denominator = jnp.sum(factor * totals_own, axis=1)
    combined = jnp.sum(factor[..., None] * parts_own, axis=1) / denominator[..., None]
    combined = combined * live_rows[:, :, None, None]
    att_win = combined.astype(jnp.bfloat16).reshape(tok_rows, width_dev)
    log_total = top_peak + jnp.log(denominator)
    g_wide = g_win.reshape(stretch_count, STRETCH, head_count, head_depth).astype(jnp.float32)
    inner_dot = jnp.sum(g_wide * combined, axis=-1)
    row_stats = jnp.repeat(jnp.stack([log_total, inner_dot], axis=1), 2, axis=0)
    stats_send = select_rows(entry_pick, row_stats.reshape(per_owner, -1)).reshape(
        shard_count, capacity, -1
    )
    stats_recv = lax.all_to_all(stats_send, "seq", split_axis=0, concat_axis=0, tiled=True)
    g_slots = select_rows(slot_pick, g_recv.reshape(shard_count * capacity, -1))
    g_slots = g_slots.reshape(slot_count, STRETCH, head_count, head_depth)
    stats_slots = select_rows(slot_pick, stats_recv.reshape(shard_count * capacity, -1))
    stats_slots = stats_slots.reshape(slot_count, 2, STRETCH, head_count)
    prob_full = jnp.exp(scores - stats_slots[:, 0][..., None])
    prob_low = prob_full.astype(jnp.bfloat16)
    grad_values = jnp.einsum(
        "sihj,sihd->sjhd", prob_low, g_slots, preferred_element_type=jnp.float32
    )
    grad_prob = jnp.einsum(
        "sihd,sjhd->sihj", g_slots, value_rows, preferred_element_type=jnp.float32
    )
    grad_scores = prob_full * (grad_prob - stats_slots[:, 1][..., None])
    scores_low = grad_scores.astype(jnp.bfloat16)
    grad_rows = (
        jnp.einsum("sihj,sjhd->sihd", scores_low, key_rows, preferred_element_type=jnp.float32)
        * scale_factor
    )
    grad_keys = (
        jnp.einsum("sihj,sihd->sjhd", scores_low, q_slots, preferred_element_type=jnp.float32)
        * scale_factor
    )
    d_kv = jnp.stack(
        [
            grad_keys.reshape(slot_count, NB_LEN, width_dev),
            grad_values.reshape(slot_count, NB_LEN, width_dev),
        ],
        axis=2,
    ).astype(jnp.bfloat16)
    bias_part = bias_fold(jnp.sum(grad_scores, axis=0).transpose(1, 0, 2))
    rows_send = select_rows(back_pick, grad_rows.reshape(slot_count, -1)).reshape(
        shard_count, capacity, -1
    )
    rows_recv = lax.all_to_all(rows_send, "seq", split_axis=0, concat_axis=0, tiled=True)
    grad_entries = select_rows(entry_back, rows_recv.reshape(shard_count * capacity, -1))
    grad_entries = grad_entries.reshape(stretch_count, 2, STRETCH * width_dev)
    grad_win = (
        (grad_entries[:, 0] + grad_entries[:, 1]).astype(jnp.bfloat16).reshape(tok_rows, width_dev)
    )
    both_before = passed_along(
        jnp.stack([att_win[tok_rows - STRETCH :], grad_win[tok_rows - STRETCH :]]), "seq", 1
    )
    att_before = both_before[0]
    grad_before = both_before[1]
    attended = jnp.concatenate([att_before[1:], att_win[: tok_rows - STRETCH + 1]])
    d_query = jnp.concatenate([grad_before[1:], grad_win[: tok_rows - STRETCH + 1]])
    raw_sum = lax.psum(bias_part, ("grp", "seq"))
    squares = lax.psum(jnp.sum(raw_sum * raw_sum), "mp")
    d_bias = raw_sum * jnp.minimum(1.0, 1.0 / jnp.sqrt(squares + 1e-12))
    return (attended[None], d_query[None], d_kv[None], d_bias)


WIDE = 2 * NB_LEN
VMEM_USE = 60 * 1024 * 1024
MESH = pl.DeviceIdType.MESH


def dot(a, b, contract=((1,), (0,))):
    return lax.dot_general(a, b, (contract, ((), ())), preferred_element_type=jnp.float32)


def iota(shape, axis):
    return lax.broadcasted_iota(jnp.int32, shape, axis)


def one_hot(flags):
    return jnp.where(flags, 1.0, 0.0).astype(jnp.bfloat16)


def halves(x):
    high = x.astype(jnp.bfloat16)
    return high, (x - high.astype(jnp.float32)).astype(jnp.bfloat16)


def dot_chosen(x, picker):
    high, rest = halves(x)
    left = x - high.astype(jnp.float32)
    low = (left - rest.astype(jnp.float32)).astype(jnp.bfloat16)
    wide = jnp.concatenate([p.astype(jnp.float32) for p in (high, rest, low)], axis=0)
    out = dot(wide.astype(jnp.bfloat16), picker)
    return out[:8] + out[8:16] + out[16:]


def pair_kernel(
    q_hbm, g_hbm, kv_hbm, target_hbm, bias_ref,
    att_hbm, dq_hbm, dkv_hbm, dbias_ref,
    target_ref, q_ref, g_ref, kv_pairs, kv_ref, q_peer, g_peer,
    windows, weights, cotangents, mixed, rows_own, rows_send, rows_recv,
    gather_ref, scatter_ref, turned_ref, kv_turned, grids, unmix_ref, bias_rows, dkv_pairs, att_ref, dq_ref,
    stat_send, stat_recv, raw_all, norm_all,
    own_sems, kv_sems, in_send, in_recv, stat_send_sems, stat_recv_sems, row_send_sems, row_recv_sems,
    raw_send_sems, raw_recv_sems, norm_send_sems, norm_recv_sems, out_sems, dkv_sems,
):
    heads, rel = bias_ref.shape
    slots = kv_ref.shape[0]
    tok = q_ref.shape[0]
    depth = kv_ref.shape[-1]
    lead = (STRETCH - 1) // 16 * 16
    late = pl.ds(lead, tok - lead)
    early = pl.ds(0, lead)
    groups, mps = lax.axis_size("grp"), lax.axis_size("mp")
    plane = 2 * groups
    scale = depth ** (-0.5)
    grp, seq, mp = lax.axis_index("grp"), lax.axis_index("seq"), lax.axis_index("mp")
    here = grp * 2 + seq
    peer = {"seq": 1 - seq}

    def plane_at(step):
        there = lax.rem(here + step, plane)
        return {"grp": there // 2, "seq": there % 2}

    def mp_at(step):
        return {"mp": lax.rem(mp + step, mps)}

    def remote(src, dst, send_sem, recv_sem, device):
        return pltpu.make_async_remote_copy(
            src_ref=src, dst_ref=dst, send_sem=send_sem, recv_sem=recv_sem,
            device_id=device, device_id_type=MESH,
        )

    def cols(h):
        return pl.ds(h * depth, depth)

    def q_copy(h, rows, lane):
        return remote(
            q_hbm.at[0, rows, cols(h)], q_peer.at[h, rows], in_send.at[lane, h], in_recv.at[lane, h], peer
        )

    def g_copy(h, rows, lane):
        return remote(
            g_hbm.at[0, rows, cols(h)], g_peer.at[h, rows], in_send.at[lane, h], in_recv.at[lane, h], peer
        )

    def in_late(h):
        return q_copy(h, late, 0), g_copy(h, late, 1)

    def in_early(h):
        return q_copy(h, early, 2), g_copy(h, early, 3)

    def kv_copy(h, r):
        return pltpu.make_async_copy(kv_hbm.at[0, r, :, :, cols(h)], kv_pairs.at[h, r], kv_sems.at[h, r])

    def stat_copy(part):
        return remote(
            stat_send.at[part], stat_recv.at[part], stat_send_sems.at[part], stat_recv_sems.at[part], peer
        )

    def row_copy(h, rows, lane):
        return remote(
            rows_send.at[h, rows], rows_recv.at[h, rows],
            row_send_sems.at[lane, h], row_recv_sems.at[lane, h], peer,
        )

    def row_late(h):
        return row_copy(h, late, 0)

    def row_early(h):
        return row_copy(h, early, 1)

    def raw_copy(k):
        return remote(raw_all.at[here], raw_all.at[here], raw_send_sems.at[k], raw_recv_sems.at[k], plane_at(k))

    def norm_copy(k):
        return remote(norm_all.at[mp], norm_all.at[mp], norm_send_sems.at[k], norm_recv_sems.at[k], mp_at(k))

    def dkv_copy(h, r):
        return pltpu.make_async_copy(dkv_pairs.at[h, r], dkv_hbm.at[0, r, :, :, cols(h)], dkv_sems.at[h, r])

    def out_copies():
        return (
            pltpu.make_async_copy(att_ref, att_hbm.at[0], out_sems.at[0]),
            pltpu.make_async_copy(dq_ref, dq_hbm.at[0], out_sems.at[1]),
        )

    def each(count, body):
        for i in range(count):
            body(i)

    barrier = pltpu.get_barrier_semaphore()
    for step in range(1, plane):
        pl.semaphore_signal(barrier, inc=1, device_id=plane_at(step), device_id_type=MESH)
    for step in range(1, mps):
        pl.semaphore_signal(barrier, inc=1, device_id=mp_at(step), device_id_type=MESH)
    own_copies = [
        pltpu.make_async_copy(target_hbm, target_ref, own_sems.at[0]),
        pltpu.make_async_copy(q_hbm.at[0], q_ref, own_sems.at[1]),
        pltpu.make_async_copy(g_hbm.at[0], g_ref, own_sems.at[2]),
    ]
    for copy in own_copies:
        copy.start()

    def start_kv(h):
        for r in range(slots):
            kv_copy(h, r).start()

    each(heads, start_kv)
    place = iota((2 * WIDE, WIDE), 0) + 2 * iota((2 * WIDE, WIDE), 1)
    unmix_ref[...] = one_hot(place == 2 * rel - 1)
    place = iota((WIDE, 2 * WIDE), 1) + 2 * iota((WIDE, 2 * WIDE), 0)
    bias_rows[...] = jnp.zeros((8, WIDE), jnp.float32)
    bias_rows[:heads, :rel] = bias_ref[...]
    turned = dot_chosen(bias_rows[...], one_hot(place == 2 * (rel - 1)))
    for h in range(heads):
        turned_ref[h] = jnp.broadcast_to(turned[h : h + 1], (8, 2 * WIDE))
    pl.semaphore_wait(barrier, plane - 1 + mps - 1)

    def start_rows(h):
        for copy in in_late(h):
            copy.start()

        @pl.when(seq == 1)
        def _():
            for copy in in_early(h):
                copy.start()

    each(heads, start_rows)

    @pl.when(seq == 1)
    def _():
        q_peer[:, early] = jnp.zeros((heads, lead, depth), jnp.bfloat16)
        g_peer[:, early] = jnp.zeros((heads, lead, depth), jnp.bfloat16)

    @pl.when(seq == 0)
    def _():
        rows_recv[:, early] = jnp.zeros((heads, lead, 2 * depth), jnp.bfloat16)

    for copy in own_copies:
        copy.wait()
    entries = [target_ref[0, r] for r in range(slots)]

    def token_of(axis, shape):
        place = iota(shape, axis)
        return jnp.where(place < tok, tok * seq + place, tok * (1 - seq) + place - tok)

    for r in range(slots):
        rows = pl.ds(r * STRETCH, STRETCH)
        first = (STRETCH - 1) + STRETCH * (entries[r] // 2)
        flat = (STRETCH, 2 * tok)
        gather_ref[rows, :] = one_hot(token_of(1, flat) == iota(flat, 0) + first)
    scatter_ref[...] = gather_ref[...].T
    odd = iota((STRETCH, WIDE), 1) % 2 == 1
    lane = iota((STRETCH, 128), 1)

    def unpair(h):
        for r in range(slots):
            kv_copy(h, r).wait()
            block = kv_pairs[h, r].reshape(WIDE, depth)
            kv_ref[r, h] = block
            kv_turned[r, h] = block.T
        wide = jnp.broadcast_to(turned_ref[h][:1], (STRETCH, 2 * WIDE))
        grid = pltpu.roll(wide, 2 * WIDE - 126, 1, stride=2, stride_axis=0)[:, :WIDE]
        grids[h] = jnp.where(odd, -1e30, grid)

    each(heads, unpair)

    def forward(h):
        table = jnp.zeros((STRETCH, 128), jnp.float32)
        mine = jnp.concatenate([q_ref[:, cols(h)], g_ref[:, cols(h)]], axis=1)
        for copy in in_late(h):
            copy.wait_recv()

        @pl.when(seq == 0)
        def _():
            for copy in in_early(h):
                copy.wait_recv()

        other = jnp.concatenate([q_peer[h], g_peer[h]], axis=1)
        picked = dot(gather_ref[...], jnp.concatenate([mine, other], axis=0)).astype(jnp.bfloat16)
        for r in range(slots):
            rows = picked[r * STRETCH : (r + 1) * STRETCH]
            both = jnp.concatenate([rows[:, :depth], rows[:, depth:]], axis=0)
            windows[h, r] = both
            prod = dot(both, kv_turned[r, h])
            scores = prod[:STRETCH] * scale + grids[h]
            grad_prob = prod[STRETCH:]
            peak = jnp.max(scores, axis=1, keepdims=True)
            expd = jnp.exp(scores - peak)
            total = jnp.sum(expd, axis=1, keepdims=True)
            expd = pltpu.roll(expd, 1, 1)
            inner = jnp.sum(expd * grad_prob, axis=1, keepdims=True)
            weights[h, r] = expd
            cotangents[h, r] = grad_prob
            base = entries[r]
            table = jnp.where(lane == base, peak, table)
            table = jnp.where(lane == base + 8, total, table)
            table = jnp.where(lane == base + 16, inner, table)
        quarter = STRETCH // 4
        packed = table[:quarter]
        for k in range(1, 4):
            packed = packed + pltpu.roll(table[k * quarter : (k + 1) * quarter], 32 * k, 1)
        stat_send[h] = packed
        stat_copy(h).start()

    def partner(x):
        return jnp.where(lane % 2 == 0, pltpu.roll(x, 127, 1), pltpu.roll(x, 1, 1))

    row8 = iota((8, 2 * WIDE), 0)

    def backward(h, stacked):
        stat_copy(h).wait_recv()
        packed = stat_send[h] + stat_recv[h]
        table = jnp.concatenate(
            [packed] + [pltpu.roll(packed, 128 - 32 * k, 1) for k in range(1, 4)], axis=0
        )
        table = jnp.where(lane < 32, table, 0.0)
        total = pltpu.roll(table, 120, 1)
        inner = pltpu.roll(table, 112, 1)
        other_peak = partner(table)
        top = jnp.maximum(table, other_peak)
        mine_f, other_f = jnp.exp(table - top), jnp.exp(other_peak - top)
        denominator = mine_f * total + other_f * partner(total)
        inner = (mine_f * inner + other_f * partner(inner)) / denominator
        norm = mine_f / denominator
        bias_sum = jnp.zeros((STRETCH, WIDE), jnp.float32)
        parts = []
        for r in range(slots):
            at = lane == entries[r]
            factor = jnp.sum(jnp.where(at, norm, 0.0), axis=1, keepdims=True)
            shift = jnp.sum(jnp.where(at, inner, 0.0), axis=1, keepdims=True)
            prob = weights[h, r] * factor
            grad = prob * (cotangents[h, r] - shift)
            bias_sum = bias_sum + grad
            mix = jnp.concatenate([pltpu.roll(grad, WIDE - 1, 1), prob], axis=0).astype(jnp.bfloat16)
            mixed[h, r] = mix
            out = dot(mix, kv_ref[r, h])
            parts.append(
                jnp.concatenate([out[STRETCH:], out[:STRETCH] * scale], axis=1).astype(jnp.bfloat16)
            )
        rows = dot(scatter_ref[...], jnp.concatenate(parts, axis=0))
        rows_own[h] = rows[:tok]
        rows_send[h] = rows[tok:].astype(jnp.bfloat16)
        row_late(h).start()

        @pl.when(seq == 0)
        def _():
            row_early(h).start()

        folded = jnp.concatenate([bias_sum, jnp.zeros_like(bias_sum)], axis=1)
        half = STRETCH // 2
        while half >= 8:
            folded = pltpu.roll(folded[:half], 2 * half, 1) + folded[half:]
            half //= 2
        for bit in (4, 2, 1):
            folded = jnp.where((row8 // bit) % 2 == 0, pltpu.roll(folded, 2 * bit, 1), folded)
        return jnp.where(row8 == h, jnp.sum(folded, axis=0, keepdims=True), stacked)

    stacked = jnp.zeros((8, 2 * WIDE), jnp.float32)
    forward(0)
    for h in range(heads):
        if h + 1 < heads:
            forward(h + 1)
        stacked = backward(h, stacked)
    raw_all[here] = dot_chosen(stacked, unmix_ref[...])
    for k in range(1, plane):
        raw_copy(k).start()

    row_scale = jnp.where(iota((WIDE, depth), 0) % 2 == 0, scale, 1.0)

    def finish_kv(h):
        for r in range(slots):
            dkv = dot(mixed[h, r], windows[h, r], ((0,), (0,))) * row_scale
            dkv_pairs[h, r] = dkv.astype(jnp.bfloat16).reshape(NB_LEN, 2, depth)
            dkv_copy(h, r).start()

    each(heads // 2, finish_kv)
    for k in range(1, plane):
        raw_copy(k).wait_recv()
    raw = raw_all[0]
    for k in range(1, plane):
        raw = raw + raw_all[k]
    norm_all[mp] = jnp.broadcast_to(jnp.sum(raw * raw, keepdims=True), (8, 128))
    for k in range(1, mps):
        norm_copy(k).start()

    each(heads - heads // 2, lambda h: finish_kv(h + heads // 2))

    def finish_rows(h):
        row_late(h).wait_recv()

        @pl.when(seq == 1)
        def _():
            row_early(h).wait_recv()

        rows = rows_own[h] + rows_recv[h].astype(jnp.float32)
        att_ref[:, cols(h)] = rows[:, :depth].astype(jnp.bfloat16)
        dq_ref[:, cols(h)] = rows[:, depth:].astype(jnp.bfloat16)

    each(heads, finish_rows)
    for copy in out_copies():
        copy.start()
    for k in range(1, mps):
        norm_copy(k).wait_recv()
    squares = norm_all[0]
    for k in range(1, mps):
        squares = squares + norm_all[k]
    clip = jnp.minimum(1.0, 1.0 / jnp.sqrt(squares[:, :1] + 1e-12))
    dbias_ref[...] = (raw * clip)[:heads, :rel]

    def drain(h):
        for copy in in_late(h):
            copy.wait_send()
        row_late(h).wait_send()
        stat_copy(h).wait_send()

        @pl.when(seq == 1)
        def _():
            for copy in in_early(h):
                copy.wait_send()

        @pl.when(seq == 0)
        def _():
            row_early(h).wait_send()

        for r in range(slots):
            dkv_copy(h, r).wait()

    each(heads, drain)
    for k in range(1, plane):
        raw_copy(k).wait_send()
    for k in range(1, mps):
        norm_copy(k).wait_send()
    for copy in out_copies():
        copy.wait()


def write_kernel(
    att, dq, dkv, dbias, att_out, dq_out, dkv_out, dbias_out,
    att_held, dq_held, dkv_held, dbias_held, load_sems, store_sems,
):
    slots = dkv.shape[1]
    routes = [(dkv.at[0, r], dkv_held.at[r], dkv_out.at[0, r]) for r in range(slots)]
    routes += [(att, att_held, att_out), (dq, dq_held, dq_out), (dbias, dbias_held, dbias_out)]
    loads = [pltpu.make_async_copy(a, b, load_sems.at[k]) for k, (a, b, _) in enumerate(routes)]
    stores = [pltpu.make_async_copy(b, c, store_sems.at[k]) for k, (_, b, c) in enumerate(routes)]
    for copy in loads:
        copy.start()
    for load, store in zip(loads, stores):
        load.wait()
        store.start()
    for copy in stores:
        copy.wait()


def pair_exchange(queries, d_out, neighbour_kv, target, bias):
    _, tok, width = queries.shape
    heads = bias.shape[0]
    depth = width // heads
    slots = neighbour_kv.shape[1]
    plane, mps = 2 * lax.axis_size("grp"), lax.axis_size("mp")
    vmem = pl.BlockSpec(memory_space=pltpu.VMEM)
    hbm = pl.BlockSpec(memory_space=pltpu.HBM)
    f32, bf16, dma = jnp.float32, jnp.bfloat16, pltpu.SemaphoreType.DMA
    results = tuple(jax.ShapeDtypeStruct(x.shape, x.dtype) for x in (queries, d_out, neighbour_kv, bias))
    parts = pl.pallas_call(
        pair_kernel,
        out_shape=results,
        in_specs=[hbm, hbm, hbm, hbm, vmem],
        out_specs=(hbm, hbm, hbm, vmem),
        scratch_shapes=[
            pltpu.SMEM(target.shape, jnp.int32),
            pltpu.VMEM((tok, width), bf16),
            pltpu.VMEM((tok, width), bf16),
            pltpu.VMEM((heads, slots, NB_LEN, 2, depth), bf16),
            pltpu.VMEM((slots, heads, WIDE, depth), bf16),
            pltpu.VMEM((heads, tok, depth), bf16),
            pltpu.VMEM((heads, tok, depth), bf16),
            pltpu.VMEM((heads, slots, 2 * STRETCH, depth), bf16),
            pltpu.VMEM((heads, slots, STRETCH, WIDE), f32),
            pltpu.VMEM((heads, slots, STRETCH, WIDE), f32),
            pltpu.VMEM((heads, slots, 2 * STRETCH, WIDE), bf16),
            pltpu.VMEM((heads, tok, 2 * depth), f32),
            pltpu.VMEM((heads, tok, 2 * depth), bf16),
            pltpu.VMEM((heads, tok, 2 * depth), bf16),
            pltpu.VMEM((slots * STRETCH, 2 * tok), bf16),
            pltpu.VMEM((2 * tok, slots * STRETCH), bf16),
            pltpu.VMEM((heads, 8, 2 * WIDE), f32),
            pltpu.VMEM((slots, heads, depth, WIDE), bf16),
            pltpu.VMEM((heads, STRETCH, WIDE), f32),
            pltpu.VMEM((2 * WIDE, WIDE), bf16),
            pltpu.VMEM((8, WIDE), f32),
            pltpu.VMEM((heads, slots, NB_LEN, 2, depth), bf16),
            pltpu.VMEM((tok, width), bf16),
            pltpu.VMEM((tok, width), bf16),
            pltpu.VMEM((heads, STRETCH // 4, 128), f32),
            pltpu.VMEM((heads, STRETCH // 4, 128), f32),
            pltpu.VMEM((plane, 8, WIDE), f32),
            pltpu.VMEM((mps, 8, 128), f32),
            dma((3,)),
            dma((heads, slots)),
            dma((4, heads)),
            dma((4, heads)),
            dma((heads,)),
            dma((heads,)),
            dma((2, heads)),
            dma((2, heads)),
            dma((plane,)),
            dma((plane,)),
            dma((mps,)),
            dma((mps,)),
            dma((2,)),
            dma((heads, slots)),
        ],
        compiler_params=pltpu.CompilerParams(
            collective_id=0, has_side_effects=True, vmem_limit_bytes=VMEM_USE
        ),
    )(queries, d_out, neighbour_kv, target, bias)
    return pl.pallas_call(
        write_kernel,
        out_shape=results,
        in_specs=[hbm] * 4,
        out_specs=(hbm,) * 4,
        scratch_shapes=[
            pltpu.VMEM(queries.shape, bf16),
            pltpu.VMEM(d_out.shape, bf16),
            pltpu.VMEM(neighbour_kv.shape[1:], bf16),
            pltpu.VMEM(bias.shape, f32),
            dma((slots + 3,)),
            dma((slots + 3,)),
        ],
        compiler_params=pltpu.CompilerParams(vmem_limit_bytes=VMEM_USE),
    )(*parts)


def local(queries, d_out, neighbour_kv, target, bias):
    tok = queries.shape[1]
    fits = (
        lax.axis_size("seq") == 2
        and neighbour_kv.shape[1] == 2 * (tok // STRETCH)
        and tok == 128
        and bias.shape == (4, 191)
        and queries.shape[2] == 512
    )
    run = pair_exchange if fits else shard_exchange
    return run(queries, d_out, neighbour_kv, target, bias)


def solution(mesh):
    in_specs = (
        P("grp", "seq", "mp"),
        P("grp", "seq", "mp"),
        P("grp", "seq", None, None, "mp"),
        P("grp", "seq"),
        P("mp", None),
    )
    out_specs = (
        P("grp", "seq", "mp"),
        P("grp", "seq", "mp"),
        P("grp", "seq", None, None, "mp"),
        P("mp", None),
    )
    return jax.shard_map(local, mesh=mesh, in_specs=in_specs, out_specs=out_specs, check_vma=False)
```
